128 devices in a mesh: row: 8 (over x, core), col: 16 (over y, z).
Axes of the slice: x: 4, y: 4, z: 4, core: 2. Of those that a mesh axis runs over, the one named last changes fastest.
Arguments:
- image_pooled: bfloat16 [16384, 1664], P(('row', 'col')), may hold values from -6 to 6
- text_pooled: bfloat16 [16384, 1280], P(('col', 'row')), may hold values from -6 to 6
- image_proj: bfloat16 [1664, 1280], replicated, may hold values from -0.8 to 0.8
- text_proj: bfloat16 [1280, 1280], replicated, may hold values from -0.8 to 0.8
- log_scale: float32 [1], replicated, may hold values from 3 to 5.1
- pair_index: int32 [16384], P(('row', 'col')), may hold values from 0 to 16383, each once
Outputs:
- loss: float32 [1], replicated
- d_image_pooled: bfloat16 [16384, 1664], P(('row', 'col'))
- d_text_pooled: bfloat16 [16384, 1280], P(('col', 'row'))
- d_image_proj: float32 [1664, 1280], replicated
- d_text_proj: float32 [1280, 1280], replicated
- d_log_scale: float32 [1], replicated
The draws below stay inside these ranges and needn't reach their ends.
Inputs may be any that keep to these rules, and one draw needn't show every extreme that they name: `pair_index`: a permutation: every text matches exactly one image.
All inputs are finite; a program needn't handle non-finite values.
Results may differ from the reference program's by a relative error of at most 0.033.
Values may be sent and summed in bfloat16 or wider, within the bound.
A program may use at most 128 MiB of HBM per device.

```python
import math
import jax
import jax.numpy as jnp
from jax import lax

DI = 1664
DT = 1280
EMB = 1280
PAIR_DEV = 128
BATCH = 16384
N_ROW = 8
N_COL = 16


def common_direction(key):
    values = jax.random.normal(jax.random.fold_in(key, 977), (EMB,), jnp.float32)
    return jnp.clip(values, -4.0, 4.0)


def pooled_rows(key, width):
    values = jax.random.normal(jax.random.fold_in(key, 1), (BATCH, width), jnp.float32)
    return jnp.clip(values, -6.0, 6.0)


def projection(key, rows):
    values = jax.random.normal(jax.random.fold_in(key, 1), (rows, EMB), jnp.float32)
    return jnp.clip(values, -4.0, 4.0) / math.sqrt(rows)


def block_ramp(key, groups, low, high):
    group_rows = BATCH // groups
    index = jnp.arange(BATCH, dtype=jnp.int32) // group_rows
    frac = index.astype(jnp.float32) / max(groups - 1, 1)
    jitter = jax.random.uniform(jax.random.fold_in(key, 5), (BATCH, 1), jnp.float32, -0.15, 0.15)
    return low + (high - low) * frac[:, None] + jitter


def draw_image_pooled(key, part):
    key = jax.random.fold_in(key, 11)
    values = pooled_rows(key, DI)
    ramp = block_ramp(key, N_ROW, 1.5, 3.5)
    values = jnp.concatenate([ramp, values[:, 1:]], axis=1)
    return values.astype(jnp.bfloat16)


def draw_text_pooled(key, part):
    key = jax.random.fold_in(key, 13)
    values = pooled_rows(key, DT)
    ramp = block_ramp(key, N_COL, 1.5, 3.5)
    values = jnp.concatenate([ramp, values[:, 1:]], axis=1)
    return values.astype(jnp.bfloat16)


def draw_image_proj(key, part):
    direction = common_direction(key)
    key = jax.random.fold_in(key, 17)
    values = projection(key, DI)
    values = jnp.concatenate([0.2 * direction[None, :], values[1:]], axis=0)
    return values.astype(jnp.bfloat16)


def draw_text_proj(key, part):
    direction = common_direction(key)
    key = jax.random.fold_in(key, 23)
    values = projection(key, DT)
    values = jnp.concatenate([0.2 * direction[None, :], values[1:]], axis=0)
    return values.astype(jnp.bfloat16)


def draw_log_scale(key, part):
    key = jax.random.fold_in(key, 29)
    values = jax.random.uniform(key, (1,), jnp.float32, 3.0, 3.6)
    return values


def setup_inputs(seed: int = 0) -> dict:
    streams_of = jax.random.split(jax.random.key(seed), 7)
    image_pooled = draw_image_pooled(jax.random.fold_in(streams_of[6], 71), 0)
    text_pooled = draw_text_pooled(jax.random.fold_in(streams_of[6], 71), 0)
    image_proj = draw_image_proj(jax.random.fold_in(streams_of[6], 71), 0)
    text_proj = draw_text_proj(jax.random.fold_in(streams_of[6], 71), 0)
    log_scale = draw_log_scale(jax.random.fold_in(streams_of[6], 71), 0)
    pair_index = jax.random.permutation(streams_of[5], BATCH).astype(jnp.int32)
    return dict(image_pooled=image_pooled, text_pooled=text_pooled, image_proj=image_proj, text_proj=text_proj, log_scale=log_scale, pair_index=pair_index)


EPS = 1e-06

def embed(pooled, proj):
    z = jnp.dot(pooled, proj, preferred_element_type=jnp.float32)
    norms = jnp.sqrt(lax.optimization_barrier(jnp.sum(z * z, axis=1, keepdims=True)) + EPS)
    unit = z / norms
    return (unit, norms, unit.astype(jnp.bfloat16))

def backward(grads, unit, norms, pooled, proj):
    inner = lax.optimization_barrier(jnp.sum(unit * grads, axis=1, keepdims=True))
    dz = ((grads - unit * inner) / norms).astype(jnp.bfloat16)
    dpool = lax.dot_general(dz, proj, (((1,), (1,)), ((), ())), preferred_element_type=jnp.float32).astype(jnp.bfloat16)
    dweight = lax.dot_general(pooled, dz, (((0,), (0,)), ((), ())), preferred_element_type=jnp.float32)
    return (dpool, dweight)

def reference(image_pooled, text_pooled, image_proj, text_proj, log_scale, pair_index):
    unit_img, norm_img, emb_img = embed(image_pooled, image_proj)
    unit_txt, norm_txt, emb_txt = embed(text_pooled, text_proj)
    scale = jnp.exp(log_scale[0])
    rows = PAIR_DEV * N_COL
    blocks = BATCH // rows
    img_blocks = emb_img.reshape(blocks, rows, EMB)
    perm_blocks = pair_index.reshape(blocks, rows)
    columns = lax.iota(jnp.int32, BATCH)

    def logits(block):
        return scale * lax.dot_general(block, emb_txt, (((1,), (1,)), ((), ())), preferred_element_type=jnp.float32)

    def first(carry, block):
        col_peak, col_total = carry
        scores = logits(block)
        peak = lax.optimization_barrier(jnp.max(scores, axis=1))
        lse_rows = peak + jnp.log(lax.optimization_barrier(jnp.sum(jnp.exp(scores - peak[:, None]), axis=1)))
        new_peak = jnp.maximum(col_peak, lax.optimization_barrier(jnp.max(scores, axis=0)))
        col_total = col_total * jnp.exp(col_peak - new_peak) + lax.optimization_barrier(jnp.sum(jnp.exp(scores - new_peak[None, :]), axis=0))
        return ((new_peak, col_total), lse_rows)
    init = (jnp.full((BATCH,), -1e+30, jnp.float32), jnp.zeros((BATCH,), jnp.float32))
    (col_peak, col_total), lse_row = lax.scan(first, init, img_blocks)
    lse_col = col_peak + jnp.log(col_total)

    def second(carry, inputs):
        text_acc, scale_acc, target_acc = carry
        block, perm, lse_rows = inputs
        scores = logits(block)
        hits = perm[:, None] == columns[None, :]
        grad = 0.5 * (jnp.exp(scores - lse_rows[:, None]) + jnp.exp(scores - lse_col[None, :])) - hits.astype(jnp.float32)
        grad_b = grad.astype(jnp.bfloat16)
        img_grad = scale * jnp.dot(grad_b, emb_txt, preferred_element_type=jnp.float32)
        text_acc = text_acc + scale * lax.dot_general(grad_b, block, (((0,), (0,)), ((), ())), preferred_element_type=jnp.float32)
        scale_acc = scale_acc + jnp.sum(grad * scores)
        target_acc = target_acc + jnp.sum(jnp.where(hits, scores, 0.0))
        return ((text_acc, scale_acc, target_acc), img_grad)
    init2 = (jnp.zeros((BATCH, EMB), jnp.float32), jnp.zeros((), jnp.float32), jnp.zeros((), jnp.float32))
    (text_grads, scale_grad, target_sum), img_grads = lax.scan(second, init2, (img_blocks, perm_blocks, lse_row))
    img_grads = img_grads.reshape(BATCH, EMB)
    total = 0.5 * (jnp.sum(lse_row) + jnp.sum(lse_col)) - target_sum
    dpi, dwi = backward(img_grads, unit_img, norm_img, image_pooled, image_proj)
    dpt, dwt = backward(text_grads, unit_txt, norm_txt, text_pooled, text_proj)
    return ((total / BATCH).reshape(1), dpi, dpt, dwi, dwt, scale_grad.reshape(1))
```

```python
import functools

import jax
import jax.numpy as jnp
from jax import lax
from jax.experimental import pallas as pl
from jax.experimental.pallas import tpu as pltpu
from jax.sharding import PartitionSpec as P

EPS = 1e-06
MESH = pl.DeviceIdType.MESH
F32 = jnp.float32
BF16 = jnp.bfloat16
PAIRS = 128
NCOL = 16
NROW = 8
EMB = 1280
DI = 1664
DT = 1280
HALF = EMB // 2
DIRS = (1, -1)
STEPS = (2, 1, -1, 0)


class Net:
    def __init__(self, send_sem, recv_sem):
        self.send_sem, self.recv_sem = send_sem, recv_sem
        row, col = lax.axis_index("row"), lax.axis_index("col")
        self.x, self.c = row // 2, row % 2
        self.y, self.z = col // 4, col % 4
        self.count = 0
        self.started = []

    def dev(self, dx=0, dy=0, dz=0):
        return (
            2 * ((self.x + dx + 4) % 4) + self.c,
            4 * ((self.y + dy + 4) % 4) + (self.z + dz + 4) % 4,
        )

    def mate(self):
        return (2 * self.x + 1 - self.c, 4 * self.y + self.z)

    def barrier(self):
        others = [self.mate()]
        for d in (1, 2, 3):
            others += [self.dev(dx=d), self.dev(dy=d), self.dev(dz=d)]
        sem = pltpu.get_barrier_semaphore()
        for other in others:
            pl.semaphore_signal(sem, inc=1, device_id=other, device_id_type=MESH)
        pl.semaphore_wait(sem, len(others))

    def copy(self, number, src, dst, device):
        return pltpu.make_async_remote_copy(
            src_ref=src,
            dst_ref=dst,
            send_sem=self.send_sem.at[number],
            recv_sem=self.recv_sem.at[number],
            device_id=device,
            device_id_type=MESH,
        )

    def send(self, src, dst, device):
        number = self.count
        self.count += 1
        copy = self.copy(number, src, dst, device)
        copy.start()
        self.started.append(copy)
        return number

    def recv(self, number, dst):
        self.copy(number, dst, dst, self.mate()).wait_recv()

    def finish(self):
        for copy in self.started:
            copy.wait_send()


def lanes(column):
    return jnp.transpose(jnp.broadcast_to(column, (PAIRS, PAIRS)))[0:1, :]


def sublanes(row):
    return jnp.transpose(jnp.broadcast_to(row, (PAIRS, PAIRS)))


def lse_over(parts):
    peak = functools.reduce(jnp.maximum, parts)
    return peak + jnp.log(sum(jnp.exp(p - peak) for p in parts))


def main_kernel(
    scale_ref, eimg, etxt, pair, gimg, gtxt, sums,
    img, txt, pid, scores, gb, pimg, ptxt,
    rg1, rg2, rb, rf1, rf2, rc, rx1, rx2,
    cmax, csum, rowl, rowz, rowy, coll, colx, colc, acc, send_sem, recv_sem,
):
    net = Net(send_sem, recv_sem)
    x, c, y, z = net.x, net.c, net.y, net.z
    me_col = 4 * y + z
    scale = scale_ref[0]

    def axes(h):
        return ((y, z), (z, y))[h]

    def gdev(h, d):
        return net.dev(dy=d) if h == 0 else net.dev(dz=d)

    def fdev(h, d):
        return net.dev(dz=d) if h == 0 else net.dev(dy=d)

    def block(h, dg, df):
        g, f = axes(h)
        g, f = (g + dg + 4) % 4, (f + df + 4) % 4
        return 4 * g + f if h == 0 else 4 * f + g

    def half(ref, q, h):
        return ref.at[q, pl.ds(64 * h, 64)]

    def sub(ref, q, h, d):
        return ref.at[q, pl.ds(64 * h + (0 if d == 1 else 32), 32)]

    def rel(dy, dz):
        return 4 * ((y + dy + 4) % 4) + (z + dz + 4) % 4

    def tblock(dx, core):
        return pl.ds(pl.multiple_of((2 * ((x + dx + 4) % 4) + core) * PAIRS, PAIRS), PAIRS)

    def tsub(dx, core, d):
        start = (2 * ((x + dx + 4) % 4) + core) * PAIRS + (0 if d == 1 else 64)
        return pl.ds(pl.multiple_of(start, 64), 64)

    img[me_col] = eimg[...]
    txt[tblock(0, c), :] = etxt[...]
    pid[me_col] = jnp.broadcast_to(pair[...], (8, PAIRS))
    cmax[...] = jnp.full_like(cmax, -1e30)
    csum[...] = jnp.zeros_like(csum)
    acc[...] = jnp.zeros_like(acc)
    net.barrier()

    f1, g1, f2, g3, g4 = {}, {}, {}, {}, {}
    for h in (0, 1):
        for d in DIRS:
            part = half(img, me_col, h)
            f1[h, d] = net.send(part, part, fdev(h, d))
    x1, x2, cx = {}, {}, {}
    for d in DIRS:
        part = txt.at[tblock(0, c)]
        x1[d] = net.send(part, part, net.dev(dx=d))
    for h in (0, 1):
        for d in DIRS:
            part = half(img, me_col, h)
            g1[h, d] = net.send(part, part, gdev(h, d))

    def to_mate(dx):
        part = txt.at[tblock(dx, c)]
        cx[dx] = net.send(part, part, net.mate())

    to_mate(0)
    pz, py = {}, {}
    for d in (1, 2, 3):
        pz[d] = net.send(pid.at[me_col], pid.at[me_col], net.dev(dz=d))

    for h in (0, 1):
        for d in DIRS:
            q = block(h, 0, -d)
            net.recv(f1[h, d], half(img, q, h))
            f2[h, d] = net.send(sub(img, q, h, d), sub(img, q, h, d), fdev(h, d))
            for e in DIRS:
                g3[h, -d, e] = net.send(half(img, q, h), half(img, q, h), gdev(h, e))

    def pass_on(h, j, d):
        q = block(h, -d, j)
        net.recv(g1[h, d] if j == 0 else g3[h, j, d], half(img, q, h))
        g4[h, j, d] = net.send(sub(img, q, h, d), sub(img, q, h, d), gdev(h, d))

    for h in (0, 1):
        for d in DIRS:
            pass_on(h, 0, d)
    for d in DIRS:
        net.recv(x1[d], txt.at[tblock(-d, c)])
        part = txt.at[tsub(-d, c, d)]
        x2[d] = net.send(part, part, net.dev(dx=d))
        to_mate(-d)
    for h in (0, 1):
        q = block(h, 0, 2)
        for d in DIRS:
            net.recv(f2[h, d], sub(img, q, h, d))
        for d in DIRS:
            g3[h, 2, d] = net.send(half(img, q, h), half(img, q, h), gdev(h, d))
    for d in (1, 2, 3):
        net.recv(pz[d], pid.at[rel(0, -d)])
    for d in (1, 2, 3):
        line = pid.at[pl.ds(4 * y, 4)]
        py[d] = net.send(line, line, net.dev(dy=d))
    for d in DIRS:
        net.recv(x2[d], txt.at[tsub(2, c, d)])
    to_mate(2)
    for dx in (0, 1, -1, 2):
        net.recv(cx[dx], txt.at[tblock(dx, 1 - c)])

    def score(q):
        s = scale * lax.dot_general(
            img[q], txt[...], (((1,), (1,)), ((), ())), preferred_element_type=F32
        )
        scores[q] = s
        peak = jnp.max(s, axis=1, keepdims=True)
        total = jnp.sum(jnp.exp(s - peak), axis=1, keepdims=True)
        rowl[pl.ds(q, 1), :] = lanes(peak + jnp.log(total))
        s3 = s.reshape(PAIRS // 8, 8, s.shape[1])
        old = cmax[...]
        new = jnp.maximum(old, jnp.max(s3, axis=0))
        csum[...] = csum[...] * jnp.exp(old - new) + jnp.sum(jnp.exp(s3 - new[None]), axis=0)
        cmax[...] = new

    def score_line(start, length, where):
        @pl.loop(start, start + length)
        def _(i):
            score(where(i))

    score_line(-1, 3, lambda i: rel(0, i))
    for h in (0, 1):
        for j in (1, -1):
            for d in DIRS:
                pass_on(h, j, d)
    score_line(-1, 3, lambda i: rel(1, i))
    for h in (0, 1):
        for d in DIRS:
            pass_on(h, 2, d)
    score_line(-1, 3, lambda i: rel(-1, i))
    for j in (0, 1, -1):
        for h in (0, 1):
            for d in DIRS:
                net.recv(g4[h, j, d], sub(img, block(h, 2, j), h, d))
    score_line(-1, 3, lambda i: rel(2, i))
    score_line(-1, 3, lambda i: rel(i, 2))
    for h in (0, 1):
        for d in DIRS:
            net.recv(g4[h, 2, d], sub(img, block(h, 2, 2), h, d))
    score(rel(2, 2))

    rz, ry, lx = {}, {}, {}
    rowz[z] = rowl[...]
    for d in (1, 2, 3):
        rz[d] = net.send(rowz.at[z], rowz.at[z], net.dev(dz=d))
    peak = jnp.max(cmax[...], axis=0, keepdims=True)
    lcol = peak + jnp.log(jnp.sum(csum[...] * jnp.exp(cmax[...] - peak), axis=0, keepdims=True))
    for r in range(NROW):
        coll[r : r + 1, :] = lcol[:, r * PAIRS : (r + 1) * PAIRS]
    colx[x] = coll[...]
    for d in (1, 2, 3):
        lx[d] = net.send(colx.at[x], colx.at[x], net.dev(dx=d))
    for d in (1, 2, 3):
        net.recv(rz[d], rowz.at[(z - d + 4) % 4])
    rowy[y] = lse_over([rowz[i] for i in range(4)])
    for d in (1, 2, 3):
        ry[d] = net.send(rowy.at[y], rowy.at[y], net.dev(dy=d))
    for d in (1, 2, 3):
        net.recv(lx[d], colx.at[(x - d + 4) % 4])
    colc[c] = lse_over([colx[i] for i in range(4)])
    lc = net.send(colc.at[c], colc.at[c], net.mate())
    for d in (1, 2, 3):
        line = pid.at[pl.ds(4 * ((y - d + 4) % 4), 4)]
        net.recv(py[d], line)
    for d in (1, 2, 3):
        net.recv(ry[d], rowy.at[(y - d + 4) % 4])
    rowl[...] = lse_over([rowy[i] for i in range(4)])
    net.recv(lc, colc.at[1 - c])
    coll[...] = lse_over([colc[i] for i in range(2)])

    first = (me_col * NROW * PAIRS).astype(F32)
    place = lax.broadcasted_iota(jnp.int32, (PAIRS, PAIRS), 1).astype(F32) + first

    def grad(q):
        lrow = sublanes(rowl[pl.ds(q, 1), :])
        mine = sublanes(pid[q][0:1, :]) - place
        hit_sum = jnp.zeros((PAIRS, PAIRS), F32)
        dot_sum = jnp.zeros((PAIRS, PAIRS), F32)
        for r in range(NROW):
            at = slice(r * PAIRS, (r + 1) * PAIRS)
            s = scores[q, :, at]
            soft = 0.5 * (jnp.exp(s - lrow) + jnp.exp(s - coll[r : r + 1, :]))
            hit = (mine == float(r * PAIRS)).astype(F32)
            g = soft - hit
            hit_sum += s * hit
            dot_sum += s * g
            gb[pl.ds(pl.multiple_of(q * PAIRS, PAIRS), PAIRS), at] = g.astype(BF16)
        acc[0] += hit_sum
        acc[1] += dot_sum
        rows = gb[pl.ds(pl.multiple_of(q * PAIRS, PAIRS), PAIRS), :]
        pimg[q] = jnp.dot(rows, txt[...], preferred_element_type=F32).astype(BF16)

    def grad_line(start, length, where):
        @pl.loop(start, start + length)
        def _(i):
            grad(where(i))

    rg1n, rg2n, rf1n, rf2n = {}, {}, {}, {}
    slot = {2: 0, 1: 1, -1: 2, 0: 3}
    side = {1: 0, -1: 1}

    def scatter1(h):
        for j in STEPS:
            for d in DIRS:
                q = block(h, 2, j)
                rg1n[h, j, d] = net.send(
                    sub(pimg, q, h, d), rg1.at[h, slot[j], side[d]], gdev(h, d)
                )

    def scatter2(j):
        for h in (0, 1):
            for d in DIRS:
                q = block(h, d, j)
                got = rg1.at[h, slot[j], side[d]]
                net.recv(rg1n[h, j, d], got)
                part = sub(pimg, q, h, d)
                part[...] = (part[...].astype(F32) + got[...].astype(F32)).astype(BF16)
                rg2n[h, j, d] = net.send(
                    half(pimg, q, h), rg2.at[h, slot[j], side[d]], gdev(h, d)
                )

    def line_sum(h, j):
        for d in DIRS:
            net.recv(rg2n[h, j, d], rg2.at[h, slot[j], side[d]])
        total = half(pimg, block(h, 0, j), h)[...].astype(F32)
        for d in DIRS:
            total += rg2[h, slot[j], side[d]].astype(F32)
        return total

    grad_line(-1, 4, lambda i: rel(2, i))
    scatter1(0)
    grad_line(-1, 3, lambda i: rel(i, 2))
    scatter1(1)
    scatter2(2)
    grad_line(0, 4, lambda i: rel(2 * (i // 2) - 1, 2 * (i % 2) - 1))
    scatter2(1)
    scatter2(-1)
    grad_line(0, 2, lambda i: rel(2 * i - 1, 0))
    grad_line(0, 2, lambda i: rel(0, 2 * i - 1))
    scatter2(0)
    grad(rel(0, 0))

    mate_n, tx1n, tx2n = {}, {}, {}

    def text_product(dx):
        xx = (x + dx + 4) % 4
        at = pl.ds(pl.multiple_of(xx * 2 * PAIRS, 2 * PAIRS), 2 * PAIRS)
        prod = lax.dot_general(
            gb[:, at], img[...].reshape(NCOL * PAIRS, EMB), (((0,), (0,)), ((), ())),
            preferred_element_type=F32,
        )
        ptxt[at, :] = prod.astype(BF16)
        mate_n[dx] = net.send(ptxt.at[tblock(dx, 1 - c)], rc.at[xx], net.mate())

    def text_pair(dx):
        xx = (x + dx + 4) % 4
        net.recv(mate_n[dx], rc.at[xx])
        return ptxt[tblock(dx, c), :].astype(F32) + rc[xx].astype(F32)

    text_product(2)
    text_product(1)
    for h in (0, 1):
        rb[h, 0] = line_sum(h, 2).astype(BF16)
        for d in DIRS:
            at = pl.ds(0 if d == 1 else 32, 32)
            rf1n[h, d] = net.send(rb.at[h, 0, at], rf1.at[h, side[d]], fdev(h, d))
    ptxt[tblock(2, c), :] = text_pair(2).astype(BF16)
    for d in DIRS:
        tx1n[d] = net.send(ptxt.at[tsub(2, c, d)], rx1.at[side[d]], net.dev(dx=d))
    text_product(-1)
    for d in DIRS:
        ptxt[tblock(d, c), :] = text_pair(d).astype(BF16)
        net.recv(tx1n[d], rx1.at[side[d]])
        part = ptxt.at[tsub(d, c, d)]
        part[...] = (part[...].astype(F32) + rx1[side[d]].astype(F32)).astype(BF16)
        tx2n[d] = net.send(ptxt.at[tblock(d, c)], rx2.at[side[d]], net.dev(dx=d))
    text_product(0)
    for h in (0, 1):
        for d in DIRS:
            total = line_sum(h, d)
            net.recv(rf1n[h, d], rf1.at[h, side[d]])
            extra = rf1[h, side[d]].astype(F32)
            lo, hi = total[0:32], total[32:64]
            if d == 1:
                lo = lo + extra
            else:
                hi = hi + extra
            rb[h, 1 + side[d], 0:32] = lo.astype(BF16)
            rb[h, 1 + side[d], 32:64] = hi.astype(BF16)
            rf2n[h, d] = net.send(rb.at[h, 1 + side[d]], rf2.at[h, side[d]], fdev(h, d))

    total = text_pair(0)
    for d in DIRS:
        net.recv(tx2n[d], rx2.at[side[d]])
        total += rx2[side[d]].astype(F32)
    gtxt[...] = scale * total
    for h in (0, 1):
        total = line_sum(h, 0)
        for d in DIRS:
            net.recv(rf2n[h, d], rf2.at[h, side[d]])
            total += rf2[h, side[d]].astype(F32)
        gimg[pl.ds(64 * h, 64), :] = scale * total
    half_lse = (0.5 / NCOL) * jnp.sum(rowl[...].reshape(2, 8, PAIRS), axis=0) + (
        0.5 / NROW
    ) * coll[...]
    sums[0] = half_lse - jnp.sum(acc[0].reshape(16, 8, PAIRS), axis=0)
    sums[1] = jnp.sum(acc[1].reshape(16, 8, PAIRS), axis=0)
    net.finish()


def weight_kernel(
    pi, pt, dzi, dzt, tile, out, tot,
    ai, at, di, dt, w, r1, r2, q1, r3, q2, r4, s4, s2, send_sem, recv_sem,
):
    net = Net(send_sem, recv_sem)
    c = net.c
    place = (net.x, net.y, net.z)

    def dev(axis, d):
        return net.dev(**{("dx", "dy", "dz")[axis]: d})

    mine = pl.ds(pl.multiple_of(c * PAIRS, PAIRS), PAIRS)
    other = pl.ds(pl.multiple_of((1 - c) * PAIRS, PAIRS), PAIRS)
    keep = pl.ds(pl.multiple_of(c * HALF, 128), HALF)
    give = pl.ds(pl.multiple_of((1 - c) * HALF, 128), HALF)

    s4[0, net.x] = tile[...]
    net.barrier()
    pair = []
    for src, dst in ((dzi.at[:, give], di), (dzt.at[:, give], dt), (pi, ai), (pt, at)):
        pair.append((net.send(src, dst.at[mine], net.mate()), dst))
    tot_n = {}

    def tot_send(axis):
        own = s4.at[axis, place[axis]]
        for d in (1, 2, 3):
            tot_n[axis, d] = net.send(own, own, dev(axis, d))

    def tot_recv(axis):
        for d in (1, 2, 3):
            net.recv(tot_n[axis, d], s4.at[axis, (place[axis] - d + 4) % 4])
        return s4[axis, 0] + s4[axis, 1] + s4[axis, 2] + s4[axis, 3]

    tot_send(0)
    ai[mine, :] = pi[...]
    at[mine, :] = pt[...]
    di[mine, :] = dzi[:, keep]
    dt[mine, :] = dzt[:, keep]
    w[DI + DT :, :] = jnp.zeros((128, HALF), BF16)
    for number, dst in pair:
        net.recv(number, dst.at[other])

    def product(left, right, base, tiles):
        @pl.loop(0, tiles)
        def _(i):
            cols = pl.ds(pl.multiple_of(i * 128, 128), 128)
            rows = pl.ds(pl.multiple_of(base + i * 128, 128), 128)
            w[rows, :] = lax.dot_general(
                left[:, cols], right[...], (((0,), (0,)), ((), ())), preferred_element_type=F32
            ).astype(BF16)

    product(ai, di, 0, DI // 128)
    product(at, dt, DI, DT // 128)

    orders = ((0, 1, 2), (1, 2, 0), (2, 0, 1))
    side = {1: 0, -1: 1}

    def near(axis, d):
        return (place[axis] + d + 4) % 4

    def rows_at(k, a, b=None, e=None, size=256):
        start = 1024 * k + 256 * a
        if b is not None:
            start = start + 64 * b
        if e is not None:
            start = start + 16 * e
        return pl.ds(pl.multiple_of(start, 16), size)

    def part(k, d, s):
        return pl.ds(pl.multiple_of(1024 * k + 256 * near(orders[k][0], d) + 128 * s, 128), 128)

    n1, n2, n3, n4 = {}, {}, {}, {}
    for k in range(3):
        for d in DIRS:
            n1[k, d] = net.send(
                w.at[part(k, 2, side[d])], r1.at[k, side[d]], dev(orders[k][0], d)
            )
    for k in range(3):
        for d in DIRS:
            net.recv(n1[k, d], r1.at[k, side[d]])
            got = part(k, d, side[d])
            w[got, :] = (w[got, :].astype(F32) + r1[k, side[d]].astype(F32)).astype(BF16)
            n2[k, d] = net.send(
                w.at[rows_at(k, near(orders[k][0], d))], r2.at[k, side[d]], dev(orders[k][0], d)
            )
    s4[1, net.y] = tot_recv(0)
    tot_send(1)
    for k in range(3):
        a_ax, b_ax, c_ax = orders[k]
        total = w[rows_at(k, place[a_ax]), :].astype(F32)
        for d in DIRS:
            net.recv(n2[k, d], r2.at[k, side[d]])
            total += r2[k, side[d]].astype(F32)
        q1[k] = total.astype(BF16)
        for d in (2, 1, 3):
            to = pl.ds(pl.multiple_of(64 * near(b_ax, d), 64), 64)
            n3[k, d] = net.send(q1.at[k, to], r3.at[k, d - 1], dev(b_ax, d))
    s4[2, net.z] = tot_recv(1)
    tot_send(2)
    for k in range(3):
        a_ax, b_ax, c_ax = orders[k]
        total = q1[k, pl.ds(pl.multiple_of(64 * place[b_ax], 64), 64), :].astype(F32)
        for d in (1, 3, 2):
            net.recv(n3[k, d], r3.at[k, d - 1])
            total += r3[k, d - 1].astype(F32)
        q2[k] = total.astype(BF16)
        for d in (2, 1, 3):
            to = pl.ds(pl.multiple_of(16 * near(c_ax, d), 16), 16)
            n4[k, d] = net.send(q2.at[k, to], r4.at[k, d - 1], dev(c_ax, d))

    m1, m2, m3, m4, mate_n = {}, {}, {}, {}, {}
    outc = out.at[c]
    s2[c] = tot_recv(2)
    tot_mate = net.send(s2.at[c], s2.at[c], net.mate())
    for k in range(3):
        a_ax, b_ax, c_ax = orders[k]
        total = q2[k, pl.ds(pl.multiple_of(16 * place[c_ax], 16), 16), :].astype(F32)
        for d in (1, 3, 2):
            net.recv(n4[k, d], r4.at[k, d - 1])
            total += r4[k, d - 1].astype(F32)
        own = rows_at(k, place[a_ax], place[b_ax], place[c_ax], 16)
        out[c, own, :] = total.astype(BF16)
        for d in (2, 1, 3):
            m1[k, d] = net.send(outc.at[own], outc.at[own], dev(c_ax, d))
    for k in range(3):
        a_ax, b_ax, c_ax = orders[k]
        for d in (1, 3, 2):
            net.recv(m1[k, d], outc.at[rows_at(k, place[a_ax], place[b_ax], near(c_ax, -d), 16)])
        own = rows_at(k, place[a_ax], place[b_ax], None, 64)
        for d in (2, 1, 3):
            m2[k, d] = net.send(outc.at[own], outc.at[own], dev(b_ax, d))

    def to_mate(name, rows):
        mate_n[name] = (net.send(outc.at[rows], outc.at[rows], net.mate()), rows)

    for k in range(3):
        a_ax, b_ax, c_ax = orders[k]
        for d in (1, 3, 2):
            net.recv(m2[k, d], outc.at[rows_at(k, place[a_ax], near(b_ax, -d), None, 64)])
        own = rows_at(k, place[a_ax])
        for d in DIRS:
            m3[k, d] = net.send(outc.at[own], outc.at[own], dev(a_ax, d))
        to_mate((k, 0), own)
    for k in range(3):
        for d in DIRS:
            net.recv(m3[k, d], outc.at[rows_at(k, near(orders[k][0], -d))])
            rows = part(k, -d, side[d])
            m4[k, d] = net.send(outc.at[rows], outc.at[rows], dev(orders[k][0], d))
        for d in DIRS:
            to_mate((k, d), rows_at(k, near(orders[k][0], -d)))
    for k in range(3):
        for d in DIRS:
            rows = part(k, 2, side[d])
            net.recv(m4[k, d], outc.at[rows])
            to_mate((k, d, 2), rows)
    for number, rows in mate_n.values():
        net.recv(number, out.at[1 - c, rows])
    net.recv(tot_mate, s2.at[1 - c])
    tot[...] = s2[0] + s2[1]
    net.finish()


def vmem(shape, dtype):
    return pltpu.VMEM(shape, dtype)


def spec():
    return pl.BlockSpec(memory_space=pltpu.VMEM)


def call_main(scale, eimg, etxt, pair):
    cols = NROW * PAIRS
    return pl.pallas_call(
        main_kernel,
        name="scores_and_gradients",
        out_shape=(
            jax.ShapeDtypeStruct((PAIRS, EMB), F32),
            jax.ShapeDtypeStruct((PAIRS, EMB), F32),
            jax.ShapeDtypeStruct((2, 8, PAIRS), F32),
        ),
        in_specs=[pl.BlockSpec(memory_space=pltpu.SMEM), spec(), spec(), spec()],
        out_specs=(spec(), spec(), spec()),
        scratch_shapes=[
            vmem((NCOL, PAIRS, EMB), BF16),
            vmem((cols, EMB), BF16),
            vmem((NCOL, 8, PAIRS), F32),
            vmem((NCOL, PAIRS, cols), F32),
            vmem((NCOL * PAIRS, cols), BF16),
            vmem((NCOL, PAIRS, EMB), BF16),
            vmem((cols, EMB), BF16),
            vmem((2, 4, 2, 32, EMB), BF16),
            vmem((2, 4, 2, 64, EMB), BF16),
            vmem((2, 3, 64, EMB), BF16),
            vmem((2, 2, 32, EMB), BF16),
            vmem((2, 2, 64, EMB), BF16),
            vmem((4, PAIRS, EMB), BF16),
            vmem((2, 64, EMB), BF16),
            vmem((2, PAIRS, EMB), BF16),
            vmem((8, cols), F32),
            vmem((8, cols), F32),
            vmem((NCOL, PAIRS), F32),
            vmem((4, NCOL, PAIRS), F32),
            vmem((4, NCOL, PAIRS), F32),
            vmem((NROW, PAIRS), F32),
            vmem((4, NROW, PAIRS), F32),
            vmem((2, NROW, PAIRS), F32),
            vmem((2, PAIRS, PAIRS), F32),
            pltpu.SemaphoreType.DMA((128,)),
            pltpu.SemaphoreType.DMA((128,)),
        ],
        compiler_params=pltpu.CompilerParams(
            collective_id=0, has_side_effects=True, vmem_limit_bytes=56 * 1024 * 1024
        ),
        cost_estimate=pl.CostEstimate(
            flops=16 * 10**9, bytes_accessed=4 * 10**6, transcendentals=8 * 10**6
        ),
    )(scale, eimg, etxt, pair)


def call_weights(pi, pt, dzi, dzt, tile):
    rows = DI + DT + 128
    return pl.pallas_call(
        weight_kernel,
        name="weight_gradients",
        out_shape=(
            jax.ShapeDtypeStruct((2, rows, HALF), BF16),
            jax.ShapeDtypeStruct((8, 128), F32),
        ),
        in_specs=[spec()] * 5,
        out_specs=(spec(), spec()),
        scratch_shapes=[
            vmem((2 * PAIRS, DI), BF16),
            vmem((2 * PAIRS, DT), BF16),
            vmem((2 * PAIRS, HALF), BF16),
            vmem((2 * PAIRS, HALF), BF16),
            vmem((rows, HALF), BF16),
            vmem((3, 2, 128, HALF), BF16),
            vmem((3, 2, 256, HALF), BF16),
            vmem((3, 256, HALF), BF16),
            vmem((3, 3, 64, HALF), BF16),
            vmem((3, 64, HALF), BF16),
            vmem((3, 3, 16, HALF), BF16),
            vmem((3, 4, 8, 128), F32),
            vmem((2, 8, 128), F32),
            pltpu.SemaphoreType.DMA((128,)),
            pltpu.SemaphoreType.DMA((128,)),
        ],
        compiler_params=pltpu.CompilerParams(
            collective_id=1, has_side_effects=True, vmem_limit_bytes=56 * 1024 * 1024
        ),
        cost_estimate=pl.CostEstimate(
            flops=10**9, bytes_accessed=16 * 10**6, transcendentals=0
        ),
    )(pi, pt, dzi, dzt, tile)


def embed(pooled, proj):
    z = jnp.dot(pooled, proj, preferred_element_type=F32)
    norms = jnp.sqrt(jnp.sum(z * z, axis=1, keepdims=True) + EPS)
    unit = z / norms
    return (unit, norms, unit.astype(BF16))


def normal_grad(grads, unit, norms):
    inner = jnp.sum(unit * grads, axis=1, keepdims=True)
    return ((grads - unit * inner) / norms).astype(BF16)


def pooled_grad(dz, proj):
    return lax.dot_general(
        dz, proj, (((1,), (1,)), ((), ())), preferred_element_type=F32
    ).astype(BF16)


def local(image_pooled, text_pooled, image_proj, text_proj, log_scale, pair_index):
    unit_img, norm_img, emb_img = embed(image_pooled, image_proj)
    unit_txt, norm_txt, emb_txt = embed(text_pooled, text_proj)
    scale = jnp.exp(log_scale)
    img_grads, txt_grads, sums = call_main(
        scale, emb_img, emb_txt, pair_index.astype(F32).reshape(1, PAIRS)
    )
    dz_img = normal_grad(img_grads, unit_img, norm_img)
    dz_txt = normal_grad(txt_grads, unit_txt, norm_txt)
    both = jnp.sum(sums, axis=(1, 2))
    lane = lax.broadcasted_iota(jnp.int32, (8, 128), 1)
    tile = jnp.where(lane == 0, both[0], jnp.where(lane == 1, both[1], 0.0))
    weights, totals = call_weights(image_pooled, text_pooled, dz_img, dz_txt, tile)
    dpi = pooled_grad(dz_img, image_proj)
    dpt = pooled_grad(dz_txt, text_proj)
    wide = jnp.concatenate([weights[0], weights[1]], axis=1).astype(F32)
    loss = totals[0, 0:1] / (PAIRS * NROW * NCOL)
    return (loss, dpi, dpt, wide[:DI], wide[DI : DI + DT], totals[0, 1:2])


def solution(mesh):
    return jax.shard_map(
        local,
        mesh=mesh,
        in_specs=(
            P(("row", "col"), None),
            P(("col", "row"), None),
            P(),
            P(),
            P(),
            P(("row", "col")),
        ),
        out_specs=(P(), P(("row", "col"), None), P(("col", "row"), None), P(), P(), P()),
        check_vma=False,
    )
```

```python
import functools

import jax
import jax.numpy as jnp
from jax import lax
from jax.experimental import pallas as pl
from jax.experimental.pallas import tpu as pltpu
from jax.sharding import PartitionSpec as P

EPS = 1e-06
MESH = pl.DeviceIdType.MESH
F32 = jnp.float32
BF16 = jnp.bfloat16
PAIRS = 128
NCOL = 16
NROW = 8
EMB = 1280
DI = 1664
DT = 1280
HALF = EMB // 2
DIRS = (1, -1)
STEPS = (2, 1, -1, 0)
WROWS = DI + DT + 128


class Net:
    def __init__(self, send_sem, recv_sem):
        self.send_sem, self.recv_sem = send_sem, recv_sem
        row, col = lax.axis_index("row"), lax.axis_index("col")
        self.x, self.c = row // 2, row % 2
        self.y, self.z = col // 4, col % 4
        self.count = 0
        self.started = []

    def dev(self, dx=0, dy=0, dz=0):
        return (
            2 * ((self.x + dx + 4) % 4) + self.c,
            4 * ((self.y + dy + 4) % 4) + (self.z + dz + 4) % 4,
        )

    def mate(self):
        return (2 * self.x + 1 - self.c, 4 * self.y + self.z)

    def greet(self):
        others = [self.mate()]
        for d in (1, 2, 3):
            others += [self.dev(dx=d), self.dev(dy=d), self.dev(dz=d)]
        self.others = len(others)
        for other in others:
            pl.semaphore_signal(
                pltpu.get_barrier_semaphore(), inc=1, device_id=other, device_id_type=MESH
            )

    def met(self):
        pl.semaphore_wait(pltpu.get_barrier_semaphore(), self.others)

    def copy(self, number, src, dst, device):
        return pltpu.make_async_remote_copy(
            src_ref=src,
            dst_ref=dst,
            send_sem=self.send_sem.at[number],
            recv_sem=self.recv_sem.at[number],
            device_id=device,
            device_id_type=MESH,
        )

    def send(self, src, dst, device):
        number = self.count
        self.count += 1
        copy = self.copy(number, src, dst, device)
        copy.start()
        self.started.append(copy)
        return number

    def recv(self, number, dst):
        self.copy(number, dst, dst, self.mate()).wait_recv()

    def finish(self):
        for copy in self.started:
            copy.wait_send()


def lanes(column):
    return jnp.transpose(jnp.broadcast_to(column, (PAIRS, PAIRS)))[0:1, :]


def sublanes(row):
    return jnp.transpose(jnp.broadcast_to(row, (PAIRS, PAIRS)))


def lse_over(parts):
    peak = functools.reduce(jnp.maximum, parts)
    return peak + jnp.log(sum(jnp.exp(p - peak) for p in parts))


def pick(i, options):
    value = options[0]
    for n in range(1, len(options)):
        value = jnp.where(i == n, options[n], value)
    return value


def kernel(
    scale_ref, pi, pt, wi_hbm, wt_hbm, pair, out, dpi, dpt, loss_ref, dscale_ref,
    img, txt, pid, scores, gb, pimg, ptxt,
    rg1, rg2, rb, rf1, rf2, rc, rx1, rx2,
    cmax, csum, rowl, rowz, rowy, coll, colx, colc, acc,
    wi, wt, unit_i, unit_t, norm_i, norm_t, turned, dz_i, dz_t, di, dt,
    w, r1, r2, q1, r3, q2, r4, fin, s4, s2,
    send_sem, recv_sem, local_sem,
):
    net = Net(send_sem, recv_sem)
    x, c, y, z = net.x, net.c, net.y, net.z
    me_col = 4 * y + z
    scale = scale_ref[0]
    load_i = pltpu.make_async_copy(wi_hbm, wi, local_sem.at[0])
    load_t = pltpu.make_async_copy(wt_hbm, wt, local_sem.at[1])
    load_i.start()
    load_t.start()
    net.greet()

    def axes(h):
        return ((y, z), (z, y))[h]

    def gdev(h, d):
        return net.dev(dy=d) if h == 0 else net.dev(dz=d)

    def fdev(h, d):
        return net.dev(dz=d) if h == 0 else net.dev(dy=d)

    def block(h, dg, df):
        g, f = axes(h)
        g, f = (g + dg + 4) % 4, (f + df + 4) % 4
        return 4 * g + f if h == 0 else 4 * f + g

    def half(ref, q, h):
        return ref.at[q, pl.ds(64 * h, 64)]

    def sub(ref, q, h, d):
        return ref.at[q, pl.ds(64 * h + (0 if d == 1 else 32), 32)]

    def rel(dy, dz):
        return 4 * ((y + dy + 4) % 4) + (z + dz + 4) % 4

    def tblock(dx, core):
        return pl.ds(pl.multiple_of((2 * ((x + dx + 4) % 4) + core) * PAIRS, PAIRS), PAIRS)

    def tsub(dx, core, d):
        start = (2 * ((x + dx + 4) % 4) + core) * PAIRS + (0 if d == 1 else 64)
        return pl.ds(pl.multiple_of(start, 64), 64)

    mine = pl.ds(pl.multiple_of(c * PAIRS, PAIRS), PAIRS)
    other = pl.ds(pl.multiple_of((1 - c) * PAIRS, PAIRS), PAIRS)
    keep = pl.ds(pl.multiple_of(c * HALF, 128), HALF)
    give = pl.ds(pl.multiple_of((1 - c) * HALF, 128), HALF)

    def embed(pooled, proj, unit, norm):
        value = jnp.dot(pooled[...], proj[...], preferred_element_type=F32)
        norms = jnp.sqrt(jnp.sum(value * value, axis=1, keepdims=True) + EPS)
        value = value / norms
        unit[...] = value
        norm[...] = jnp.broadcast_to(norms, norm.shape)
        return value.astype(BF16)

    pid[me_col] = jnp.broadcast_to(pair[...], (8, PAIRS))
    load_i.wait()
    img[me_col] = embed(pi, wi, unit_i, norm_i)
    net.met()

    f1, g1, f2, g3, g4 = {}, {}, {}, {}, {}
    x1, x2, cx = {}, {}, {}
    pz, py = {}, {}
    for h in (0, 1):
        for d in DIRS:
            part = half(img, me_col, h)
            f1[h, d] = net.send(part, part, fdev(h, d))
    for h in (0, 1):
        for d in DIRS:
            part = half(img, me_col, h)
            g1[h, d] = net.send(part, part, gdev(h, d))
    load_t.wait()
    txt[tblock(0, c), :] = embed(pt, wt, unit_t, norm_t)
    for d in DIRS:
        part = txt.at[tblock(0, c)]
        x1[d] = net.send(part, part, net.dev(dx=d))

    def to_mate(dx):
        part = txt.at[tblock(dx, c)]
        cx[dx] = net.send(part, part, net.mate())

    to_mate(0)
    for d in (1, 2, 3):
        pz[d] = net.send(pid.at[me_col], pid.at[me_col], net.dev(dz=d))
    turned[0:DT, mine] = jnp.transpose(pt[...])
    turned[DT:, mine] = jnp.transpose(pi[...])
    turn_n = net.send(turned.at[:, mine], turned.at[:, mine], net.mate())
    cmax[...] = jnp.full_like(cmax, -1e30)
    csum[...] = jnp.zeros_like(csum)
    acc[...] = jnp.zeros_like(acc)

    for h in (0, 1):
        for d in DIRS:
            q = block(h, 0, -d)
            net.recv(f1[h, d], half(img, q, h))
            f2[h, d] = net.send(sub(img, q, h, d), sub(img, q, h, d), fdev(h, d))
            for e in DIRS:
                g3[h, -d, e] = net.send(half(img, q, h), half(img, q, h), gdev(h, e))

    def pass_on(h, j, d):
        q = block(h, -d, j)
        net.recv(g1[h, d] if j == 0 else g3[h, j, d], half(img, q, h))
        g4[h, j, d] = net.send(sub(img, q, h, d), sub(img, q, h, d), gdev(h, d))

    for h in (0, 1):
        for d in DIRS:
            pass_on(h, 0, d)
    for d in DIRS:
        net.recv(x1[d], txt.at[tblock(-d, c)])
        part = txt.at[tsub(-d, c, d)]
        x2[d] = net.send(part, part, net.dev(dx=d))
        to_mate(-d)
    for h in (0, 1):
        q = block(h, 0, 2)
        for d in DIRS:
            net.recv(f2[h, d], sub(img, q, h, d))
        for d in DIRS:
            g3[h, 2, d] = net.send(half(img, q, h), half(img, q, h), gdev(h, d))
    for d in (1, 2, 3):
        net.recv(pz[d], pid.at[rel(0, -d)])
    for d in (1, 2, 3):
        line = pid.at[pl.ds(4 * y, 4)]
        py[d] = net.send(line, line, net.dev(dy=d))
    for d in DIRS:
        net.recv(x2[d], txt.at[tsub(2, c, d)])
    to_mate(2)
    for dx in (0, 1, -1, 2):
        net.recv(cx[dx], txt.at[tblock(dx, 1 - c)])

    def score(qa, qb):
        left = jnp.concatenate([img[qa], img[qb]], axis=0)
        s2q = scale * lax.dot_general(
            left, txt[...], (((1,), (1,)), ((), ())), preferred_element_type=F32
        )
        for q, s in ((qa, s2q[:PAIRS]), (qb, s2q[PAIRS:])):
            scores[q] = s
            peak = jnp.max(s, axis=1, keepdims=True)
            total = jnp.sum(jnp.exp(s - peak), axis=1, keepdims=True)
            rowl[pl.ds(q, 1), :] = lanes(peak + jnp.log(total))
        s3 = s2q.reshape(2 * PAIRS // 8, 8, s2q.shape[1])
        old = cmax[...]
        new = jnp.maximum(old, jnp.max(s3, axis=0))
        csum[...] = csum[...] * jnp.exp(old - new) + jnp.sum(jnp.exp(s3 - new[None]), axis=0)
        cmax[...] = new

    def in_pairs(work, *pairs):
        if len(pairs) == 1:
            (a, b), (e, f) = pairs[0]
            work(rel(a, b), rel(e, f))
            return

        @pl.loop(0, len(pairs))
        def _(i):
            a, b, e, f = (pick(i, [p[m][n] for p in pairs]) for m in (0, 1) for n in (0, 1))
            work(rel(a, b), rel(e, f))

    def last_hop(j):
        for h in (0, 1):
            for d in DIRS:
                net.recv(g4[h, j, d], sub(img, block(h, 2, j), h, d))

    in_pairs(score, ((0, 0), (0, 1)))
    for h in (0, 1):
        for j in (1, -1):
            for d in DIRS:
                pass_on(h, j, d)
    in_pairs(score, ((0, -1), (1, 0)), ((-1, 0), (1, 1)))
    for h in (0, 1):
        for d in DIRS:
            pass_on(h, 2, d)
    last_hop(0)
    in_pairs(score, ((1, -1), (-1, 1)), ((-1, -1), (2, 0)))
    last_hop(1)
    last_hop(-1)
    in_pairs(score, ((0, 2), (2, 1)), ((1, 2), (2, -1)))
    last_hop(2)
    in_pairs(score, ((-1, 2), (2, 2)))

    rz, ry, lx = {}, {}, {}
    rowz[z] = rowl[...]
    for d in (1, 2, 3):
        rz[d] = net.send(rowz.at[z], rowz.at[z], net.dev(dz=d))
    peak = jnp.max(cmax[...], axis=0, keepdims=True)
    lcol = peak + jnp.log(jnp.sum(csum[...] * jnp.exp(cmax[...] - peak), axis=0, keepdims=True))
    for r in range(NROW):
        coll[r : r + 1, :] = lcol[:, r * PAIRS : (r + 1) * PAIRS]
    colx[x] = coll[...]
    for d in (1, 2, 3):
        lx[d] = net.send(colx.at[x], colx.at[x], net.dev(dx=d))
    for d in (1, 2, 3):
        net.recv(rz[d], rowz.at[(z - d + 4) % 4])
    rowy[y] = lse_over([rowz[i] for i in range(4)])
    for d in (1, 2, 3):
        ry[d] = net.send(rowy.at[y], rowy.at[y], net.dev(dy=d))
    for d in (1, 2, 3):
        net.recv(lx[d], colx.at[(x - d + 4) % 4])
    colc[c] = lse_over([colx[i] for i in range(4)])
    lc = net.send(colc.at[c], colc.at[c], net.mate())
    for d in (1, 2, 3):
        line = pid.at[pl.ds(4 * ((y - d + 4) % 4), 4)]
        net.recv(py[d], line)
    for d in (1, 2, 3):
        net.recv(ry[d], rowy.at[(y - d + 4) % 4])
    rowl[...] = lse_over([rowy[i] for i in range(4)])
    net.recv(lc, colc.at[1 - c])
    coll[...] = lse_over([colc[i] for i in range(2)])

    first = (me_col * NROW * PAIRS).astype(F32)
    place = lax.broadcasted_iota(jnp.int32, (PAIRS, PAIRS), 1).astype(F32) + first

    def grad(qa, qb):
        rows = []
        for q in (qa, qb):
            lrow = sublanes(rowl[pl.ds(q, 1), :])
            target = sublanes(pid[q][0:1, :]) - place
            hit_sum = jnp.zeros((PAIRS, PAIRS), F32)
            dot_sum = jnp.zeros((PAIRS, PAIRS), F32)
            here = pl.ds(pl.multiple_of(q * PAIRS, PAIRS), PAIRS)
            for r in range(NROW):
                at = slice(r * PAIRS, (r + 1) * PAIRS)
                s = scores[q, :, at]
                soft = 0.5 * (jnp.exp(s - lrow) + jnp.exp(s - coll[r : r + 1, :]))
                hit = (target == float(r * PAIRS)).astype(F32)
                g = soft - hit
                hit_sum += s * hit
                dot_sum += s * g
                gb[here, at] = g.astype(BF16)
            acc[0] += hit_sum
            acc[1] += dot_sum
            rows.append(gb[here, :])
        prod = jnp.dot(jnp.concatenate(rows, axis=0), txt[...], preferred_element_type=F32)
        pimg[qa] = prod[:PAIRS].astype(BF16)
        pimg[qb] = prod[PAIRS:].astype(BF16)

    rg1n, rg2n, rf1n, rf2n = {}, {}, {}, {}
    slot = {2: 0, 1: 1, -1: 2, 0: 3}
    side = {1: 0, -1: 1}

    def scatter1(h, *js):
        for j in js:
            for d in DIRS:
                q = block(h, 2, j)
                rg1n[h, j, d] = net.send(
                    sub(pimg, q, h, d), rg1.at[h, slot[j], side[d]], gdev(h, d)
                )

    def scatter2(j):
        for h in (0, 1):
            for d in DIRS:
                q = block(h, d, j)
                got = rg1.at[h, slot[j], side[d]]
                net.recv(rg1n[h, j, d], got)
                part = sub(pimg, q, h, d)
                part[...] = (part[...].astype(F32) + got[...].astype(F32)).astype(BF16)
                rg2n[h, j, d] = net.send(
                    half(pimg, q, h), rg2.at[h, slot[j], side[d]], gdev(h, d)
                )

    def line_sum(h, j):
        for d in DIRS:
            net.recv(rg2n[h, j, d], rg2.at[h, slot[j], side[d]])
        total = half(pimg, block(h, 0, j), h)[...].astype(F32)
        for d in DIRS:
            total += rg2[h, slot[j], side[d]].astype(F32)
        return total

    in_pairs(grad, ((2, 2), (2, 1)))
    scatter1(0, 2, 1)
    in_pairs(grad, ((2, -1), (2, 0)), ((1, 2), (-1, 2)))
    scatter1(0, -1, 0)
    scatter1(1, 2, 1, -1)
    in_pairs(grad, ((0, 2), (1, 1)), ((1, -1), (-1, 1)))
    scatter1(1, 0)
    scatter2(2)
    in_pairs(grad, ((-1, -1), (1, 0)), ((0, 1), (-1, 0)))
    scatter2(1)
    scatter2(-1)
    in_pairs(grad, ((0, -1), (0, 0)))
    scatter2(0)

    mate_n, tx1n, tx2n = {}, {}, {}

    def text_product(dx):
        xx = (x + dx + 4) % 4
        at = pl.ds(pl.multiple_of(xx * 2 * PAIRS, 2 * PAIRS), 2 * PAIRS)
        prod = lax.dot_general(
            gb[:, at], img[...].reshape(NCOL * PAIRS, EMB), (((0,), (0,)), ((), ())),
            preferred_element_type=F32,
        )
        ptxt[at, :] = prod.astype(BF16)
        mate_n[dx] = net.send(ptxt.at[tblock(dx, 1 - c)], rc.at[xx], net.mate())

    def text_pair(dx):
        xx = (x + dx + 4) % 4
        net.recv(mate_n[dx], rc.at[xx])
        return ptxt[tblock(dx, c), :].astype(F32) + rc[xx].astype(F32)

    text_product(2)
    text_product(1)
    for h in (0, 1):
        rb[h, 0] = line_sum(h, 2).astype(BF16)
        for d in DIRS:
            at = pl.ds(0 if d == 1 else 32, 32)
            rf1n[h, d] = net.send(rb.at[h, 0, at], rf1.at[h, side[d]], fdev(h, d))
    ptxt[tblock(2, c), :] = text_pair(2).astype(BF16)
    for d in DIRS:
        tx1n[d] = net.send(ptxt.at[tsub(2, c, d)], rx1.at[side[d]], net.dev(dx=d))
    text_product(-1)
    for d in DIRS:
        ptxt[tblock(d, c), :] = text_pair(d).astype(BF16)
        net.recv(tx1n[d], rx1.at[side[d]])
        part = ptxt.at[tsub(d, c, d)]
        part[...] = (part[...].astype(F32) + rx1[side[d]].astype(F32)).astype(BF16)
        tx2n[d] = net.send(ptxt.at[tblock(d, c)], rx2.at[side[d]], net.dev(dx=d))
    text_product(0)
    for h in (0, 1):
        for d in DIRS:
            total = line_sum(h, d)
            net.recv(rf1n[h, d], rf1.at[h, side[d]])
            extra = rf1[h, side[d]].astype(F32)
            lo, hi = total[0:32], total[32:64]
            if d == 1:
                lo = lo + extra
            else:
                hi = hi + extra
            rb[h, 1 + side[d], 0:32] = lo.astype(BF16)
            rb[h, 1 + side[d], 32:64] = hi.astype(BF16)
            rf2n[h, d] = net.send(rb.at[h, 1 + side[d]], rf2.at[h, side[d]], fdev(h, d))

    where = (x, y, z)

    def dev(axis, d):
        return net.dev(**{("dx", "dy", "dz")[axis]: d})

    tot_n = {}

    def tot_send(axis):
        own = s4.at[axis, where[axis]]
        for d in (1, 2, 3):
            tot_n[axis, d] = net.send(own, own, dev(axis, d))

    def tot_recv(axis):
        for d in (1, 2, 3):
            net.recv(tot_n[axis, d], s4.at[axis, (where[axis] - d + 4) % 4])
        return s4[axis, 0] + s4[axis, 1] + s4[axis, 2] + s4[axis, 3]

    half_lse = (0.5 / NCOL) * jnp.sum(rowl[...].reshape(2, 8, PAIRS), axis=0) + (
        0.5 / NROW
    ) * coll[...]
    s4[0, x, 0:8] = half_lse - jnp.sum(acc[0].reshape(16, 8, PAIRS), axis=0)
    s4[0, x, 8:16] = jnp.sum(acc[1].reshape(16, 8, PAIRS), axis=0)
    tot_send(0)

    def normal_grad(grads, unit, norm, dz, halves):
        u = unit[...]
        inner = jnp.sum(u * grads, axis=1, keepdims=True)
        dz[...] = ((grads - u * inner) / norm[:, 0:1]).astype(BF16)
        number = net.send(dz.at[:, give], halves.at[mine], net.mate())
        halves[mine, :] = dz[:, keep]
        return number

    total = text_pair(0)
    for d in DIRS:
        net.recv(tx2n[d], rx2.at[side[d]])
        total += rx2[side[d]].astype(F32)
    dt_n = normal_grad(scale * total, unit_t, norm_t, dz_t, dt)
    w[DI + DT :, :] = jnp.zeros((WROWS - DI - DT, HALF), BF16)
    net.recv(turn_n, turned.at[:, other])

    orders = ((0, 1, 2), (1, 2, 0), (2, 0, 1))

    def near(axis, d):
        return (where[axis] + d + 4) % 4

    def rows_at(k, a, b=None, e=None, size=256):
        start = 1024 * k + 256 * a
        if b is not None:
            start = start + 64 * b
        if e is not None:
            start = start + 16 * e
        return pl.ds(pl.multiple_of(start, 16), size)

    def part_at(k, d, s):
        return pl.ds(pl.multiple_of(1024 * k + 256 * near(orders[k][0], d) + 128 * s, 128), 128)

    def weights(first_row, rows, right):
        @pl.loop(0, rows // 128)
        def _(i):
            at = pl.ds(pl.multiple_of(first_row + i * 128, 128), 128)
            w[at, :] = jnp.dot(turned[at, :], right[...], preferred_element_type=F32).astype(BF16)

    n1, n2, n3, n4 = {}, {}, {}, {}

    def reduce1(k):
        for d in DIRS:
            n1[k, d] = net.send(
                w.at[part_at(k, 2, side[d])], r1.at[k, side[d]], dev(orders[k][0], d)
            )

    net.recv(dt_n, dt.at[other])
    weights(0, DT, dt)
    reduce1(0)

    halves = []
    for h in (0, 1):
        total = line_sum(h, 0)
        for d in DIRS:
            net.recv(rf2n[h, d], rf2.at[h, side[d]])
            total += rf2[h, side[d]].astype(F32)
        halves.append(scale * total)
    di_n = normal_grad(jnp.concatenate(halves, axis=0), unit_i, norm_i, dz_i, di)
    net.recv(di_n, di.at[other])
    weights(DT, DI, di)
    reduce1(1)
    reduce1(2)

    def pooled_grad(dz, proj, result, rows):
        @pl.loop(0, rows // 128)
        def _(i):
            at = pl.ds(pl.multiple_of(i * 128, 128), 128)
            result[:, at] = lax.dot_general(
                dz[...], proj[at, :], (((1,), (1,)), ((), ())), preferred_element_type=F32
            ).astype(BF16)

    for k in range(3):
        for d in DIRS:
            net.recv(n1[k, d], r1.at[k, side[d]])
            got = part_at(k, d, side[d])
            w[got, :] = (w[got, :].astype(F32) + r1[k, side[d]].astype(F32)).astype(BF16)
            n2[k, d] = net.send(
                w.at[rows_at(k, near(orders[k][0], d))], r2.at[k, side[d]], dev(orders[k][0], d)
            )
    s4[1, y] = tot_recv(0)
    tot_send(1)
    pooled_grad(dz_i, wi, dpi, DI)
    pooled_grad(dz_t, wt, dpt, DT)
    for k in range(3):
        a_ax, b_ax, c_ax = orders[k]
        total = w[rows_at(k, where[a_ax]), :].astype(F32)
        for d in DIRS:
            net.recv(n2[k, d], r2.at[k, side[d]])
            total += r2[k, side[d]].astype(F32)
        q1[k] = total.astype(BF16)
        for d in (2, 1, 3):
            to = pl.ds(pl.multiple_of(64 * near(b_ax, d), 64), 64)
            n3[k, d] = net.send(q1.at[k, to], r3.at[k, d - 1], dev(b_ax, d))
    s4[2, z] = tot_recv(1)
    tot_send(2)
    for k in range(3):
        a_ax, b_ax, c_ax = orders[k]
        total = q1[k, pl.ds(pl.multiple_of(64 * where[b_ax], 64), 64), :].astype(F32)
        for d in (1, 3, 2):
            net.recv(n3[k, d], r3.at[k, d - 1])
            total += r3[k, d - 1].astype(F32)
        q2[k] = total.astype(BF16)
        for d in (2, 1, 3):
            to = pl.ds(pl.multiple_of(16 * near(c_ax, d), 16), 16)
            n4[k, d] = net.send(q2.at[k, to], r4.at[k, d - 1], dev(c_ax, d))
    s2[c] = tot_recv(2)
    tot_mate = net.send(s2.at[c], s2.at[c], net.mate())

    m1, m2, m3, m4, back = {}, {}, {}, {}, {}

    def cut(rows):
        return out.at[rows, keep]

    for k in range(3):
        a_ax, b_ax, c_ax = orders[k]
        total = q2[k, pl.ds(pl.multiple_of(16 * where[c_ax], 16), 16), :].astype(F32)
        for d in (1, 3, 2):
            net.recv(n4[k, d], r4.at[k, d - 1])
            total += r4[k, d - 1].astype(F32)
        fin[k] = total.astype(BF16)
        own = cut(rows_at(k, where[a_ax], where[b_ax], where[c_ax], 16))
        for d in (2, 1, 3):
            m1[k, d] = net.send(fin.at[k], own, dev(c_ax, d))
        back[k] = pltpu.make_async_copy(fin.at[k], own, local_sem.at[2 + k])
        back[k].start()
    for k in range(3):
        a_ax, b_ax, c_ax = orders[k]
        back[k].wait()
        for d in (1, 3, 2):
            net.recv(m1[k, d], cut(rows_at(k, where[a_ax], where[b_ax], near(c_ax, -d), 16)))
        own = cut(rows_at(k, where[a_ax], where[b_ax], None, 64))
        for d in (2, 1, 3):
            m2[k, d] = net.send(own, own, dev(b_ax, d))

    over = []

    def to_mate(rows):
        over.append((net.send(cut(rows), cut(rows), net.mate()), rows))

    for k in range(3):
        a_ax, b_ax, c_ax = orders[k]
        for d in (1, 3, 2):
            net.recv(m2[k, d], cut(rows_at(k, where[a_ax], near(b_ax, -d), None, 64)))
        rows = rows_at(k, where[a_ax])
        for d in DIRS:
            m3[k, d] = net.send(cut(rows), cut(rows), dev(a_ax, d))
        to_mate(rows)
    for k in range(3):
        for d in DIRS:
            net.recv(m3[k, d], cut(rows_at(k, near(orders[k][0], -d))))
            rows = part_at(k, -d, side[d])
            m4[k, d] = net.send(cut(rows), cut(rows), dev(orders[k][0], d))
        for d in DIRS:
            to_mate(rows_at(k, near(orders[k][0], -d)))
    for k in range(3):
        for d in DIRS:
            rows = part_at(k, 2, side[d])
            net.recv(m4[k, d], cut(rows))
            to_mate(rows)
    net.recv(tot_mate, s2.at[1 - c])
    totals = s2[0] + s2[1]
    loss_ref[0] = jnp.sum(totals[0:8]) * (1.0 / (PAIRS * NROW * NCOL))
    dscale_ref[0] = jnp.sum(totals[8:16])
    for number, rows in over:
        net.recv(number, out.at[rows, give])
    net.finish()


def local(image_pooled, text_pooled, image_proj, text_proj, log_scale, pair_index):
    cols = NROW * PAIRS
    vmem = pltpu.VMEM
    held = pl.BlockSpec(memory_space=pltpu.VMEM)
    scalar = pl.BlockSpec(memory_space=pltpu.SMEM)
    far = pl.BlockSpec(memory_space=pl.ANY)
    weights, dpi, dpt, loss, dscale = pl.pallas_call(
        kernel,
        name="contrastive_loss",
        out_shape=(
            jax.ShapeDtypeStruct((WROWS, EMB), BF16),
            jax.ShapeDtypeStruct((PAIRS, DI), BF16),
            jax.ShapeDtypeStruct((PAIRS, DT), BF16),
            jax.ShapeDtypeStruct((1,), F32),
            jax.ShapeDtypeStruct((1,), F32),
        ),
        in_specs=[scalar, held, held, far, far, held],
        out_specs=(far, held, held, scalar, scalar),
        scratch_shapes=[
            vmem((NCOL, PAIRS, EMB), BF16),
            vmem((cols, EMB), BF16),
            vmem((NCOL, 8, PAIRS), F32),
            vmem((NCOL, PAIRS, cols), F32),
            vmem((NCOL * PAIRS, cols), BF16),
            vmem((NCOL, PAIRS, EMB), BF16),
            vmem((cols, EMB), BF16),
            vmem((2, 4, 2, 32, EMB), BF16),
            vmem((2, 4, 2, 64, EMB), BF16),
            vmem((2, 3, 64, EMB), BF16),
            vmem((2, 2, 32, EMB), BF16),
            vmem((2, 2, 64, EMB), BF16),
            vmem((4, PAIRS, EMB), BF16),
            vmem((2, 64, EMB), BF16),
            vmem((2, PAIRS, EMB), BF16),
            vmem((8, cols), F32),
            vmem((8, cols), F32),
            vmem((NCOL, PAIRS), F32),
            vmem((4, NCOL, PAIRS), F32),
            vmem((4, NCOL, PAIRS), F32),
            vmem((NROW, PAIRS), F32),
            vmem((4, NROW, PAIRS), F32),
            vmem((2, NROW, PAIRS), F32),
            vmem((2, PAIRS, PAIRS), F32),
            vmem((DI, EMB), BF16),
            vmem((DT, EMB), BF16),
            vmem((PAIRS, EMB), F32),
            vmem((PAIRS, EMB), F32),
            vmem((PAIRS, 128), F32),
            vmem((PAIRS, 128), F32),
            vmem((DI + DT, 2 * PAIRS), BF16),
            vmem((PAIRS, EMB), BF16),
            vmem((PAIRS, EMB), BF16),
            vmem((2 * PAIRS, HALF), BF16),
            vmem((2 * PAIRS, HALF), BF16),
            vmem((WROWS, HALF), BF16),
            vmem((3, 2, 128, HALF), BF16),
            vmem((3, 2, 256, HALF), BF16),
            vmem((3, 256, HALF), BF16),
            vmem((3, 3, 64, HALF), BF16),
            vmem((3, 64, HALF), BF16),
            vmem((3, 3, 16, HALF), BF16),
            vmem((3, 16, HALF), BF16),
            vmem((3, 4, 16, 128), F32),
            vmem((2, 16, 128), F32),
            pltpu.SemaphoreType.DMA((256,)),
            pltpu.SemaphoreType.DMA((256,)),
            pltpu.SemaphoreType.DMA((8,)),
        ],
        compiler_params=pltpu.CompilerParams(
            collective_id=0, has_side_effects=True, vmem_limit_bytes=60 * 1024 * 1024
        ),
        cost_estimate=pl.CostEstimate(
            flops=19 * 10**9, bytes_accessed=24 * 10**6, transcendentals=8 * 10**6
        ),
    )(
        jnp.exp(log_scale), image_pooled, text_pooled, image_proj, text_proj,
        pair_index.astype(F32).reshape(1, PAIRS),
    )
    dwt = weights[:DT].astype(F32)
    dwi = weights[DT : DT + DI].astype(F32)
    return (loss, dpi, dpt, dwi, dwt, dscale)


def solution(mesh):
    return jax.shard_map(
        local,
        mesh=mesh,
        in_specs=(
            P(("row", "col"), None),
            P(("col", "row"), None),
            P(),
            P(),
            P(),
            P(("row", "col")),
        ),
        out_specs=(P(), P(("row", "col"), None), P(("col", "row"), None), P(), P(), P()),
        check_vma=False,
    )
```

```python
import functools

import jax
import jax.numpy as jnp
from jax import lax
from jax.experimental import pallas as pl
from jax.experimental.pallas import tpu as pltpu
from jax.sharding import PartitionSpec as P

EPS = 1e-06
MESH = pl.DeviceIdType.MESH
F32 = jnp.float32
BF16 = jnp.bfloat16
PAIRS = 128
NCOL = 16
NROW = 8
EMB = 1280
DI = 1664
DT = 1280
HALF = EMB // 2
DIRS = (1, -1)
STEPS = (2, 1, -1, 0)
WROWS = DI + DT + 128


class Net:
    def __init__(self, send_sem, recv_sem):
        self.send_sem, self.recv_sem = send_sem, recv_sem
        row, col = lax.axis_index("row"), lax.axis_index("col")
        self.x, self.c = row // 2, row % 2
        self.y, self.z = col // 4, col % 4
        self.count = 0
        self.started = []

    def dev(self, dx=0, dy=0, dz=0):
        return (
            2 * ((self.x + dx + 4) % 4) + self.c,
            4 * ((self.y + dy + 4) % 4) + (self.z + dz + 4) % 4,
        )

    def mate(self):
        return (2 * self.x + 1 - self.c, 4 * self.y + self.z)

    def greet(self):
        others = [self.mate()]
        for d in (1, 2, 3):
            others += [self.dev(dx=d), self.dev(dy=d), self.dev(dz=d)]
        self.others = len(others)
        for other in others:
            pl.semaphore_signal(
                pltpu.get_barrier_semaphore(), inc=1, device_id=other, device_id_type=MESH
            )

    def met(self):
        pl.semaphore_wait(pltpu.get_barrier_semaphore(), self.others)

    def copy(self, number, src, dst, device):
        return pltpu.make_async_remote_copy(
            src_ref=src,
            dst_ref=dst,
            send_sem=self.send_sem.at[number],
            recv_sem=self.recv_sem.at[number],
            device_id=device,
            device_id_type=MESH,
        )

    def send(self, src, dst, device):
        number = self.count
        self.count += 1
        copy = self.copy(number, src, dst, device)
        copy.start()
        self.started.append(copy)
        return number

    def recv(self, number, dst):
        self.copy(number, dst, dst, self.mate()).wait_recv()

    def finish(self):
        for copy in self.started:
            copy.wait_send()


def lanes(column):
    return jnp.transpose(jnp.broadcast_to(column, (PAIRS, PAIRS)))[0:1, :]


def sublanes(row):
    return jnp.transpose(jnp.broadcast_to(row, (PAIRS, PAIRS)))


def lse_over(parts):
    peak = functools.reduce(jnp.maximum, parts)
    return peak + jnp.log(sum(jnp.exp(p - peak) for p in parts))


def pick(i, options):
    value = options[0]
    for n in range(1, len(options)):
        value = jnp.where(i == n, options[n], value)
    return value


def kernel(
    scale_ref, pi, pt, wi_hbm, wt_hbm, pair, out, dpi, dpt, loss_ref, dscale_ref,
    img, txt, pid, scores, gb, pimg, ptxt,
    rg1, rg2, rb, rf1, rf2, rc, rx1, rx2,
    cmax, csum, rowl, rowz, rowy, coll, colx, colc, acc,
    wi, wt, unit_i, unit_t, norm_i, norm_t, turned, dz_i, dz_t, di, dt,
    w, r1, r2, q1, r3, q2, r4, fin, s4, s2,
    send_sem, recv_sem, local_sem,
):
    net = Net(send_sem, recv_sem)
    x, c, y, z = net.x, net.c, net.y, net.z
    me_col = 4 * y + z
    scale = jnp.exp(jnp.full((8, 128), scale_ref[0], F32))[0:1, 0:1]
    load_i = pltpu.make_async_copy(wi_hbm, wi, local_sem.at[0])
    load_t = pltpu.make_async_copy(wt_hbm, wt, local_sem.at[1])
    load_i.start()
    load_t.start()
    net.greet()

    def axes(h):
        return ((y, z), (z, y))[h]

    def gdev(h, d):
        return net.dev(dy=d) if h == 0 else net.dev(dz=d)

    def fdev(h, d):
        return net.dev(dz=d) if h == 0 else net.dev(dy=d)

    def block(h, dg, df):
        g, f = axes(h)
        g, f = (g + dg + 4) % 4, (f + df + 4) % 4
        return 4 * g + f if h == 0 else 4 * f + g

    def half(ref, q, h):
        return ref.at[q, pl.ds(64 * h, 64)]

    def sub(ref, q, h, d):
        return ref.at[q, pl.ds(64 * h + (0 if d == 1 else 32), 32)]

    def rel(dy, dz):
        return 4 * ((y + dy + 4) % 4) + (z + dz + 4) % 4

    def tblock(dx, core):
        return pl.ds(pl.multiple_of((2 * ((x + dx + 4) % 4) + core) * PAIRS, PAIRS), PAIRS)

    def tsub(dx, core, d):
        start = (2 * ((x + dx + 4) % 4) + core) * PAIRS + (0 if d == 1 else 64)
        return pl.ds(pl.multiple_of(start, 64), 64)

    mine = pl.ds(pl.multiple_of(c * PAIRS, PAIRS), PAIRS)
    other = pl.ds(pl.multiple_of((1 - c) * PAIRS, PAIRS), PAIRS)
    keep = pl.ds(pl.multiple_of(c * HALF, 128), HALF)
    give = pl.ds(pl.multiple_of((1 - c) * HALF, 128), HALF)

    def embed(pooled, proj, unit, norm):
        value = jnp.dot(pooled[...], proj[...], preferred_element_type=F32)
        norms = jnp.sqrt(jnp.sum(value * value, axis=1, keepdims=True) + EPS)
        value = value / norms
        unit[...] = value
        norm[...] = jnp.broadcast_to(norms, norm.shape)
        return value.astype(BF16)

    pid[me_col] = jnp.broadcast_to(pair[...].astype(F32), (8, PAIRS))
    load_i.wait()
    img[me_col] = embed(pi, wi, unit_i, norm_i)
    net.met()

    f1, g1, f2, g3, g4 = {}, {}, {}, {}, {}
    x1, x2, cx = {}, {}, {}
    pz, py = {}, {}
    for h in (0, 1):
        for d in DIRS:
            part = half(img, me_col, h)
            f1[h, d] = net.send(part, part, fdev(h, d))
    for h in (0, 1):
        for d in DIRS:
            part = half(img, me_col, h)
            g1[h, d] = net.send(part, part, gdev(h, d))
    load_t.wait()
    txt[tblock(0, c), :] = embed(pt, wt, unit_t, norm_t)
    for d in DIRS:
        part = txt.at[tblock(0, c)]
        x1[d] = net.send(part, part, net.dev(dx=d))

    def to_mate(dx):
        part = txt.at[tblock(dx, c)]
        cx[dx] = net.send(part, part, net.mate())

    to_mate(0)
    for d in (1, 2, 3):
        pz[d] = net.send(pid.at[me_col], pid.at[me_col], net.dev(dz=d))
    turned[0:DT, mine] = jnp.transpose(pt[...])
    turned[DT:, mine] = jnp.transpose(pi[...])
    turn_n = net.send(turned.at[:, mine], turned.at[:, mine], net.mate())
    cmax[...] = jnp.full_like(cmax, -1e30)
    csum[...] = jnp.zeros_like(csum)
    acc[...] = jnp.zeros_like(acc)

    for h in (0, 1):
        for d in DIRS:
            q = block(h, 0, -d)
            net.recv(f1[h, d], half(img, q, h))
            f2[h, d] = net.send(sub(img, q, h, d), sub(img, q, h, d), fdev(h, d))
            for e in DIRS:
                g3[h, -d, e] = net.send(half(img, q, h), half(img, q, h), gdev(h, e))

    def pass_on(h, j, d):
        q = block(h, -d, j)
        net.recv(g1[h, d] if j == 0 else g3[h, j, d], half(img, q, h))
        g4[h, j, d] = net.send(sub(img, q, h, d), sub(img, q, h, d), gdev(h, d))

    for h in (0, 1):
        for d in DIRS:
            pass_on(h, 0, d)
    for d in DIRS:
        net.recv(x1[d], txt.at[tblock(-d, c)])
        part = txt.at[tsub(-d, c, d)]
        x2[d] = net.send(part, part, net.dev(dx=d))
        to_mate(-d)
    for h in (0, 1):
        q = block(h, 0, 2)
        for d in DIRS:
            net.recv(f2[h, d], sub(img, q, h, d))
        for d in DIRS:
            g3[h, 2, d] = net.send(half(img, q, h), half(img, q, h), gdev(h, d))
    for d in (1, 2, 3):
        net.recv(pz[d], pid.at[rel(0, -d)])
    for d in (1, 2, 3):
        line = pid.at[pl.ds(4 * y, 4)]
        py[d] = net.send(line, line, net.dev(dy=d))
    for d in DIRS:
        net.recv(x2[d], txt.at[tsub(2, c, d)])
    to_mate(2)
    for dx in (0, 1, -1, 2):
        net.recv(cx[dx], txt.at[tblock(dx, 1 - c)])

    def score(qa, qb):
        left = jnp.concatenate([img[qa], img[qb]], axis=0)
        s2q = scale * lax.dot_general(
            left, txt[...], (((1,), (1,)), ((), ())), preferred_element_type=F32
        )
        for q, s in ((qa, s2q[:PAIRS]), (qb, s2q[PAIRS:])):
            scores[q] = s
            peak = jnp.max(s, axis=1, keepdims=True)
            total = jnp.sum(jnp.exp(s - peak), axis=1, keepdims=True)
            rowl[pl.ds(q, 1), :] = lanes(peak + jnp.log(total))
        s3 = s2q.reshape(2 * PAIRS // 8, 8, s2q.shape[1])
        old = cmax[...]
        new = jnp.maximum(old, jnp.max(s3, axis=0))
        csum[...] = csum[...] * jnp.exp(old - new) + jnp.sum(jnp.exp(s3 - new[None]), axis=0)
        cmax[...] = new

    def in_pairs(work, *pairs):
        if len(pairs) == 1:
            (a, b), (e, f) = pairs[0]
            work(rel(a, b), rel(e, f))
            return

        @pl.loop(0, len(pairs))
        def _(i):
            a, b, e, f = (pick(i, [p[m][n] for p in pairs]) for m in (0, 1) for n in (0, 1))
            work(rel(a, b), rel(e, f))

    def last_hop(j):
        for h in (0, 1):
            for d in DIRS:
                net.recv(g4[h, j, d], sub(img, block(h, 2, j), h, d))

    in_pairs(score, ((0, 0), (0, 1)))
    for h in (0, 1):
        for j in (1, -1):
            for d in DIRS:
                pass_on(h, j, d)
    in_pairs(score, ((0, -1), (1, 0)), ((-1, 0), (1, 1)))
    for h in (0, 1):
        for d in DIRS:
            pass_on(h, 2, d)
    last_hop(0)
    in_pairs(score, ((1, -1), (-1, 1)), ((-1, -1), (2, 0)))
    last_hop(1)
    last_hop(-1)
    in_pairs(score, ((0, 2), (2, 1)), ((1, 2), (2, -1)))
    last_hop(2)
    in_pairs(score, ((-1, 2), (2, 2)))

    rz, ry, lx = {}, {}, {}
    rowz[z] = rowl[...]
    for d in (1, 2, 3):
        rz[d] = net.send(rowz.at[z], rowz.at[z], net.dev(dz=d))
    peak = jnp.max(cmax[...], axis=0, keepdims=True)
    lcol = peak + jnp.log(jnp.sum(csum[...] * jnp.exp(cmax[...] - peak), axis=0, keepdims=True))
    for r in range(NROW):
        coll[r : r + 1, :] = lcol[:, r * PAIRS : (r + 1) * PAIRS]
    colx[x] = coll[...]
    for d in (1, 2, 3):
        lx[d] = net.send(colx.at[x], colx.at[x], net.dev(dx=d))
    for d in (1, 2, 3):
        net.recv(rz[d], rowz.at[(z - d + 4) % 4])
    rowy[y] = lse_over([rowz[i] for i in range(4)])
    for d in (1, 2, 3):
        ry[d] = net.send(rowy.at[y], rowy.at[y], net.dev(dy=d))
    for d in (1, 2, 3):
        net.recv(lx[d], colx.at[(x - d + 4) % 4])
    colc[c] = lse_over([colx[i] for i in range(4)])
    lc = net.send(colc.at[c], colc.at[c], net.mate())
    for d in (1, 2, 3):
        line = pid.at[pl.ds(4 * ((y - d + 4) % 4), 4)]
        net.recv(py[d], line)
    for d in (1, 2, 3):
        net.recv(ry[d], rowy.at[(y - d + 4) % 4])
    rowl[...] = lse_over([rowy[i] for i in range(4)])
    net.recv(lc, colc.at[1 - c])
    coll[...] = lse_over([colc[i] for i in range(2)])

    first = (me_col * NROW * PAIRS).astype(F32)
    place = lax.broadcasted_iota(jnp.int32, (PAIRS, PAIRS), 1).astype(F32) + first

    def grad(qa, qb):
        rows = []
        for q in (qa, qb):
            lrow = sublanes(rowl[pl.ds(q, 1), :])
            target = sublanes(pid[q][0:1, :]) - place
            hit_sum = jnp.zeros((PAIRS, PAIRS), F32)
            dot_sum = jnp.zeros((PAIRS, PAIRS), F32)
            here = pl.ds(pl.multiple_of(q * PAIRS, PAIRS), PAIRS)
            for r in range(NROW):
                at = slice(r * PAIRS, (r + 1) * PAIRS)
                s = scores[q, :, at]
                soft = 0.5 * (jnp.exp(s - lrow) + jnp.exp(s - coll[r : r + 1, :]))
                hit = (target == float(r * PAIRS)).astype(F32)
                g = soft - hit
                hit_sum += s * hit
                dot_sum += s * g
                gb[here, at] = g.astype(BF16)
            acc[0] += hit_sum
            acc[1] += dot_sum
            rows.append(gb[here, :])
        prod = jnp.dot(jnp.concatenate(rows, axis=0), txt[...], preferred_element_type=F32)
        pimg[qa] = prod[:PAIRS].astype(BF16)
        pimg[qb] = prod[PAIRS:].astype(BF16)

    rg1n, rg2n, rf1n, rf2n = {}, {}, {}, {}
    slot = {2: 0, 1: 1, -1: 2, 0: 3}
    side = {1: 0, -1: 1}

    def scatter1(h, *js):
        for j in js:
            for d in DIRS:
                q = block(h, 2, j)
                rg1n[h, j, d] = net.send(
                    sub(pimg, q, h, d), rg1.at[h, slot[j], side[d]], gdev(h, d)
                )

    def scatter2(j):
        for h in (0, 1):
            for d in DIRS:
                q = block(h, d, j)
                got = rg1.at[h, slot[j], side[d]]
                net.recv(rg1n[h, j, d], got)
                part = sub(pimg, q, h, d)
                part[...] = (part[...].astype(F32) + got[...].astype(F32)).astype(BF16)
                rg2n[h, j, d] = net.send(
                    half(pimg, q, h), rg2.at[h, slot[j], side[d]], gdev(h, d)
                )

    def line_sum(h, j):
        for d in DIRS:
            net.recv(rg2n[h, j, d], rg2.at[h, slot[j], side[d]])
        total = half(pimg, block(h, 0, j), h)[...].astype(F32)
        for d in DIRS:
            total += rg2[h, slot[j], side[d]].astype(F32)
        return total

    in_pairs(grad, ((2, 2), (2, 1)))
    scatter1(0, 2, 1)
    scatter1(1, 2)
    in_pairs(grad, ((1, 2), (2, -1)))
    scatter1(1, 1)
    scatter1(0, -1)
    in_pairs(grad, ((-1, 2), (2, 0)))
    scatter1(1, -1)
    scatter1(0, 0)
    in_pairs(grad, ((0, 2), (1, 1)))
    scatter1(1, 0)
    scatter2(2)
    in_pairs(grad, ((1, -1), (-1, 1)), ((-1, -1), (1, 0)))
    scatter2(1)
    scatter2(-1)
    in_pairs(grad, ((0, 1), (-1, 0)), ((0, -1), (0, 0)))
    scatter2(0)

    mate_n, tx1n, tx2n = {}, {}, {}

    def text_product(dx):
        xx = (x + dx + 4) % 4
        at = pl.ds(pl.multiple_of(xx * 2 * PAIRS, 2 * PAIRS), 2 * PAIRS)
        prod = lax.dot_general(
            gb[:, at], img[...].reshape(NCOL * PAIRS, EMB), (((0,), (0,)), ((), ())),
            preferred_element_type=F32,
        )
        ptxt[at, :] = prod.astype(BF16)
        mate_n[dx] = net.send(ptxt.at[tblock(dx, 1 - c)], rc.at[xx], net.mate())

    def text_pair(dx):
        xx = (x + dx + 4) % 4
        net.recv(mate_n[dx], rc.at[xx])
        return ptxt[tblock(dx, c), :].astype(F32) + rc[xx].astype(F32)

    text_product(2)
    text_product(1)
    for h in (0, 1):
        rb[h, 0] = line_sum(h, 2).astype(BF16)
        for d in DIRS:
            at = pl.ds(0 if d == 1 else 32, 32)
            rf1n[h, d] = net.send(rb.at[h, 0, at], rf1.at[h, side[d]], fdev(h, d))
    ptxt[tblock(2, c), :] = text_pair(2).astype(BF16)
    for d in DIRS:
        tx1n[d] = net.send(ptxt.at[tsub(2, c, d)], rx1.at[side[d]], net.dev(dx=d))
    text_product(-1)
    for d in DIRS:
        ptxt[tblock(d, c), :] = text_pair(d).astype(BF16)
        net.recv(tx1n[d], rx1.at[side[d]])
        part = ptxt.at[tsub(d, c, d)]
        part[...] = (part[...].astype(F32) + rx1[side[d]].astype(F32)).astype(BF16)
        tx2n[d] = net.send(ptxt.at[tblock(d, c)], rx2.at[side[d]], net.dev(dx=d))
    text_product(0)
    for h in (0, 1):
        for d in DIRS:
            total = line_sum(h, d)
            net.recv(rf1n[h, d], rf1.at[h, side[d]])
            extra = rf1[h, side[d]].astype(F32)
            lo, hi = total[0:32], total[32:64]
            if d == 1:
                lo = lo + extra
            else:
                hi = hi + extra
            rb[h, 1 + side[d], 0:32] = lo.astype(BF16)
            rb[h, 1 + side[d], 32:64] = hi.astype(BF16)
            rf2n[h, d] = net.send(rb.at[h, 1 + side[d]], rf2.at[h, side[d]], fdev(h, d))

    where = (x, y, z)

    def dev(axis, d):
        return net.dev(**{("dx", "dy", "dz")[axis]: d})

    tot_n = {}

    def tot_send(axis):
        own = s4.at[axis, where[axis]]
        for d in (1, 2, 3):
            tot_n[axis, d] = net.send(own, own, dev(axis, d))

    def tot_recv(axis):
        for d in (1, 2, 3):
            net.recv(tot_n[axis, d], s4.at[axis, (where[axis] - d + 4) % 4])
        return s4[axis, 0] + s4[axis, 1] + s4[axis, 2] + s4[axis, 3]

    half_lse = (0.5 / NCOL) * jnp.sum(rowl[...].reshape(2, 8, PAIRS), axis=0) + (
        0.5 / NROW
    ) * coll[...]
    s4[0, x, 0:8] = half_lse - jnp.sum(acc[0].reshape(16, 8, PAIRS), axis=0)
    s4[0, x, 8:16] = jnp.sum(acc[1].reshape(16, 8, PAIRS), axis=0)
    tot_send(0)

    def normal_grad(grads, unit, norm, dz, halves):
        u = unit[...]
        inner = jnp.sum(u * grads, axis=1, keepdims=True)
        dz[...] = ((grads - u * inner) / norm[:, 0:1]).astype(BF16)
        number = net.send(dz.at[:, give], halves.at[mine], net.mate())
        halves[mine, :] = dz[:, keep]
        return number

    total = text_pair(0)
    for d in DIRS:
        net.recv(tx2n[d], rx2.at[side[d]])
        total += rx2[side[d]].astype(F32)
    dt_n = normal_grad(scale * total, unit_t, norm_t, dz_t, dt)
    w[DI + DT :, :] = jnp.zeros((WROWS - DI - DT, HALF), BF16)
    net.recv(turn_n, turned.at[:, other])

    orders = ((0, 1, 2), (1, 2, 0), (2, 0, 1))

    def near(axis, d):
        return (where[axis] + d + 4) % 4

    def rows_at(k, a, b=None, e=None, size=256):
        start = 1024 * k + 256 * a
        if b is not None:
            start = start + 64 * b
        if e is not None:
            start = start + 16 * e
        return pl.ds(pl.multiple_of(start, 16), size)

    def part_at(k, d, s):
        return pl.ds(pl.multiple_of(1024 * k + 256 * near(orders[k][0], d) + 128 * s, 128), 128)

    def weights(first_row, rows, right):
        @pl.loop(0, rows // 128)
        def _(i):
            at = pl.ds(pl.multiple_of(first_row + i * 128, 128), 128)
            w[at, :] = jnp.dot(turned[at, :], right[...], preferred_element_type=F32).astype(BF16)

    wide = [(k, 0, 384) for k in range(3)]
    slim = [(k, 384, 256) for k in range(3)]
    n1, n2, n3, n4 = {}, {}, {}, {}
    m1, m2, m3, m4, back = {}, {}, {}, {}, {}
    over = []

    def step(k, d):
        return dev(orders[k][0], d)

    def cut(ch, rows):
        start = pl.multiple_of(c * HALF + ch[1], 128)
        return out.at[rows, pl.ds(start, ch[2])]

    def at_mate(ch, rows):
        start = pl.multiple_of((1 - c) * HALF + ch[1], 128)
        return out.at[rows, pl.ds(start, ch[2])]

    def to_mate_w(ch, rows):
        over.append((net.send(cut(ch, rows), cut(ch, rows), net.mate()), ch, rows))

    def reduce1(ch):
        k, lane = ch[0], pl.ds(ch[1], ch[2])
        for d in DIRS:
            n1[ch, d] = net.send(
                w.at[part_at(k, 2, side[d]), lane], r1.at[k, side[d], :, lane], step(k, d)
            )

    def reduce2(ch):
        k, lane = ch[0], pl.ds(ch[1], ch[2])
        for d in DIRS:
            net.recv(n1[ch, d], r1.at[k, side[d], :, lane])
            got = part_at(k, d, side[d])
            w[got, lane] = (w[got, lane].astype(F32) + r1[k, side[d], :, lane].astype(F32)).astype(
                BF16
            )
            n2[ch, d] = net.send(
                w.at[rows_at(k, near(orders[k][0], d)), lane], r2.at[k, side[d], :, lane],
                step(k, d),
            )

    def reduce3(ch):
        k, lane = ch[0], pl.ds(ch[1], ch[2])
        a_ax, b_ax, _ = orders[k]
        total = w[rows_at(k, where[a_ax]), lane].astype(F32)
        for d in DIRS:
            net.recv(n2[ch, d], r2.at[k, side[d], :, lane])
            total += r2[k, side[d], :, lane].astype(F32)
        q1[k, :, lane] = total.astype(BF16)
        for d in (2, 1, 3):
            to = pl.ds(pl.multiple_of(64 * near(b_ax, d), 64), 64)
            n3[ch, d] = net.send(q1.at[k, to, lane], r3.at[k, d - 1, :, lane], dev(b_ax, d))

    def reduce4(ch):
        k, lane = ch[0], pl.ds(ch[1], ch[2])
        _, b_ax, c_ax = orders[k]
        total = q1[k, pl.ds(pl.multiple_of(64 * where[b_ax], 64), 64), lane].astype(F32)
        for d in (1, 3, 2):
            net.recv(n3[ch, d], r3.at[k, d - 1, :, lane])
            total += r3[k, d - 1, :, lane].astype(F32)
        q2[k, :, lane] = total.astype(BF16)
        for d in (2, 1, 3):
            to = pl.ds(pl.multiple_of(16 * near(c_ax, d), 16), 16)
            n4[ch, d] = net.send(q2.at[k, to, lane], r4.at[k, d - 1, :, lane], dev(c_ax, d))

    def gather1(ch):
        k, lane = ch[0], pl.ds(ch[1], ch[2])
        a_ax, b_ax, c_ax = orders[k]
        total = q2[k, pl.ds(pl.multiple_of(16 * where[c_ax], 16), 16), lane].astype(F32)
        for d in (1, 3, 2):
            net.recv(n4[ch, d], r4.at[k, d - 1, :, lane])
            total += r4[k, d - 1, :, lane].astype(F32)
        fin[k, :, lane] = total.astype(BF16)
        own = cut(ch, rows_at(k, where[a_ax], where[b_ax], where[c_ax], 16))
        for d in (2, 1, 3):
            m1[ch, d] = net.send(fin.at[k, :, lane], own, dev(c_ax, d))
        back[ch] = pltpu.make_async_copy(fin.at[k, :, lane], own, local_sem.at[2 + len(back)])
        back[ch].start()

    def gather2(ch):
        k = ch[0]
        a_ax, b_ax, c_ax = orders[k]
        back[ch].wait()
        for d in (1, 3, 2):
            rows = rows_at(k, where[a_ax], where[b_ax], near(c_ax, -d), 16)
            net.recv(m1[ch, d], cut(ch, rows))
        own = cut(ch, rows_at(k, where[a_ax], where[b_ax], None, 64))
        for d in (2, 1, 3):
            m2[ch, d] = net.send(own, own, dev(b_ax, d))

    def gather3(ch):
        k = ch[0]
        a_ax, b_ax, _ = orders[k]
        for d in (1, 3, 2):
            net.recv(m2[ch, d], cut(ch, rows_at(k, where[a_ax], near(b_ax, -d), None, 64)))
        rows = rows_at(k, where[a_ax])
        for d in DIRS:
            m3[ch, d] = net.send(cut(ch, rows), cut(ch, rows), step(k, d))
        to_mate_w(ch, rows)

    def gather4(ch):
        k = ch[0]
        for d in DIRS:
            net.recv(m3[ch, d], cut(ch, rows_at(k, near(orders[k][0], -d))))
            rows = cut(ch, part_at(k, -d, side[d]))
            m4[ch, d] = net.send(rows, rows, step(k, d))
        for d in DIRS:
            to_mate_w(ch, rows_at(k, near(orders[k][0], -d)))

    def gather5(ch):
        for d in DIRS:
            rows = part_at(ch[0], 2, side[d])
            net.recv(m4[ch, d], cut(ch, rows))
            to_mate_w(ch, rows)

    def each(work, *chunks):
        for ch in chunks:
            work(ch)

    early = (wide[0], slim[0])
    lead = (wide[1], wide[2])
    tail = (slim[1], slim[2])

    net.recv(dt_n, dt.at[other])
    weights(0, DT, dt)
    each(reduce1, *early)

    halves = []
    for h in (0, 1):
        total = line_sum(h, 0)
        for d in DIRS:
            net.recv(rf2n[h, d], rf2.at[h, side[d]])
            total += rf2[h, side[d]].astype(F32)
        halves.append(scale * total)
    di_n = normal_grad(jnp.concatenate(halves, axis=0), unit_i, norm_i, dz_i, di)
    each(reduce2, *early)
    net.recv(di_n, di.at[other])
    weights(DT, DI, di)
    each(reduce1, *lead)
    each(reduce1, *tail)

    def pooled_grad(dz, proj, result, rows):
        @pl.loop(0, rows // 128)
        def _(i):
            at = pl.ds(pl.multiple_of(i * 128, 128), 128)
            result[:, at] = lax.dot_general(
                dz[...], proj[at, :], (((1,), (1,)), ((), ())), preferred_element_type=F32
            ).astype(BF16)

    pooled_grad(dz_i, wi, dpi, DI)
    each(reduce2, *lead)
    each(reduce3, *early)
    each(reduce2, *tail)
    s4[1, y] = tot_recv(0)
    tot_send(1)
    pooled_grad(dz_t, wt, dpt, DT)
    each(reduce3, *lead)
    each(reduce4, *early)
    each(reduce3, *tail)
    s4[2, z] = tot_recv(1)
    tot_send(2)
    each(reduce4, *lead)
    each(gather1, *early)
    each(reduce4, *tail)
    s2[c] = tot_recv(2)
    tot_mate = net.send(s2.at[c], s2.at[c], net.mate())
    each(gather1, *lead)
    each(gather2, *early)
    each(gather1, *tail)
    each(gather2, *lead)
    each(gather3, *early)
    each(gather2, *tail)
    each(gather3, *lead)
    each(gather4, *early)
    each(gather3, *tail)
    each(gather4, *lead)
    each(gather5, *early)
    each(gather4, *tail)
    each(gather5, *lead)
    each(gather5, *tail)
    net.recv(tot_mate, s2.at[1 - c])
    totals = s2[0] + s2[1]
    loss_ref[0] = jnp.sum(totals[0:8]) * (1.0 / (PAIRS * NROW * NCOL))
    dscale_ref[0] = jnp.sum(totals[8:16])
    for number, ch, rows in over:
        net.recv(number, at_mate(ch, rows))
    net.finish()


def local(image_pooled, text_pooled, image_proj, text_proj, log_scale, pair_index):
    cols = NROW * PAIRS
    vmem = pltpu.VMEM
    held = pl.BlockSpec(memory_space=pltpu.VMEM)
    scalar = pl.BlockSpec(memory_space=pltpu.SMEM)
    far = pl.BlockSpec(memory_space=pl.ANY)
    weights, dpi, dpt, loss, dscale = pl.pallas_call(
        kernel,
        name="contrastive_loss",
        out_shape=(
            jax.ShapeDtypeStruct((WROWS, EMB), BF16),
            jax.ShapeDtypeStruct((PAIRS, DI), BF16),
            jax.ShapeDtypeStruct((PAIRS, DT), BF16),
            jax.ShapeDtypeStruct((1,), F32),
            jax.ShapeDtypeStruct((1,), F32),
        ),
        in_specs=[scalar, held, held, far, far, held],
        out_specs=(far, held, held, scalar, scalar),
        scratch_shapes=[
            vmem((NCOL, PAIRS, EMB), BF16),
            vmem((cols, EMB), BF16),
            vmem((NCOL, 8, PAIRS), F32),
            vmem((NCOL, PAIRS, cols), F32),
            vmem((NCOL * PAIRS, cols), BF16),
            vmem((NCOL, PAIRS, EMB), BF16),
            vmem((cols, EMB), BF16),
            vmem((2, 4, 2, 32, EMB), BF16),
            vmem((2, 4, 2, 64, EMB), BF16),
            vmem((2, 3, 64, EMB), BF16),
            vmem((2, 2, 32, EMB), BF16),
            vmem((2, 2, 64, EMB), BF16),
            vmem((4, PAIRS, EMB), BF16),
            vmem((2, 64, EMB), BF16),
            vmem((2, PAIRS, EMB), BF16),
            vmem((8, cols), F32),
            vmem((8, cols), F32),
            vmem((NCOL, PAIRS), F32),
            vmem((4, NCOL, PAIRS), F32),
            vmem((4, NCOL, PAIRS), F32),
            vmem((NROW, PAIRS), F32),
            vmem((4, NROW, PAIRS), F32),
            vmem((2, NROW, PAIRS), F32),
            vmem((2, PAIRS, PAIRS), F32),
            vmem((DI, EMB), BF16),
            vmem((DT, EMB), BF16),
            vmem((PAIRS, EMB), F32),
            vmem((PAIRS, EMB), F32),
            vmem((PAIRS, 128), F32),
            vmem((PAIRS, 128), F32),
            vmem((DI + DT, 2 * PAIRS), BF16),
            vmem((PAIRS, EMB), BF16),
            vmem((PAIRS, EMB), BF16),
            vmem((2 * PAIRS, HALF), BF16),
            vmem((2 * PAIRS, HALF), BF16),
            vmem((WROWS, HALF), BF16),
            vmem((3, 2, 128, HALF), BF16),
            vmem((3, 2, 256, HALF), BF16),
            vmem((3, 256, HALF), BF16),
            vmem((3, 3, 64, HALF), BF16),
            vmem((3, 64, HALF), BF16),
            vmem((3, 3, 16, HALF), BF16),
            vmem((3, 16, HALF), BF16),
            vmem((3, 4, 16, 128), F32),
            vmem((2, 16, 128), F32),
            pltpu.SemaphoreType.DMA((288,)),
            pltpu.SemaphoreType.DMA((288,)),
            pltpu.SemaphoreType.DMA((8,)),
        ],
        compiler_params=pltpu.CompilerParams(
            collective_id=0, has_side_effects=True, vmem_limit_bytes=60 * 1024 * 1024
        ),
        cost_estimate=pl.CostEstimate(
            flops=19 * 10**9, bytes_accessed=24 * 10**6, transcendentals=8 * 10**6
        ),
    )(
        log_scale, image_pooled, text_pooled, image_proj, text_proj,
        pair_index.reshape(1, PAIRS),
    )
    dwt = weights[:DT].astype(F32)
    dwi = weights[DT : DT + DI].astype(F32)
    return (loss, dpi, dpt, dwi, dwt, dscale)


def solution(mesh):
    return jax.shard_map(
        local,
        mesh=mesh,
        in_specs=(
            P(("row", "col"), None),
            P(("col", "row"), None),
            P(),
            P(),
            P(),
            P(("row", "col")),
        ),
        out_specs=(P(), P(("row", "col"), None), P(("col", "row"), None), P(), P(), P()),
        check_vma=False,
    )
```

```python
import functools

import jax
import jax.numpy as jnp
from jax import lax
from jax.experimental import pallas as pl
from jax.experimental.pallas import tpu as pltpu
from jax.sharding import PartitionSpec as P

EPS = 1e-06
MESH = pl.DeviceIdType.MESH
F32 = jnp.float32
BF16 = jnp.bfloat16
PAIRS = 128
NCOL = 16
NROW = 8
EMB = 1280
DI = 1664
DT = 1280
HALF = EMB // 2
DIRS = (1, -1)
STEPS = (2, 1, -1, 0)
WROWS = DI + DT + 128


class Net:
    def __init__(self, send_sem, recv_sem):
        self.send_sem, self.recv_sem = send_sem, recv_sem
        row, col = lax.axis_index("row"), lax.axis_index("col")
        self.x, self.c = row // 2, row % 2
        self.y, self.z = col // 4, col % 4
        self.count = 0
        self.started = {}

    def dev(self, dx=0, dy=0, dz=0):
        return (
            2 * ((self.x + dx + 4) % 4) + self.c,
            4 * ((self.y + dy + 4) % 4) + (self.z + dz + 4) % 4,
        )

    def mate(self):
        return (2 * self.x + 1 - self.c, 4 * self.y + self.z)

    def greet(self):
        others = [self.mate()]
        for d in (1, 2, 3):
            others += [self.dev(dx=d), self.dev(dy=d), self.dev(dz=d)]
        self.others = len(others)
        for other in others:
            pl.semaphore_signal(
                pltpu.get_barrier_semaphore(), inc=1, device_id=other, device_id_type=MESH
            )

    def met(self):
        pl.semaphore_wait(pltpu.get_barrier_semaphore(), self.others)

    def copy(self, number, src, dst, device):
        return pltpu.make_async_remote_copy(
            src_ref=src,
            dst_ref=dst,
            send_sem=self.send_sem.at[number],
            recv_sem=self.recv_sem.at[number],
            device_id=device,
            device_id_type=MESH,
        )

    def send(self, src, dst, device):
        number = self.count
        self.count += 1
        copy = self.copy(number, src, dst, device)
        copy.start()
        self.started[number] = copy
        return number

    def recv(self, number, dst):
        self.copy(number, dst, dst, self.mate()).wait_recv()

    def drain(self, numbers):
        for number in numbers:
            self.started.pop(number).wait_send()

    def finish(self):
        for copy in self.started.values():
            copy.wait_send()


def lanes(column):
    return jnp.transpose(jnp.broadcast_to(column, (PAIRS, PAIRS)))[0:1, :]


def sublanes(row):
    return jnp.transpose(jnp.broadcast_to(row, (PAIRS, PAIRS)))


def lse_over(parts):
    peak = functools.reduce(jnp.maximum, parts)
    return peak + jnp.log(sum(jnp.exp(p - peak) for p in parts))


def pick(i, options):
    value = options[0]
    for n in range(1, len(options)):
        value = jnp.where(i == n, options[n], value)
    return value


def kernel(
    scale_ref, pi, pt, wi_hbm, wt_hbm, pair, out, dpi, dpt, loss_ref, dscale_ref,
    img, txt, pid, scores, gb, pimg, ptxt,
    rg1, rg2, rb, rf1, rf2, rc, rx1, rx2,
    cmax, csum, rowl, rowz, rowy, coll, colx, colc, acc,
    wi, wt, unit_i, unit_t, norm_i, norm_t, turned, dz_i, dz_t, di, dt,
    w, r1, r2, q1, r3, q2, r4, fin, s4, s2,
    send_sem, recv_sem, local_sem,
):
    net = Net(send_sem, recv_sem)
    x, c, y, z = net.x, net.c, net.y, net.z
    me_col = 4 * y + z
    scale = jnp.exp(jnp.full((8, 128), scale_ref[0], F32))[0:1, 0:1]
    load_i = pltpu.make_async_copy(wi_hbm, wi, local_sem.at[0])
    load_t = pltpu.make_async_copy(wt_hbm, wt, local_sem.at[1])
    load_i.start()
    load_t.start()
    net.greet()

    def axes(h):
        return ((y, z), (z, y))[h]

    def gdev(h, d):
        return net.dev(dy=d) if h == 0 else net.dev(dz=d)

    def fdev(h, d):
        return net.dev(dz=d) if h == 0 else net.dev(dy=d)

    def block(h, dg, df):
        g, f = axes(h)
        g, f = (g + dg + 4) % 4, (f + df + 4) % 4
        return 4 * g + f if h == 0 else 4 * f + g

    def half(ref, q, h):
        return ref.at[q, pl.ds(64 * h, 64)]

    def sub(ref, q, h, d):
        return ref.at[q, pl.ds(64 * h + (0 if d == 1 else 32), 32)]

    def rel(dy, dz):
        return 4 * ((y + dy + 4) % 4) + (z + dz + 4) % 4

    def tblock(dx, core):
        return pl.ds(pl.multiple_of((2 * ((x + dx + 4) % 4) + core) * PAIRS, PAIRS), PAIRS)

    def tsub(dx, core, d):
        start = (2 * ((x + dx + 4) % 4) + core) * PAIRS + (0 if d == 1 else 64)
        return pl.ds(pl.multiple_of(start, 64), 64)

    mine = pl.ds(pl.multiple_of(c * PAIRS, PAIRS), PAIRS)
    other = pl.ds(pl.multiple_of((1 - c) * PAIRS, PAIRS), PAIRS)
    keep = pl.ds(pl.multiple_of(c * HALF, 128), HALF)
    give = pl.ds(pl.multiple_of((1 - c) * HALF, 128), HALF)

    def embed(pooled, proj, unit, norm):
        value = jnp.dot(pooled[...], proj[...], preferred_element_type=F32)
        norms = jnp.sqrt(jnp.sum(value * value, axis=1, keepdims=True) + EPS)
        value = value / norms
        unit[...] = value
        norm[...] = jnp.broadcast_to(norms, norm.shape)
        return value.astype(BF16)

    pid[me_col] = jnp.broadcast_to(pair[...].astype(F32), (8, PAIRS))
    load_i.wait()
    img[me_col] = embed(pi, wi, unit_i, norm_i)
    net.met()

    f1, g1, f2, g3, g4 = {}, {}, {}, {}, {}
    x1, x2, cx = {}, {}, {}
    pz, py = {}, {}
    for h in (0, 1):
        for d in DIRS:
            part = half(img, me_col, h)
            f1[h, d] = net.send(part, part, fdev(h, d))
    load_t.wait()
    txt[tblock(0, c), :] = embed(pt, wt, unit_t, norm_t)
    for d in DIRS:
        part = txt.at[tblock(0, c)]
        x1[d] = net.send(part, part, net.dev(dx=d))
    net.drain(f1.values())
    for h in (0, 1):
        for d in DIRS:
            part = half(img, me_col, h)
            g1[h, d] = net.send(part, part, gdev(h, d))

    def to_mate(dx):
        part = txt.at[tblock(dx, c)]
        cx[dx] = net.send(part, part, net.mate())

    to_mate(0)
    for d in (1, 2, 3):
        pz[d] = net.send(pid.at[me_col], pid.at[me_col], net.dev(dz=d))
    turned[0:DT, mine] = jnp.transpose(pt[...])
    turned[DT:, mine] = jnp.transpose(pi[...])
    turn_n = net.send(turned.at[:, mine], turned.at[:, mine], net.mate())
    cmax[...] = jnp.full_like(cmax, -1e30)
    csum[...] = jnp.zeros_like(csum)
    acc[...] = jnp.zeros_like(acc)

    for h in (0, 1):
        for d in DIRS:
            q = block(h, 0, -d)
            net.recv(f1[h, d], half(img, q, h))
            f2[h, d] = net.send(sub(img, q, h, d), sub(img, q, h, d), fdev(h, d))
            for e in DIRS:
                g3[h, -d, e] = net.send(half(img, q, h), half(img, q, h), gdev(h, e))

    def pass_on(h, j, d):
        q = block(h, -d, j)
        net.recv(g1[h, d] if j == 0 else g3[h, j, d], half(img, q, h))
        g4[h, j, d] = net.send(sub(img, q, h, d), sub(img, q, h, d), gdev(h, d))

    for h in (0, 1):
        for d in DIRS:
            pass_on(h, 0, d)
    for d in DIRS:
        net.recv(x1[d], txt.at[tblock(-d, c)])
        part = txt.at[tsub(-d, c, d)]
        x2[d] = net.send(part, part, net.dev(dx=d))
        to_mate(-d)
    for h in (0, 1):
        q = block(h, 0, 2)
        for d in DIRS:
            net.recv(f2[h, d], sub(img, q, h, d))
        for d in DIRS:
            g3[h, 2, d] = net.send(half(img, q, h), half(img, q, h), gdev(h, d))
    for d in (1, 2, 3):
        net.recv(pz[d], pid.at[rel(0, -d)])
    for d in (1, 2, 3):
        line = pid.at[pl.ds(4 * y, 4)]
        py[d] = net.send(line, line, net.dev(dy=d))
    for d in DIRS:
        net.recv(x2[d], txt.at[tsub(2, c, d)])
    to_mate(2)
    for dx in (0, 1, -1, 2):
        net.recv(cx[dx], txt.at[tblock(dx, 1 - c)])

    def score(qa, qb):
        left = jnp.concatenate([img[qa], img[qb]], axis=0)
        s2q = scale * lax.dot_general(
            left, txt[...], (((1,), (1,)), ((), ())), preferred_element_type=F32
        )
        for q, s in ((qa, s2q[:PAIRS]), (qb, s2q[PAIRS:])):
            scores[q] = s
            peak = jnp.max(s, axis=1, keepdims=True)
            total = jnp.sum(jnp.exp(s - peak), axis=1, keepdims=True)
            rowl[pl.ds(q, 1), :] = lanes(peak + jnp.log(total))
        s3 = s2q.reshape(2 * PAIRS // 8, 8, s2q.shape[1])
        old = cmax[...]
        new = jnp.maximum(old, jnp.max(s3, axis=0))
        csum[...] = csum[...] * jnp.exp(old - new) + jnp.sum(jnp.exp(s3 - new[None]), axis=0)
        cmax[...] = new

    def in_pairs(work, *pairs):
        if len(pairs) == 1:
            (a, b), (e, f) = pairs[0]
            work(rel(a, b), rel(e, f))
            return

        @pl.loop(0, len(pairs))
        def _(i):
            a, b, e, f = (pick(i, [p[m][n] for p in pairs]) for m in (0, 1) for n in (0, 1))
            work(rel(a, b), rel(e, f))

    def last_hop(j):
        for h in (0, 1):
            for d in DIRS:
                net.recv(g4[h, j, d], sub(img, block(h, 2, j), h, d))

    in_pairs(score, ((0, 0), (0, 1)))
    for h in (0, 1):
        for j in (1, -1):
            for d in DIRS:
                pass_on(h, j, d)
    in_pairs(score, ((0, -1), (1, 0)), ((-1, 0), (1, 1)))
    for h in (0, 1):
        for d in DIRS:
            pass_on(h, 2, d)
    last_hop(0)
    in_pairs(score, ((1, -1), (-1, 1)), ((-1, -1), (2, 0)))
    last_hop(1)
    last_hop(-1)
    in_pairs(score, ((0, 2), (2, 1)), ((1, 2), (2, -1)))
    last_hop(2)
    in_pairs(score, ((-1, 2), (2, 2)))

    rz, ry, lx = {}, {}, {}
    rowz[z] = rowl[...]
    for d in (1, 2, 3):
        rz[d] = net.send(rowz.at[z], rowz.at[z], net.dev(dz=d))
    peak = jnp.max(cmax[...], axis=0, keepdims=True)
    lcol = peak + jnp.log(jnp.sum(csum[...] * jnp.exp(cmax[...] - peak), axis=0, keepdims=True))
    for r in range(NROW):
        coll[r : r + 1, :] = lcol[:, r * PAIRS : (r + 1) * PAIRS]
    colx[x] = coll[...]
    for d in (1, 2, 3):
        lx[d] = net.send(colx.at[x], colx.at[x], net.dev(dx=d))
    for d in (1, 2, 3):
        net.recv(rz[d], rowz.at[(z - d + 4) % 4])
    rowy[y] = lse_over([rowz[i] for i in range(4)])
    for d in (1, 2, 3):
        ry[d] = net.send(rowy.at[y], rowy.at[y], net.dev(dy=d))
    for d in (1, 2, 3):
        net.recv(lx[d], colx.at[(x - d + 4) % 4])
    colc[c] = lse_over([colx[i] for i in range(4)])
    lc = net.send(colc.at[c], colc.at[c], net.mate())
    for d in (1, 2, 3):
        line = pid.at[pl.ds(4 * ((y - d + 4) % 4), 4)]
        net.recv(py[d], line)
    for d in (1, 2, 3):
        net.recv(ry[d], rowy.at[(y - d + 4) % 4])
    rowl[...] = lse_over([rowy[i] for i in range(4)])
    net.recv(lc, colc.at[1 - c])
    coll[...] = lse_over([colc[i] for i in range(2)])

    first = (me_col * NROW * PAIRS).astype(F32)
    place = lax.broadcasted_iota(jnp.int32, (PAIRS, PAIRS), 1).astype(F32) + first

    def soft_grad(*pair_of):
        for q in pair_of:
            lrow = sublanes(rowl[pl.ds(q, 1), :])
            target = sublanes(pid[q][0:1, :]) - place
            hit_sum = jnp.zeros((PAIRS, PAIRS), F32)
            dot_sum = jnp.zeros((PAIRS, PAIRS), F32)
            here = pl.ds(pl.multiple_of(q * PAIRS, PAIRS), PAIRS)
            for r in range(NROW):
                at = slice(r * PAIRS, (r + 1) * PAIRS)
                s = scores[q, :, at]
                soft = 0.5 * (jnp.exp(s - lrow) + jnp.exp(s - coll[r : r + 1, :]))
                hit = (target == float(r * PAIRS)).astype(F32)
                g = soft - hit
                hit_sum += s * hit
                dot_sum += s * g
                gb[here, at] = g.astype(BF16)
            acc[0] += hit_sum
            acc[1] += dot_sum

    def image_product(qa, qb):
        rows = [gb[pl.ds(pl.multiple_of(q * PAIRS, PAIRS), PAIRS), :] for q in (qa, qb)]
        prod = jnp.dot(jnp.concatenate(rows, axis=0), txt[...], preferred_element_type=F32)
        pimg[qa] = prod[:PAIRS].astype(BF16)
        pimg[qb] = prod[PAIRS:].astype(BF16)

    def grad(qa, qb):
        soft_grad(qa, qb)
        image_product(qa, qb)

    rg1n, rg2n, rf1n, rf2n = {}, {}, {}, {}
    slot = {2: 0, 1: 1, -1: 2, 0: 3}
    side = {1: 0, -1: 1}

    def scatter1(h, *js):
        for j in js:
            for d in DIRS:
                q = block(h, 2, j)
                rg1n[h, j, d] = net.send(
                    sub(pimg, q, h, d), rg1.at[h, slot[j], side[d]], gdev(h, d)
                )

    def scatter2(j):
        for h in (0, 1):
            for d in DIRS:
                q = block(h, d, j)
                got = rg1.at[h, slot[j], side[d]]
                net.recv(rg1n[h, j, d], got)
                part = sub(pimg, q, h, d)
                part[...] = (part[...].astype(F32) + got[...].astype(F32)).astype(BF16)
                rg2n[h, j, d] = net.send(
                    half(pimg, q, h), rg2.at[h, slot[j], side[d]], gdev(h, d)
                )

    def line_sum(h, j):
        for d in DIRS:
            net.recv(rg2n[h, j, d], rg2.at[h, slot[j], side[d]])
        total = half(pimg, block(h, 0, j), h)[...].astype(F32)
        for d in DIRS:
            total += rg2[h, slot[j], side[d]].astype(F32)
        return total

    in_pairs(grad, ((2, 2), (2, 1)))
    scatter1(0, 2, 1)
    scatter1(1, 2)
    in_pairs(grad, ((1, 2), (2, -1)))
    scatter1(1, 1)
    scatter1(0, -1)
    in_pairs(grad, ((-1, 2), (2, 0)))
    scatter1(1, -1)
    scatter1(0, 0)
    in_pairs(grad, ((0, 2), (1, 1)))
    scatter1(1, 0)
    scatter2(2)
    near_pairs = (((1, -1), (-1, 1)), ((-1, -1), (1, 0)))
    last_pairs = (((0, 1), (-1, 0)), ((0, -1), (0, 0)))
    in_pairs(soft_grad, *near_pairs, *last_pairs)

    mate_n, tx1n, tx2n = {}, {}, {}

    def text_product(dx):
        xx = (x + dx + 4) % 4
        at = pl.ds(pl.multiple_of(xx * 2 * PAIRS, 2 * PAIRS), 2 * PAIRS)
        prod = lax.dot_general(
            gb[:, at], img[...].reshape(NCOL * PAIRS, EMB), (((0,), (0,)), ((), ())),
            preferred_element_type=F32,
        )
        ptxt[at, :] = prod.astype(BF16)
        mate_n[dx] = net.send(ptxt.at[tblock(dx, 1 - c)], rc.at[xx], net.mate())

    def text_pair(dx):
        xx = (x + dx + 4) % 4
        net.recv(mate_n[dx], rc.at[xx])
        return ptxt[tblock(dx, c), :].astype(F32) + rc[xx].astype(F32)

    text_product(2)
    in_pairs(image_product, *near_pairs)
    scatter2(1)
    scatter2(-1)
    ptxt[tblock(2, c), :] = text_pair(2).astype(BF16)
    for d in DIRS:
        tx1n[d] = net.send(ptxt.at[tsub(2, c, d)], rx1.at[side[d]], net.dev(dx=d))
    text_product(1)
    text_product(-1)
    for h in (0, 1):
        rb[h, 0] = line_sum(h, 2).astype(BF16)
        for d in DIRS:
            at = pl.ds(0 if d == 1 else 32, 32)
            rf1n[h, d] = net.send(rb.at[h, 0, at], rf1.at[h, side[d]], fdev(h, d))
    in_pairs(image_product, *last_pairs)
    for d in DIRS:
        ptxt[tblock(d, c), :] = text_pair(d).astype(BF16)
        net.recv(tx1n[d], rx1.at[side[d]])
        part = ptxt.at[tsub(d, c, d)]
        part[...] = (part[...].astype(F32) + rx1[side[d]].astype(F32)).astype(BF16)
        tx2n[d] = net.send(ptxt.at[tblock(d, c)], rx2.at[side[d]], net.dev(dx=d))
    net.drain(rg2n[h, j, d] for h in (0, 1) for j in (1, -1) for d in DIRS)
    scatter2(0)
    text_product(0)
    for h in (0, 1):
        for d in DIRS:
            total = line_sum(h, d)
            net.recv(rf1n[h, d], rf1.at[h, side[d]])
            extra = rf1[h, side[d]].astype(F32)
            lo, hi = total[0:32], total[32:64]
            if d == 1:
                lo = lo + extra
            else:
                hi = hi + extra
            rb[h, 1 + side[d], 0:32] = lo.astype(BF16)
            rb[h, 1 + side[d], 32:64] = hi.astype(BF16)
            rf2n[h, d] = net.send(rb.at[h, 1 + side[d]], rf2.at[h, side[d]], fdev(h, d))

    where = (x, y, z)

    def dev(axis, d):
        return net.dev(**{("dx", "dy", "dz")[axis]: d})

    tot_n = {}

    def tot_send(axis):
        own = s4.at[axis, where[axis]]
        for d in (1, 2, 3):
            tot_n[axis, d] = net.send(own, own, dev(axis, d))

    def tot_recv(axis):
        for d in (1, 2, 3):
            net.recv(tot_n[axis, d], s4.at[axis, (where[axis] - d + 4) % 4])
        return s4[axis, 0] + s4[axis, 1] + s4[axis, 2] + s4[axis, 3]

    half_lse = (0.5 / NCOL) * jnp.sum(rowl[...].reshape(2, 8, PAIRS), axis=0) + (
        0.5 / NROW
    ) * coll[...]
    s4[0, x, 0:8] = half_lse - jnp.sum(acc[0].reshape(16, 8, PAIRS), axis=0)
    s4[0, x, 8:16] = jnp.sum(acc[1].reshape(16, 8, PAIRS), axis=0)
    tot_send(0)

    def normal_grad(grads, unit, norm, dz, halves):
        u = unit[...]
        inner = jnp.sum(u * grads, axis=1, keepdims=True)
        dz[...] = ((grads - u * inner) / norm[:, 0:1]).astype(BF16)
        number = net.send(dz.at[:, give], halves.at[mine], net.mate())
        halves[mine, :] = dz[:, keep]
        return number

    total = text_pair(0)
    for d in DIRS:
        net.recv(tx2n[d], rx2.at[side[d]])
        total += rx2[side[d]].astype(F32)
    dt_n = normal_grad(scale * total, unit_t, norm_t, dz_t, dt)
    w[DI + DT :, :] = jnp.zeros((WROWS - DI - DT, HALF), BF16)
    net.recv(turn_n, turned.at[:, other])

    orders = ((0, 1, 2), (1, 2, 0), (2, 0, 1))

    def near(axis, d):
        return (where[axis] + d + 4) % 4

    def rows_at(k, a, b=None, e=None, size=256):
        start = 1024 * k + 256 * a
        if b is not None:
            start = start + 64 * b
        if e is not None:
            start = start + 16 * e
        return pl.ds(pl.multiple_of(start, 16), size)

    def part_at(k, d, s):
        return pl.ds(pl.multiple_of(1024 * k + 256 * near(orders[k][0], d) + 128 * s, 128), 128)

    def weights(first_row, rows, right):
        @pl.loop(0, rows // 128)
        def _(i):
            at = pl.ds(pl.multiple_of(first_row + i * 128, 128), 128)
            w[at, :] = jnp.dot(turned[at, :], right[...], preferred_element_type=F32).astype(BF16)

    wide = [(k, 0, 384) for k in range(3)]
    slim = [(k, 384, 256) for k in range(3)]
    n1, n2, n3, n4 = {}, {}, {}, {}
    m1, m2, m3, m4, back = {}, {}, {}, {}, {}
    over = []

    def step(k, d):
        return dev(orders[k][0], d)

    def cut(ch, rows):
        start = pl.multiple_of(c * HALF + ch[1], 128)
        return out.at[rows, pl.ds(start, ch[2])]

    def at_mate(ch, rows):
        start = pl.multiple_of((1 - c) * HALF + ch[1], 128)
        return out.at[rows, pl.ds(start, ch[2])]

    def to_mate_w(ch, rows):
        over.append((net.send(cut(ch, rows), cut(ch, rows), net.mate()), ch, rows))

    def reduce1(ch, behind=()):
        k, lane = ch[0], pl.ds(ch[1], ch[2])
        net.drain(behind)
        for d in DIRS:
            n1[ch, d] = net.send(
                w.at[part_at(k, 2, side[d]), lane], r1.at[k, side[d], :, lane], step(k, d)
            )

    def reduce2(ch, behind=()):
        k, lane = ch[0], pl.ds(ch[1], ch[2])
        for d in DIRS:
            net.recv(n1[ch, d], r1.at[k, side[d], :, lane])
            got = part_at(k, d, side[d])
            w[got, lane] = (w[got, lane].astype(F32) + r1[k, side[d], :, lane].astype(F32)).astype(
                BF16
            )
        net.drain(behind)
        for d in DIRS:
            n2[ch, d] = net.send(
                w.at[rows_at(k, near(orders[k][0], d)), lane], r2.at[k, side[d], :, lane],
                step(k, d),
            )

    def reduce3(ch, behind=()):
        k, lane = ch[0], pl.ds(ch[1], ch[2])
        a_ax, b_ax, _ = orders[k]
        total = w[rows_at(k, where[a_ax]), lane].astype(F32)
        for d in DIRS:
            net.recv(n2[ch, d], r2.at[k, side[d], :, lane])
            total += r2[k, side[d], :, lane].astype(F32)
        q1[k, :, lane] = total.astype(BF16)
        net.drain(behind)
        for d in (2, 1, 3):
            to = pl.ds(pl.multiple_of(64 * near(b_ax, d), 64), 64)
            n3[ch, d] = net.send(q1.at[k, to, lane], r3.at[k, d - 1, :, lane], dev(b_ax, d))

    def reduce4(ch, behind=()):
        k, lane = ch[0], pl.ds(ch[1], ch[2])
        _, b_ax, c_ax = orders[k]
        total = q1[k, pl.ds(pl.multiple_of(64 * where[b_ax], 64), 64), lane].astype(F32)
        for d in (1, 3, 2):
            net.recv(n3[ch, d], r3.at[k, d - 1, :, lane])
            total += r3[k, d - 1, :, lane].astype(F32)
        q2[k, :, lane] = total.astype(BF16)
        net.drain(behind)
        for d in (2, 1, 3):
            to = pl.ds(pl.multiple_of(16 * near(c_ax, d), 16), 16)
            n4[ch, d] = net.send(q2.at[k, to, lane], r4.at[k, d - 1, :, lane], dev(c_ax, d))

    def gather1(ch, behind=()):
        k, lane = ch[0], pl.ds(ch[1], ch[2])
        a_ax, b_ax, c_ax = orders[k]
        total = q2[k, pl.ds(pl.multiple_of(16 * where[c_ax], 16), 16), lane].astype(F32)
        for d in (1, 3, 2):
            net.recv(n4[ch, d], r4.at[k, d - 1, :, lane])
            total += r4[k, d - 1, :, lane].astype(F32)
        fin[k, :, lane] = total.astype(BF16)
        own = cut(ch, rows_at(k, where[a_ax], where[b_ax], where[c_ax], 16))
        net.drain(behind)
        for d in (2, 1, 3):
            m1[ch, d] = net.send(fin.at[k, :, lane], own, dev(c_ax, d))
        back[ch] = pltpu.make_async_copy(fin.at[k, :, lane], own, local_sem.at[2 + len(back)])
        back[ch].start()

    def gather2(ch, behind=()):
        k = ch[0]
        a_ax, b_ax, c_ax = orders[k]
        back[ch].wait()
        for d in (1, 3, 2):
            rows = rows_at(k, where[a_ax], where[b_ax], near(c_ax, -d), 16)
            net.recv(m1[ch, d], cut(ch, rows))
        own = cut(ch, rows_at(k, where[a_ax], where[b_ax], None, 64))
        net.drain(behind)
        for d in (2, 1, 3):
            m2[ch, d] = net.send(own, own, dev(b_ax, d))

    def gather3(ch, behind=()):
        k = ch[0]
        a_ax, b_ax, _ = orders[k]
        for d in (1, 3, 2):
            net.recv(m2[ch, d], cut(ch, rows_at(k, where[a_ax], near(b_ax, -d), None, 64)))
        rows = rows_at(k, where[a_ax])
        net.drain(behind)
        for d in DIRS:
            m3[ch, d] = net.send(cut(ch, rows), cut(ch, rows), step(k, d))
        to_mate_w(ch, rows)

    def gather4(ch, behind=()):
        k = ch[0]
        for d in DIRS:
            net.recv(m3[ch, d], cut(ch, rows_at(k, near(orders[k][0], -d))))
        net.drain(behind)
        for d in DIRS:
            rows = cut(ch, part_at(k, -d, side[d]))
            m4[ch, d] = net.send(rows, rows, step(k, d))
        for d in DIRS:
            to_mate_w(ch, rows_at(k, near(orders[k][0], -d)))

    def gather5(ch):
        for d in DIRS:
            rows = part_at(ch[0], 2, side[d])
            net.recv(m4[ch, d], cut(ch, rows))
            to_mate_w(ch, rows)

    def both(work, sent, ways):
        for ch in wide:
            work(ch)
        for ch, first in zip(slim, wide):
            work(ch, [sent[first, d] for d in ways])

    net.recv(dt_n, dt.at[other])
    weights(0, DT, dt)

    halves = []
    for h in (0, 1):
        total = line_sum(h, 0)
        for d in DIRS:
            net.recv(rf2n[h, d], rf2.at[h, side[d]])
            total += rf2[h, side[d]].astype(F32)
        halves.append(scale * total)
    di_n = normal_grad(jnp.concatenate(halves, axis=0), unit_i, norm_i, dz_i, di)
    net.recv(di_n, di.at[other])
    weights(DT, DI, di)
    both(reduce1, n1, DIRS)

    def pooled_grad(dz, proj, result, rows):
        @pl.loop(0, rows // 128)
        def _(i):
            at = pl.ds(pl.multiple_of(i * 128, 128), 128)
            result[:, at] = lax.dot_general(
                dz[...], proj[at, :], (((1,), (1,)), ((), ())), preferred_element_type=F32
            ).astype(BF16)

    both(reduce2, n2, DIRS)
    s4[1, y] = tot_recv(0)
    tot_send(1)
    pooled_grad(dz_i, wi, dpi, DI)
    pooled_grad(dz_t, wt, dpt, DT)
    hops = (1, 2, 3)
    both(reduce3, n3, hops)
    s4[2, z] = tot_recv(1)
    tot_send(2)
    both(reduce4, n4, hops)
    s2[c] = tot_recv(2)
    tot_mate = net.send(s2.at[c], s2.at[c], net.mate())
    both(gather1, m1, hops)
    both(gather2, m2, hops)
    both(gather3, m3, DIRS)
    both(gather4, m4, DIRS)
    for ch in wide + slim:
        gather5(ch)
    net.recv(tot_mate, s2.at[1 - c])
    totals = s2[0] + s2[1]
    loss_ref[0] = jnp.sum(totals[0:8]) * (1.0 / (PAIRS * NROW * NCOL))
    dscale_ref[0] = jnp.sum(totals[8:16])
    for number, ch, rows in over:
        net.recv(number, at_mate(ch, rows))
    net.finish()


def local(image_pooled, text_pooled, image_proj, text_proj, log_scale, pair_index):
    cols = NROW * PAIRS
    vmem = pltpu.VMEM
    held = pl.BlockSpec(memory_space=pltpu.VMEM)
    scalar = pl.BlockSpec(memory_space=pltpu.SMEM)
    far = pl.BlockSpec(memory_space=pl.ANY)
    weights, dpi, dpt, loss, dscale = pl.pallas_call(
        kernel,
        name="contrastive_loss",
        out_shape=(
            jax.ShapeDtypeStruct((WROWS, EMB), BF16),
            jax.ShapeDtypeStruct((PAIRS, DI), BF16),
            jax.ShapeDtypeStruct((PAIRS, DT), BF16),
            jax.ShapeDtypeStruct((1,), F32),
            jax.ShapeDtypeStruct((1,), F32),
        ),
        in_specs=[scalar, held, held, far, far, held],
        out_specs=(far, held, held, scalar, scalar),
        scratch_shapes=[
            vmem((NCOL, PAIRS, EMB), BF16),
            vmem((cols, EMB), BF16),
            vmem((NCOL, 8, PAIRS), F32),
            vmem((NCOL, PAIRS, cols), F32),
            vmem((NCOL * PAIRS, cols), BF16),
            vmem((NCOL, PAIRS, EMB), BF16),
            vmem((cols, EMB), BF16),
            vmem((2, 4, 2, 32, EMB), BF16),
            vmem((2, 4, 2, 64, EMB), BF16),
            vmem((2, 3, 64, EMB), BF16),
            vmem((2, 2, 32, EMB), BF16),
            vmem((2, 2, 64, EMB), BF16),
            vmem((4, PAIRS, EMB), BF16),
            vmem((2, 64, EMB), BF16),
            vmem((2, PAIRS, EMB), BF16),
            vmem((8, cols), F32),
            vmem((8, cols), F32),
            vmem((NCOL, PAIRS), F32),
            vmem((4, NCOL, PAIRS), F32),
            vmem((4, NCOL, PAIRS), F32),
            vmem((NROW, PAIRS), F32),
            vmem((4, NROW, PAIRS), F32),
            vmem((2, NROW, PAIRS), F32),
            vmem((2, PAIRS, PAIRS), F32),
            vmem((DI, EMB), BF16),
            vmem((DT, EMB), BF16),
            vmem((PAIRS, EMB), F32),
            vmem((PAIRS, EMB), F32),
            vmem((PAIRS, 128), F32),
            vmem((PAIRS, 128), F32),
            vmem((DI + DT, 2 * PAIRS), BF16),
            vmem((PAIRS, EMB), BF16),
            vmem((PAIRS, EMB), BF16),
            vmem((2 * PAIRS, HALF), BF16),
            vmem((2 * PAIRS, HALF), BF16),
            vmem((WROWS, HALF), BF16),
            vmem((3, 2, 128, HALF), BF16),
            vmem((3, 2, 256, HALF), BF16),
            vmem((3, 256, HALF), BF16),
            vmem((3, 3, 64, HALF), BF16),
            vmem((3, 64, HALF), BF16),
            vmem((3, 3, 16, HALF), BF16),
            vmem((3, 16, HALF), BF16),
            vmem((3, 4, 16, 128), F32),
            vmem((2, 16, 128), F32),
            pltpu.SemaphoreType.DMA((288,)),
            pltpu.SemaphoreType.DMA((288,)),
            pltpu.SemaphoreType.DMA((8,)),
        ],
        compiler_params=pltpu.CompilerParams(
            collective_id=0, has_side_effects=True, vmem_limit_bytes=60 * 1024 * 1024
        ),
        cost_estimate=pl.CostEstimate(
            flops=19 * 10**9, bytes_accessed=24 * 10**6, transcendentals=8 * 10**6
        ),
    )(
        log_scale, image_pooled, text_pooled, image_proj, text_proj,
        pair_index.reshape(1, PAIRS),
    )
    dwt = weights[:DT].astype(F32)
    dwi = weights[DT : DT + DI].astype(F32)
    return (loss, dpi, dpt, dwi, dwt, dscale)


def solution(mesh):
    return jax.shard_map(
        local,
        mesh=mesh,
        in_specs=(
            P(("row", "col"), None),
            P(("col", "row"), None),
            P(),
            P(),
            P(),
            P(("row", "col")),
        ),
        out_specs=(P(), P(("row", "col"), None), P(("col", "row"), None), P(), P(), P()),
        check_vma=False,
    )
```

```python
import functools

import jax
import jax.numpy as jnp
from jax import lax
from jax.experimental import pallas as pl
from jax.experimental.pallas import tpu as pltpu
from jax.sharding import PartitionSpec as P

EPS = 1e-06
MESH = pl.DeviceIdType.MESH
F32 = jnp.float32
BF16 = jnp.bfloat16
PAIRS = 128
NCOL = 16
NROW = 8
EMB = 1280
DI = 1664
DT = 1280
HALF = EMB // 2
DIRS = (1, -1)
STEPS = (2, 1, -1, 0)
WROWS = DI + DT + 128
LANES = ((0, 256), (256, 256), (512, 128))
HOLD = False
CAST = 128


class Net:
    def __init__(self, send_sem, recv_sem):
        self.send_sem, self.recv_sem = send_sem, recv_sem
        row, col = lax.axis_index("row"), lax.axis_index("col")
        self.x, self.c = row // 2, row % 2
        self.y, self.z = col // 4, col % 4
        self.count = 0
        self.started = {}

    def dev(self, dx=0, dy=0, dz=0):
        return (
            2 * ((self.x + dx + 4) % 4) + self.c,
            4 * ((self.y + dy + 4) % 4) + (self.z + dz + 4) % 4,
        )

    def mate(self):
        return (2 * self.x + 1 - self.c, 4 * self.y + self.z)

    def greet(self):
        others = [self.mate()]
        for d in (1, 2, 3):
            others += [self.dev(dx=d), self.dev(dy=d), self.dev(dz=d)]
        self.others = len(others)
        for other in others:
            pl.semaphore_signal(
                pltpu.get_barrier_semaphore(), inc=1, device_id=other, device_id_type=MESH
            )

    def met(self):
        pl.semaphore_wait(pltpu.get_barrier_semaphore(), self.others)

    def copy(self, number, src, dst, device):
        return pltpu.make_async_remote_copy(
            src_ref=src,
            dst_ref=dst,
            send_sem=self.send_sem.at[number],
            recv_sem=self.recv_sem.at[number],
            device_id=device,
            device_id_type=MESH,
        )

    def send(self, src, dst, device):
        number = self.count
        self.count += 1
        copy = self.copy(number, src, dst, device)
        copy.start()
        self.started[number] = copy
        return number

    def recv(self, number, dst):
        self.copy(number, dst, dst, self.mate()).wait_recv()

    def drain(self, numbers):
        for number in numbers:
            self.started.pop(number).wait_send()

    def finish(self):
        for copy in self.started.values():
            copy.wait_send()


def lanes(column):
    return jnp.transpose(jnp.broadcast_to(column, (PAIRS, PAIRS)))[0:1, :]


def sublanes(row):
    return jnp.transpose(jnp.broadcast_to(row, (PAIRS, PAIRS)))


def lse_over(parts):
    peak = functools.reduce(jnp.maximum, parts)
    return peak + jnp.log(sum(jnp.exp(p - peak) for p in parts))


def pick(i, options):
    value = options[0]
    for n in range(1, len(options)):
        value = jnp.where(i == n, options[n], value)
    return value


def kernel(
    scale_ref, pi, pt, wi_hbm, wt_hbm, pair, out, dpi, dpt, loss_ref, dscale_ref,
    img, txt, pid, scores, gb, pimg, ptxt,
    rg1, rg2, rb, rf1, rf2, rc, rx1, rx2,
    cmax, csum, rowl, rowz, rowy, coll, colx, colc, acc,
    wi, wt, unit_i, unit_t, norm_i, norm_t, turned, dz_i, dz_t, di, dt,
    w, r1, r2, q1, r3, q2, r4, fin, s4, s2,
    send_sem, recv_sem, local_sem,
):
    net = Net(send_sem, recv_sem)
    x, c, y, z = net.x, net.c, net.y, net.z
    me_col = 4 * y + z
    scale = jnp.exp(jnp.full((8, 128), scale_ref[0], F32))[0:1, 0:1]
    load_i = pltpu.make_async_copy(wi_hbm, wi, local_sem.at[0])
    load_t = pltpu.make_async_copy(wt_hbm, wt, local_sem.at[1])
    load_i.start()
    load_t.start()
    net.greet()

    def axes(h):
        return ((y, z), (z, y))[h]

    def gdev(h, d):
        return net.dev(dy=d) if h == 0 else net.dev(dz=d)

    def fdev(h, d):
        return net.dev(dz=d) if h == 0 else net.dev(dy=d)

    def block(h, dg, df):
        g, f = axes(h)
        g, f = (g + dg + 4) % 4, (f + df + 4) % 4
        return 4 * g + f if h == 0 else 4 * f + g

    def half(ref, q, h):
        return ref.at[q, pl.ds(64 * h, 64)]

    def sub(ref, q, h, d):
        return ref.at[q, pl.ds(64 * h + (0 if d == 1 else 32), 32)]

    def rel(dy, dz):
        return 4 * ((y + dy + 4) % 4) + (z + dz + 4) % 4

    def tblock(dx, core):
        return pl.ds(pl.multiple_of((2 * ((x + dx + 4) % 4) + core) * PAIRS, PAIRS), PAIRS)

    def tsub(dx, core, d):
        start = (2 * ((x + dx + 4) % 4) + core) * PAIRS + (0 if d == 1 else 64)
        return pl.ds(pl.multiple_of(start, 64), 64)

    mine = pl.ds(pl.multiple_of(c * PAIRS, PAIRS), PAIRS)
    other = pl.ds(pl.multiple_of((1 - c) * PAIRS, PAIRS), PAIRS)
    keep = pl.ds(pl.multiple_of(c * HALF, 128), HALF)
    give = pl.ds(pl.multiple_of((1 - c) * HALF, 128), HALF)

    def embed(pooled, proj, unit, norm):
        value = jnp.dot(pooled[...], proj[...], preferred_element_type=F32)
        norms = jnp.sqrt(jnp.sum(value * value, axis=1, keepdims=True) + EPS)
        value = value / norms
        unit[...] = value
        norm[...] = jnp.broadcast_to(norms, norm.shape)
        return value.astype(BF16)

    pid[me_col] = jnp.broadcast_to(pair[...].astype(F32), (8, PAIRS))
    load_i.wait()
    img[me_col] = embed(pi, wi, unit_i, norm_i)
    net.met()

    f1, g1, f2, g3, g4 = {}, {}, {}, {}, {}
    x1, x2, cx = {}, {}, {}
    pz, py = {}, {}
    for h in (0, 1):
        for d in DIRS:
            part = half(img, me_col, h)
            f1[h, d] = net.send(part, part, fdev(h, d))
    load_t.wait()
    txt[tblock(0, c), :] = embed(pt, wt, unit_t, norm_t)
    for d in DIRS:
        part = txt.at[tblock(0, c)]
        x1[d] = net.send(part, part, net.dev(dx=d))
    net.drain(f1.values())
    for h in (0, 1):
        for d in DIRS:
            part = half(img, me_col, h)
            g1[h, d] = net.send(part, part, gdev(h, d))

    def to_mate(dx):
        part = txt.at[tblock(dx, c)]
        cx[dx] = net.send(part, part, net.mate())

    to_mate(0)
    for d in (1, 2, 3):
        pz[d] = net.send(pid.at[me_col], pid.at[me_col], net.dev(dz=d))
    turned[0:DT, mine] = jnp.transpose(pt[...])
    turned[DT:, mine] = jnp.transpose(pi[...])
    turn_n = net.send(turned.at[:, mine], turned.at[:, mine], net.mate())
    cmax[...] = jnp.full_like(cmax, -1e30)
    csum[...] = jnp.zeros_like(csum)
    acc[...] = jnp.zeros_like(acc)

    for h in (0, 1):
        for d in DIRS:
            q = block(h, 0, -d)
            net.recv(f1[h, d], half(img, q, h))
            f2[h, d] = net.send(sub(img, q, h, d), sub(img, q, h, d), fdev(h, d))
            for e in DIRS:
                g3[h, -d, e] = net.send(half(img, q, h), half(img, q, h), gdev(h, e))

    def pass_on(h, j, d):
        q = block(h, -d, j)
        net.recv(g1[h, d] if j == 0 else g3[h, j, d], half(img, q, h))
        g4[h, j, d] = net.send(sub(img, q, h, d), sub(img, q, h, d), gdev(h, d))

    for h in (0, 1):
        for d in DIRS:
            pass_on(h, 0, d)
    for d in DIRS:
        net.recv(x1[d], txt.at[tblock(-d, c)])
        part = txt.at[tsub(-d, c, d)]
        x2[d] = net.send(part, part, net.dev(dx=d))
        to_mate(-d)
    for h in (0, 1):
        q = block(h, 0, 2)
        for d in DIRS:
            net.recv(f2[h, d], sub(img, q, h, d))
        for d in DIRS:
            g3[h, 2, d] = net.send(half(img, q, h), half(img, q, h), gdev(h, d))
    for d in (1, 2, 3):
        net.recv(pz[d], pid.at[rel(0, -d)])
    for d in (1, 2, 3):
        line = pid.at[pl.ds(4 * y, 4)]
        py[d] = net.send(line, line, net.dev(dy=d))
    for d in DIRS:
        net.recv(x2[d], txt.at[tsub(2, c, d)])
    to_mate(2)
    for dx in (0, 1, -1, 2):
        net.recv(cx[dx], txt.at[tblock(dx, 1 - c)])

    def score(qa, qb):
        left = jnp.concatenate([img[qa], img[qb]], axis=0)
        s2q = scale * lax.dot_general(
            left, txt[...], (((1,), (1,)), ((), ())), preferred_element_type=F32
        )
        for q, s in ((qa, s2q[:PAIRS]), (qb, s2q[PAIRS:])):
            scores[q] = s
            peak = jnp.max(s, axis=1, keepdims=True)
            total = jnp.sum(jnp.exp(s - peak), axis=1, keepdims=True)
            rowl[pl.ds(q, 1), :] = lanes(peak + jnp.log(total))
        s3 = s2q.reshape(2 * PAIRS // 8, 8, s2q.shape[1])
        old = cmax[...]
        new = jnp.maximum(old, jnp.max(s3, axis=0))
        csum[...] = csum[...] * jnp.exp(old - new) + jnp.sum(jnp.exp(s3 - new[None]), axis=0)
        cmax[...] = new

    def in_pairs(work, *pairs):
        if len(pairs) == 1:
            (a, b), (e, f) = pairs[0]
            work(rel(a, b), rel(e, f))
            return

        @pl.loop(0, len(pairs))
        def _(i):
            a, b, e, f = (pick(i, [p[m][n] for p in pairs]) for m in (0, 1) for n in (0, 1))
            work(rel(a, b), rel(e, f))

    def last_hop(j):
        for h in (0, 1):
            for d in DIRS:
                net.recv(g4[h, j, d], sub(img, block(h, 2, j), h, d))

    in_pairs(score, ((0, 0), (0, 1)))
    for h in (0, 1):
        for j in (1, -1):
            for d in DIRS:
                pass_on(h, j, d)
    in_pairs(score, ((0, -1), (1, 0)), ((-1, 0), (1, 1)))
    for h in (0, 1):
        for d in DIRS:
            pass_on(h, 2, d)
    last_hop(0)
    in_pairs(score, ((1, -1), (-1, 1)), ((-1, -1), (2, 0)))
    last_hop(1)
    last_hop(-1)
    in_pairs(score, ((0, 2), (2, 1)), ((1, 2), (2, -1)))
    last_hop(2)
    in_pairs(score, ((-1, 2), (2, 2)))

    rz, ry, lx = {}, {}, {}
    rowz[z] = rowl[...]
    for d in (1, 2, 3):
        rz[d] = net.send(rowz.at[z], rowz.at[z], net.dev(dz=d))
    peak = jnp.max(cmax[...], axis=0, keepdims=True)
    lcol = peak + jnp.log(jnp.sum(csum[...] * jnp.exp(cmax[...] - peak), axis=0, keepdims=True))
    for r in range(NROW):
        coll[r : r + 1, :] = lcol[:, r * PAIRS : (r + 1) * PAIRS]
    colx[x] = coll[...]
    for d in (1, 2, 3):
        lx[d] = net.send(colx.at[x], colx.at[x], net.dev(dx=d))
    for d in (1, 2, 3):
        net.recv(rz[d], rowz.at[(z - d + 4) % 4])
    rowy[y] = lse_over([rowz[i] for i in range(4)])
    for d in (1, 2, 3):
        ry[d] = net.send(rowy.at[y], rowy.at[y], net.dev(dy=d))
    for d in (1, 2, 3):
        net.recv(lx[d], colx.at[(x - d + 4) % 4])
    colc[c] = lse_over([colx[i] for i in range(4)])
    lc = net.send(colc.at[c], colc.at[c], net.mate())
    for d in (1, 2, 3):
        line = pid.at[pl.ds(4 * ((y - d + 4) % 4), 4)]
        net.recv(py[d], line)
    for d in (1, 2, 3):
        net.recv(ry[d], rowy.at[(y - d + 4) % 4])
    rowl[...] = lse_over([rowy[i] for i in range(4)])
    net.recv(lc, colc.at[1 - c])
    coll[...] = lse_over([colc[i] for i in range(2)])

    first = (me_col * NROW * PAIRS).astype(F32)
    place = lax.broadcasted_iota(jnp.int32, (PAIRS, PAIRS), 1).astype(F32) + first

    def soft_grad(*pair_of):
        for q in pair_of:
            lrow = sublanes(rowl[pl.ds(q, 1), :])
            target = sublanes(pid[q][0:1, :]) - place
            hit_sum = jnp.zeros((PAIRS, PAIRS), F32)
            dot_sum = jnp.zeros((PAIRS, PAIRS), F32)
            here = pl.ds(pl.multiple_of(q * PAIRS, PAIRS), PAIRS)
            for r in range(NROW):
                at = slice(r * PAIRS, (r + 1) * PAIRS)
                s = scores[q, :, at]
                soft = 0.5 * (jnp.exp(s - lrow) + jnp.exp(s - coll[r : r + 1, :]))
                hit = (target == float(r * PAIRS)).astype(F32)
                g = soft - hit
                hit_sum += s * hit
                dot_sum += s * g
                gb[here, at] = g.astype(BF16)
            acc[0] += hit_sum
            acc[1] += dot_sum

    def image_product(qa, qb):
        rows = [gb[pl.ds(pl.multiple_of(q * PAIRS, PAIRS), PAIRS), :] for q in (qa, qb)]
        prod = jnp.dot(jnp.concatenate(rows, axis=0), txt[...], preferred_element_type=F32)
        pimg[qa] = prod[:PAIRS].astype(BF16)
        pimg[qb] = prod[PAIRS:].astype(BF16)

    def grad(qa, qb):
        soft_grad(qa, qb)
        image_product(qa, qb)

    rg1n, rg2n, rf1n, rf2n = {}, {}, {}, {}
    slot = {2: 0, 1: 1, -1: 2, 0: 3}
    side = {1: 0, -1: 1}

    def scatter1(h, *js):
        for j in js:
            for d in DIRS:
                q = block(h, 2, j)
                rg1n[h, j, d] = net.send(
                    sub(pimg, q, h, d), rg1.at[h, slot[j], side[d]], gdev(h, d)
                )

    def scatter2(j):
        for h in (0, 1):
            for d in DIRS:
                q = block(h, d, j)
                got = rg1.at[h, slot[j], side[d]]
                net.recv(rg1n[h, j, d], got)
                part = sub(pimg, q, h, d)
                part[...] = (part[...].astype(F32) + got[...].astype(F32)).astype(BF16)
                rg2n[h, j, d] = net.send(
                    half(pimg, q, h), rg2.at[h, slot[j], side[d]], gdev(h, d)
                )

    def line_sum(h, j):
        for d in DIRS:
            net.recv(rg2n[h, j, d], rg2.at[h, slot[j], side[d]])
        total = half(pimg, block(h, 0, j), h)[...].astype(F32)
        for d in DIRS:
            total += rg2[h, slot[j], side[d]].astype(F32)
        return total

    in_pairs(grad, ((2, 2), (2, 1)))
    scatter1(0, 2, 1)
    scatter1(1, 2)
    in_pairs(grad, ((1, 2), (2, -1)))
    scatter1(1, 1)
    scatter1(0, -1)
    in_pairs(grad, ((-1, 2), (2, 0)))
    scatter1(1, -1)
    scatter1(0, 0)
    in_pairs(grad, ((0, 2), (1, 1)))
    scatter1(1, 0)
    scatter2(2)
    near_pairs = (((1, -1), (-1, 1)), ((-1, -1), (1, 0)))
    last_pairs = (((0, 1), (-1, 0)), ((0, -1), (0, 0)))
    in_pairs(soft_grad, *near_pairs, *last_pairs)

    mate_n, tx1n, tx2n = {}, {}, {}

    def text_product(dx):
        xx = (x + dx + 4) % 4
        at = pl.ds(pl.multiple_of(xx * 2 * PAIRS, 2 * PAIRS), 2 * PAIRS)
        prod = lax.dot_general(
            gb[:, at], img[...].reshape(NCOL * PAIRS, EMB), (((0,), (0,)), ((), ())),
            preferred_element_type=F32,
        )
        ptxt[at, :] = prod.astype(BF16)
        mate_n[dx] = net.send(ptxt.at[tblock(dx, 1 - c)], rc.at[xx], net.mate())

    def text_pair(dx):
        xx = (x + dx + 4) % 4
        net.recv(mate_n[dx], rc.at[xx])
        return ptxt[tblock(dx, c), :].astype(F32) + rc[xx].astype(F32)

    text_product(2)
    in_pairs(image_product, *near_pairs)
    scatter2(1)
    scatter2(-1)
    ptxt[tblock(2, c), :] = text_pair(2).astype(BF16)
    for d in DIRS:
        tx1n[d] = net.send(ptxt.at[tsub(2, c, d)], rx1.at[side[d]], net.dev(dx=d))
    text_product(1)
    text_product(-1)
    for h in (0, 1):
        rb[h, 0] = line_sum(h, 2).astype(BF16)
        for d in DIRS:
            at = pl.ds(0 if d == 1 else 32, 32)
            rf1n[h, d] = net.send(rb.at[h, 0, at], rf1.at[h, side[d]], fdev(h, d))
    in_pairs(image_product, *last_pairs)
    for d in DIRS:
        ptxt[tblock(d, c), :] = text_pair(d).astype(BF16)
        net.recv(tx1n[d], rx1.at[side[d]])
        part = ptxt.at[tsub(d, c, d)]
        part[...] = (part[...].astype(F32) + rx1[side[d]].astype(F32)).astype(BF16)
        tx2n[d] = net.send(ptxt.at[tblock(d, c)], rx2.at[side[d]], net.dev(dx=d))
    net.drain(rg2n[h, j, d] for h in (0, 1) for j in (1, -1) for d in DIRS)
    scatter2(0)
    text_product(0)
    for h in (0, 1):
        for d in DIRS:
            total = line_sum(h, d)
            net.recv(rf1n[h, d], rf1.at[h, side[d]])
            extra = rf1[h, side[d]].astype(F32)
            lo, hi = total[0:32], total[32:64]
            if d == 1:
                lo = lo + extra
            else:
                hi = hi + extra
            rb[h, 1 + side[d], 0:32] = lo.astype(BF16)
            rb[h, 1 + side[d], 32:64] = hi.astype(BF16)
            rf2n[h, d] = net.send(rb.at[h, 1 + side[d]], rf2.at[h, side[d]], fdev(h, d))

    where = (x, y, z)

    def dev(axis, d):
        return net.dev(**{("dx", "dy", "dz")[axis]: d})

    tot_n = {}

    def tot_send(axis):
        own = s4.at[axis, where[axis]]
        for d in (1, 2, 3):
            tot_n[axis, d] = net.send(own, own, dev(axis, d))

    def tot_recv(axis):
        for d in (1, 2, 3):
            net.recv(tot_n[axis, d], s4.at[axis, (where[axis] - d + 4) % 4])
        return s4[axis, 0] + s4[axis, 1] + s4[axis, 2] + s4[axis, 3]

    half_lse = (0.5 / NCOL) * jnp.sum(rowl[...].reshape(2, 8, PAIRS), axis=0) + (
        0.5 / NROW
    ) * coll[...]
    s4[0, x, 0:8] = half_lse - jnp.sum(acc[0].reshape(16, 8, PAIRS), axis=0)
    s4[0, x, 8:16] = jnp.sum(acc[1].reshape(16, 8, PAIRS), axis=0)
    tot_send(0)

    def normal_grad(grads, unit, norm, dz, halves):
        u = unit[...]
        inner = jnp.sum(u * grads, axis=1, keepdims=True)
        dz[...] = ((grads - u * inner) / norm[:, 0:1]).astype(BF16)
        number = net.send(dz.at[:, give], halves.at[mine], net.mate())
        halves[mine, :] = dz[:, keep]
        return number

    total = text_pair(0)
    for d in DIRS:
        net.recv(tx2n[d], rx2.at[side[d]])
        total += rx2[side[d]].astype(F32)
    dt_n = normal_grad(scale * total, unit_t, norm_t, dz_t, dt)
    w[DI + DT :, :] = jnp.zeros((WROWS - DI - DT, HALF), BF16)
    net.recv(turn_n, turned.at[:, other])

    orders = ((0, 1, 2), (1, 2, 0), (2, 0, 1))

    def near(axis, d):
        return (where[axis] + d + 4) % 4

    def rows_at(k, a, b=None, e=None, size=256):
        start = 1024 * k + 256 * a
        if b is not None:
            start = start + 64 * b
        if e is not None:
            start = start + 16 * e
        return pl.ds(pl.multiple_of(start, 16), size)

    def part_at(k, d, s):
        return pl.ds(pl.multiple_of(1024 * k + 256 * near(orders[k][0], d) + 128 * s, 128), 128)

    def weights(first_row, rows, right):
        tall = rows // 4

        @pl.loop(0, 4)
        def _(i):
            at = pl.ds(pl.multiple_of(first_row + i * tall, 16), tall)
            w[at, :] = jnp.dot(turned[at, :], right[...], preferred_element_type=F32).astype(BF16)

    def pooled_grad(dz, proj, result, rows):
        @pl.loop(0, rows // 128)
        def _(i):
            at = pl.ds(pl.multiple_of(i * 128, 128), 128)
            result[:, at] = lax.dot_general(
                dz[...], proj[at, :], (((1,), (1,)), ((), ())), preferred_element_type=F32
            ).astype(BF16)

    groups = [[(k, first, size) for k in range(3)] for first, size in LANES]
    n1, n2, n3, n4 = {}, {}, {}, {}
    m1, m2, m3, m4, back = {}, {}, {}, {}, {}
    over = []

    def step(k, d):
        return dev(orders[k][0], d)

    def cut(ch, rows):
        start = pl.multiple_of(c * HALF + ch[1], 128)
        return out.at[rows, pl.ds(start, ch[2])]

    def at_mate(ch, rows):
        start = pl.multiple_of((1 - c) * HALF + ch[1], 128)
        return out.at[rows, pl.ds(start, ch[2])]

    def to_mate_w(ch, rows):
        over.append((net.send(cut(ch, rows), cut(ch, rows), net.mate()), ch, rows))

    def reduce1(ch, behind=()):
        k, lane = ch[0], pl.ds(ch[1], ch[2])
        net.drain(behind)
        for d in DIRS:
            n1[ch, d] = net.send(
                w.at[part_at(k, 2, side[d]), lane], r1.at[k, side[d], :, lane], step(k, d)
            )

    def reduce2(ch, behind=()):
        k, lane = ch[0], pl.ds(ch[1], ch[2])
        for d in DIRS:
            net.recv(n1[ch, d], r1.at[k, side[d], :, lane])
            got = part_at(k, d, side[d])
            w[got, lane] = (w[got, lane].astype(F32) + r1[k, side[d], :, lane].astype(F32)).astype(
                BF16
            )
        net.drain(behind)
        for d in DIRS:
            n2[ch, d] = net.send(
                w.at[rows_at(k, near(orders[k][0], d)), lane], r2.at[k, side[d], :, lane],
                step(k, d),
            )

    def reduce3(ch, behind=()):
        k, lane = ch[0], pl.ds(ch[1], ch[2])
        a_ax, b_ax, _ = orders[k]
        total = w[rows_at(k, where[a_ax]), lane].astype(F32)
        for d in DIRS:
            net.recv(n2[ch, d], r2.at[k, side[d], :, lane])
            total += r2[k, side[d], :, lane].astype(F32)
        q1[k, :, lane] = total.astype(BF16)
        net.drain(behind)
        for d in (2, 1, 3):
            to = pl.ds(pl.multiple_of(64 * near(b_ax, d), 64), 64)
            n3[ch, d] = net.send(q1.at[k, to, lane], r3.at[k, d - 1, :, lane], dev(b_ax, d))

    def reduce4(ch, behind=()):
        k, lane = ch[0], pl.ds(ch[1], ch[2])
        _, b_ax, c_ax = orders[k]
        total = q1[k, pl.ds(pl.multiple_of(64 * where[b_ax], 64), 64), lane].astype(F32)
        for d in (1, 3, 2):
            net.recv(n3[ch, d], r3.at[k, d - 1, :, lane])
            total += r3[k, d - 1, :, lane].astype(F32)
        q2[k, :, lane] = total.astype(BF16)
        net.drain(behind)
        for d in (2, 1, 3):
            to = pl.ds(pl.multiple_of(16 * near(c_ax, d), 16), 16)
            n4[ch, d] = net.send(q2.at[k, to, lane], r4.at[k, d - 1, :, lane], dev(c_ax, d))

    def gather1(ch, behind=()):
        k, lane = ch[0], pl.ds(ch[1], ch[2])
        a_ax, b_ax, c_ax = orders[k]
        total = q2[k, pl.ds(pl.multiple_of(16 * where[c_ax], 16), 16), lane].astype(F32)
        for d in (1, 3, 2):
            net.recv(n4[ch, d], r4.at[k, d - 1, :, lane])
            total += r4[k, d - 1, :, lane].astype(F32)
        fin[k, :, lane] = total.astype(BF16)
        own = cut(ch, rows_at(k, where[a_ax], where[b_ax], where[c_ax], 16))
        net.drain(behind)
        for d in (2, 1, 3):
            m1[ch, d] = net.send(fin.at[k, :, lane], own, dev(c_ax, d))
        back[ch] = pltpu.make_async_copy(fin.at[k, :, lane], own, local_sem.at[2 + len(back)])
        back[ch].start()

    def gather2(ch, behind=()):
        k = ch[0]
        a_ax, b_ax, c_ax = orders[k]
        back[ch].wait()
        for d in (1, 3, 2):
            rows = rows_at(k, where[a_ax], where[b_ax], near(c_ax, -d), 16)
            net.recv(m1[ch, d], cut(ch, rows))
        own = cut(ch, rows_at(k, where[a_ax], where[b_ax], None, 64))
        net.drain(behind)
        for d in (2, 1, 3):
            m2[ch, d] = net.send(own, own, dev(b_ax, d))

    def gather3(ch, behind=()):
        k = ch[0]
        a_ax, b_ax, _ = orders[k]
        for d in (1, 3, 2):
            net.recv(m2[ch, d], cut(ch, rows_at(k, where[a_ax], near(b_ax, -d), None, 64)))
        rows = rows_at(k, where[a_ax])
        net.drain(behind)
        for d in DIRS:
            m3[ch, d] = net.send(cut(ch, rows), cut(ch, rows), step(k, d))
        to_mate_w(ch, rows)

    def gather4(ch, behind=()):
        k = ch[0]
        for d in DIRS:
            net.recv(m3[ch, d], cut(ch, rows_at(k, near(orders[k][0], -d))))
        net.drain(behind)
        for d in DIRS:
            rows = cut(ch, part_at(k, -d, side[d]))
            m4[ch, d] = net.send(rows, rows, step(k, d))
        for d in DIRS:
            to_mate_w(ch, rows_at(k, near(orders[k][0], -d)))

    def gather5(ch):
        for d in DIRS:
            rows = part_at(ch[0], 2, side[d])
            net.recv(m4[ch, d], cut(ch, rows))
            to_mate_w(ch, rows)

    def both(work, sent, ways):
        for n, group in enumerate(groups):
            for k, ch in enumerate(group):
                hold = HOLD and n > 0
                work(ch, [sent[groups[n - 1][k], d] for d in ways] if hold else ())

    net.recv(dt_n, dt.at[other])
    weights(0, DT, dt)
    pooled_grad(dz_t, wt, dpt, DT)

    halves = []
    for h in (0, 1):
        total = line_sum(h, 0)
        for d in DIRS:
            net.recv(rf2n[h, d], rf2.at[h, side[d]])
            total += rf2[h, side[d]].astype(F32)
        halves.append(scale * total)
    di_n = normal_grad(jnp.concatenate(halves, axis=0), unit_i, norm_i, dz_i, di)
    net.recv(di_n, di.at[other])
    weights(DT, DI, di)
    both(reduce1, n1, DIRS)
    pooled_grad(dz_i, wi, dpi, DI)

    both(reduce2, n2, DIRS)
    s4[1, y] = tot_recv(0)
    tot_send(1)
    hops = (1, 2, 3)
    both(reduce3, n3, hops)
    s4[2, z] = tot_recv(1)
    tot_send(2)
    both(reduce4, n4, hops)
    s2[c] = tot_recv(2)
    tot_mate = net.send(s2.at[c], s2.at[c], net.mate())
    both(gather1, m1, hops)
    both(gather2, m2, hops)
    both(gather3, m3, DIRS)
    both(gather4, m4, DIRS)
    for group in groups:
        for ch in group:
            gather5(ch)
    net.recv(tot_mate, s2.at[1 - c])
    totals = s2[0] + s2[1]
    loss_ref[0] = jnp.sum(totals[0:8]) * (1.0 / (PAIRS * NROW * NCOL))
    dscale_ref[0] = jnp.sum(totals[8:16])
    for number, ch, rows in over:
        net.recv(number, at_mate(ch, rows))
    net.finish()


def cast_kernel(w, dpi, dpt, wt_out, wi_out, dpi_out, dpt_out, narrow, wide, got, put, passed):
    hand_on = [
        pltpu.make_async_copy(dpi, dpi_out, passed.at[0]),
        pltpu.make_async_copy(dpt, dpt_out, passed.at[1]),
    ]
    blocks = (DT + DI) // CAST
    reads, writes = [], []
    for i in range(blocks):
        reads.append(pltpu.make_async_copy(w.at[pl.ds(i * CAST, CAST)], narrow.at[i], got.at[i]))
        first = i * CAST
        to = wt_out.at[pl.ds(first, CAST)] if first < DT else wi_out.at[pl.ds(first - DT, CAST)]
        writes.append(pltpu.make_async_copy(wide.at[i], to, put.at[i]))
    for copy in reads + hand_on:
        copy.start()
    for i in range(blocks):
        reads[i].wait()
        wide[i] = narrow[i].astype(F32)
        writes[i].start()
    for copy in writes + hand_on:
        copy.wait()


def local(image_pooled, text_pooled, image_proj, text_proj, log_scale, pair_index):
    cols = NROW * PAIRS
    vmem = pltpu.VMEM
    held = pl.BlockSpec(memory_space=pltpu.VMEM)
    scalar = pl.BlockSpec(memory_space=pltpu.SMEM)
    far = pl.BlockSpec(memory_space=pl.ANY)
    weights, dpi, dpt, loss, dscale = pl.pallas_call(
        kernel,
        name="contrastive_loss",
        out_shape=(
            jax.ShapeDtypeStruct((WROWS, EMB), BF16),
            jax.ShapeDtypeStruct((PAIRS, DI), BF16),
            jax.ShapeDtypeStruct((PAIRS, DT), BF16),
            jax.ShapeDtypeStruct((1,), F32),
            jax.ShapeDtypeStruct((1,), F32),
        ),
        in_specs=[scalar, held, held, far, far, held],
        out_specs=(far, held, held, scalar, scalar),
        scratch_shapes=[
            vmem((NCOL, PAIRS, EMB), BF16),
            vmem((cols, EMB), BF16),
            vmem((NCOL, 8, PAIRS), F32),
            vmem((NCOL, PAIRS, cols), F32),
            vmem((NCOL * PAIRS, cols), BF16),
            vmem((NCOL, PAIRS, EMB), BF16),
            vmem((cols, EMB), BF16),
            vmem((2, 4, 2, 32, EMB), BF16),
            vmem((2, 4, 2, 64, EMB), BF16),
            vmem((2, 3, 64, EMB), BF16),
            vmem((2, 2, 32, EMB), BF16),
            vmem((2, 2, 64, EMB), BF16),
            vmem((4, PAIRS, EMB), BF16),
            vmem((2, 64, EMB), BF16),
            vmem((2, PAIRS, EMB), BF16),
            vmem((8, cols), F32),
            vmem((8, cols), F32),
            vmem((NCOL, PAIRS), F32),
            vmem((4, NCOL, PAIRS), F32),
            vmem((4, NCOL, PAIRS), F32),
            vmem((NROW, PAIRS), F32),
            vmem((4, NROW, PAIRS), F32),
            vmem((2, NROW, PAIRS), F32),
            vmem((2, PAIRS, PAIRS), F32),
            vmem((DI, EMB), BF16),
            vmem((DT, EMB), BF16),
            vmem((PAIRS, EMB), F32),
            vmem((PAIRS, EMB), F32),
            vmem((PAIRS, 128), F32),
            vmem((PAIRS, 128), F32),
            vmem((DI + DT, 2 * PAIRS), BF16),
            vmem((PAIRS, EMB), BF16),
            vmem((PAIRS, EMB), BF16),
            vmem((2 * PAIRS, HALF), BF16),
            vmem((2 * PAIRS, HALF), BF16),
            vmem((WROWS, HALF), BF16),
            vmem((3, 2, 128, HALF), BF16),
            vmem((3, 2, 256, HALF), BF16),
            vmem((3, 256, HALF), BF16),
            vmem((3, 3, 64, HALF), BF16),
            vmem((3, 64, HALF), BF16),
            vmem((3, 3, 16, HALF), BF16),
            vmem((3, 16, HALF), BF16),
            vmem((3, 4, 16, 128), F32),
            vmem((2, 16, 128), F32),
            pltpu.SemaphoreType.DMA((384,)),
            pltpu.SemaphoreType.DMA((384,)),
            pltpu.SemaphoreType.DMA((16,)),
        ],
        compiler_params=pltpu.CompilerParams(
            collective_id=0, has_side_effects=True, vmem_limit_bytes=60 * 1024 * 1024
        ),
        cost_estimate=pl.CostEstimate(
            flops=19 * 10**9, bytes_accessed=24 * 10**6, transcendentals=8 * 10**6
        ),
    )(
        log_scale, image_pooled, text_pooled, image_proj, text_proj,
        pair_index.reshape(1, PAIRS),
    )
    blocks = (DT + DI) // CAST
    dwt, dwi, dpi, dpt = pl.pallas_call(
        cast_kernel,
        name="casts",
        out_shape=(
            jax.ShapeDtypeStruct((DT, EMB), F32),
            jax.ShapeDtypeStruct((DI, EMB), F32),
            jax.ShapeDtypeStruct((PAIRS, DI), BF16),
            jax.ShapeDtypeStruct((PAIRS, DT), BF16),
        ),
        in_specs=[far, held, held],
        out_specs=(far, far, far, far),
        scratch_shapes=[
            vmem((blocks, CAST, EMB), BF16),
            vmem((blocks, CAST, EMB), F32),
            pltpu.SemaphoreType.DMA((blocks,)),
            pltpu.SemaphoreType.DMA((blocks,)),
            pltpu.SemaphoreType.DMA((2,)),
        ],
        compiler_params=pltpu.CompilerParams(vmem_limit_bytes=48 * 1024 * 1024),
        cost_estimate=pl.CostEstimate(flops=0, bytes_accessed=24 * 10**6, transcendentals=0),
    )(weights, dpi, dpt)
    return (loss, dpi, dpt, dwi, dwt, dscale)


def solution(mesh):
    return jax.shard_map(
        local,
        mesh=mesh,
        in_specs=(
            P(("row", "col"), None),
            P(("col", "row"), None),
            P(),
            P(),
            P(),
            P(("row", "col")),
        ),
        out_specs=(P(), P(("row", "col"), None), P(("col", "row"), None), P(), P(), P()),
        check_vma=False,
    )
```

```python
import functools

import jax
import jax.numpy as jnp
from jax import lax
from jax.experimental import pallas as pl
from jax.experimental.pallas import tpu as pltpu
from jax.sharding import PartitionSpec as P

EPS = 1e-06
MESH = pl.DeviceIdType.MESH
F32 = jnp.float32
BF16 = jnp.bfloat16
PAIRS = 128
NCOL = 16
NROW = 8
EMB = 1280
DI = 1664
DT = 1280
HALF = EMB // 2
DIRS = (1, -1)
STEPS = (2, 1, -1, 0)
WROWS = DI + DT + 128
LANES = ((0, 256), (256, 256), (512, 128))
HOLD = False
CAST = 128


class Net:
    def __init__(self, send_sem, recv_sem):
        self.send_sem, self.recv_sem = send_sem, recv_sem
        row, col = lax.axis_index("row"), lax.axis_index("col")
        self.x, self.c = row // 2, row % 2
        self.y, self.z = col // 4, col % 4
        self.count = 0
        self.started = {}

    def dev(self, dx=0, dy=0, dz=0, swap=0):
        core = 1 - self.c if swap else self.c
        return (
            2 * ((self.x + dx + 4) % 4) + core,
            4 * ((self.y + dy + 4) % 4) + (self.z + dz + 4) % 4,
        )

    def mate(self):
        return (2 * self.x + 1 - self.c, 4 * self.y + self.z)

    def greet(self):
        others = [self.dev(dx=d, swap=s) for d in range(4) for s in (0, 1)][1:]
        others += [self.dev(dy=d, dz=e) for d in range(4) for e in range(4)][1:]
        self.others = len(others)
        for other in others:
            pl.semaphore_signal(
                pltpu.get_barrier_semaphore(), inc=1, device_id=other, device_id_type=MESH
            )

    def met(self):
        pl.semaphore_wait(pltpu.get_barrier_semaphore(), self.others)

    def copy(self, number, src, dst, device):
        return pltpu.make_async_remote_copy(
            src_ref=src,
            dst_ref=dst,
            send_sem=self.send_sem.at[number],
            recv_sem=self.recv_sem.at[number],
            device_id=device,
            device_id_type=MESH,
        )

    def send(self, src, dst, device):
        number = self.count
        self.count += 1
        copy = self.copy(number, src, dst, device)
        copy.start()
        self.started[number] = copy
        return number

    def recv(self, number, dst):
        self.copy(number, dst, dst, self.mate()).wait_recv()

    def drain(self, numbers):
        for number in numbers:
            self.started.pop(number).wait_send()

    def finish(self):
        for copy in self.started.values():
            copy.wait_send()


def lanes(column):
    return jnp.transpose(jnp.broadcast_to(column, (PAIRS, PAIRS)))[0:1, :]


def sublanes(row):
    return jnp.transpose(jnp.broadcast_to(row, (PAIRS, PAIRS)))


def lse_over(parts):
    peak = functools.reduce(jnp.maximum, parts)
    return peak + jnp.log(sum(jnp.exp(p - peak) for p in parts))


def pick(i, options):
    value = options[0]
    for n in range(1, len(options)):
        value = jnp.where(i == n, options[n], value)
    return value


def kernel(
    scale_ref, pi, pt, wi_hbm, wt_hbm, pair, out, dpi, dpt, loss_ref, dscale_ref,
    img, txt, pid, scores, gb, pimg, ptxt,
    rg1, rg2, rb, rf1, rf2, rc, rx1, rx2,
    cmax, csum, rowl, rowq, coll, colq, acc,
    wi, wt, unit_i, unit_t, norm_i, norm_t, turned, dz_i, dz_t, di, dt,
    w, r1, r2, q1, r3, q2, r4, fin, s4, s2,
    send_sem, recv_sem, local_sem,
):
    net = Net(send_sem, recv_sem)
    x, c, y, z = net.x, net.c, net.y, net.z
    me_col = 4 * y + z
    scale = jnp.exp(jnp.full((8, 128), scale_ref[0], F32))[0:1, 0:1]
    load_i = pltpu.make_async_copy(wi_hbm, wi, local_sem.at[0])
    load_t = pltpu.make_async_copy(wt_hbm, wt, local_sem.at[1])
    load_i.start()
    load_t.start()
    net.greet()

    def axes(h):
        return ((y, z), (z, y))[h]

    def gdev(h, d):
        return net.dev(dy=d) if h == 0 else net.dev(dz=d)

    def fdev(h, d):
        return net.dev(dz=d) if h == 0 else net.dev(dy=d)

    def block(h, dg, df):
        g, f = axes(h)
        g, f = (g + dg + 4) % 4, (f + df + 4) % 4
        return 4 * g + f if h == 0 else 4 * f + g

    def half(ref, q, h):
        return ref.at[q, pl.ds(64 * h, 64)]

    def sub(ref, q, h, d):
        return ref.at[q, pl.ds(64 * h + (0 if d == 1 else 32), 32)]

    def rel(dy, dz):
        return 4 * ((y + dy + 4) % 4) + (z + dz + 4) % 4

    def tblock(dx, core):
        return pl.ds(pl.multiple_of((2 * ((x + dx + 4) % 4) + core) * PAIRS, PAIRS), PAIRS)

    def tsub(dx, core, d):
        start = (2 * ((x + dx + 4) % 4) + core) * PAIRS + (0 if d == 1 else 64)
        return pl.ds(pl.multiple_of(start, 64), 64)

    mine = pl.ds(pl.multiple_of(c * PAIRS, PAIRS), PAIRS)
    other = pl.ds(pl.multiple_of((1 - c) * PAIRS, PAIRS), PAIRS)
    keep = pl.ds(pl.multiple_of(c * HALF, 128), HALF)
    give = pl.ds(pl.multiple_of((1 - c) * HALF, 128), HALF)

    def embed(pooled, proj, unit, norm):
        value = jnp.dot(pooled[...], proj[...], preferred_element_type=F32)
        norms = jnp.sqrt(jnp.sum(value * value, axis=1, keepdims=True) + EPS)
        value = value / norms
        unit[...] = value
        norm[...] = jnp.broadcast_to(norms, norm.shape)
        return value.astype(BF16)

    pid[me_col] = jnp.broadcast_to(pair[...].astype(F32), (8, PAIRS))
    load_i.wait()
    img[me_col] = embed(pi, wi, unit_i, norm_i)
    net.met()

    f1, g1, f2, g3, g4 = {}, {}, {}, {}, {}
    x1, x2, cx = {}, {}, {}
    pz, py = {}, {}
    for h in (0, 1):
        for d in DIRS:
            part = half(img, me_col, h)
            f1[h, d] = net.send(part, part, fdev(h, d))
    load_t.wait()
    txt[tblock(0, c), :] = embed(pt, wt, unit_t, norm_t)
    for d in DIRS:
        part = txt.at[tblock(0, c)]
        x1[d] = net.send(part, part, net.dev(dx=d))
    net.drain(f1.values())
    for h in (0, 1):
        for d in DIRS:
            part = half(img, me_col, h)
            g1[h, d] = net.send(part, part, gdev(h, d))

    def to_mate(dx):
        part = txt.at[tblock(dx, c)]
        cx[dx] = net.send(part, part, net.mate())

    to_mate(0)
    for d in (1, 2, 3):
        pz[d] = net.send(pid.at[me_col], pid.at[me_col], net.dev(dz=d))
    turned[0:DT, mine] = jnp.transpose(pt[...])
    turned[DT:, mine] = jnp.transpose(pi[...])
    turn_n = net.send(turned.at[:, mine], turned.at[:, mine], net.mate())
    cmax[...] = jnp.full_like(cmax, -1e30)
    csum[...] = jnp.zeros_like(csum)
    acc[...] = jnp.zeros_like(acc)

    for h in (0, 1):
        for d in DIRS:
            q = block(h, 0, -d)
            net.recv(f1[h, d], half(img, q, h))
            f2[h, d] = net.send(sub(img, q, h, d), sub(img, q, h, d), fdev(h, d))
            for e in DIRS:
                g3[h, -d, e] = net.send(half(img, q, h), half(img, q, h), gdev(h, e))

    def pass_on(h, j, d):
        q = block(h, -d, j)
        net.recv(g1[h, d] if j == 0 else g3[h, j, d], half(img, q, h))
        g4[h, j, d] = net.send(sub(img, q, h, d), sub(img, q, h, d), gdev(h, d))

    for h in (0, 1):
        for d in DIRS:
            pass_on(h, 0, d)
    for d in DIRS:
        net.recv(x1[d], txt.at[tblock(-d, c)])
        part = txt.at[tsub(-d, c, d)]
        x2[d] = net.send(part, part, net.dev(dx=d))
        to_mate(-d)
    for h in (0, 1):
        q = block(h, 0, 2)
        for d in DIRS:
            net.recv(f2[h, d], sub(img, q, h, d))
        for d in DIRS:
            g3[h, 2, d] = net.send(half(img, q, h), half(img, q, h), gdev(h, d))
    for d in (1, 2, 3):
        net.recv(pz[d], pid.at[rel(0, -d)])
    for d in (1, 2, 3):
        line = pid.at[pl.ds(4 * y, 4)]
        py[d] = net.send(line, line, net.dev(dy=d))
    for d in DIRS:
        net.recv(x2[d], txt.at[tsub(2, c, d)])
    to_mate(2)
    for dx in (0, 1, -1, 2):
        net.recv(cx[dx], txt.at[tblock(dx, 1 - c)])

    def score(qa, qb):
        left = jnp.concatenate([img[qa], img[qb]], axis=0)
        s2q = scale * lax.dot_general(
            left, txt[...], (((1,), (1,)), ((), ())), preferred_element_type=F32
        )
        for q, s in ((qa, s2q[:PAIRS]), (qb, s2q[PAIRS:])):
            scores[q] = s
            peak = jnp.max(s, axis=1, keepdims=True)
            total = jnp.sum(jnp.exp(s - peak), axis=1, keepdims=True)
            rowl[pl.ds(q, 1), :] = lanes(peak + jnp.log(total))
        s3 = s2q.reshape(2 * PAIRS // 8, 8, s2q.shape[1])
        old = cmax[...]
        new = jnp.maximum(old, jnp.max(s3, axis=0))
        csum[...] = csum[...] * jnp.exp(old - new) + jnp.sum(jnp.exp(s3 - new[None]), axis=0)
        cmax[...] = new

    def in_pairs(work, *pairs):
        if len(pairs) == 1:
            (a, b), (e, f) = pairs[0]
            work(rel(a, b), rel(e, f))
            return

        @pl.loop(0, len(pairs))
        def _(i):
            a, b, e, f = (pick(i, [p[m][n] for p in pairs]) for m in (0, 1) for n in (0, 1))
            work(rel(a, b), rel(e, f))

    def last_hop(j):
        for h in (0, 1):
            for d in DIRS:
                net.recv(g4[h, j, d], sub(img, block(h, 2, j), h, d))

    in_pairs(score, ((0, 0), (0, 1)))
    for h in (0, 1):
        for j in (1, -1):
            for d in DIRS:
                pass_on(h, j, d)
    in_pairs(score, ((0, -1), (1, 0)), ((-1, 0), (1, 1)))
    for h in (0, 1):
        for d in DIRS:
            pass_on(h, 2, d)
    last_hop(0)
    in_pairs(score, ((1, -1), (-1, 1)), ((-1, -1), (2, 0)))
    last_hop(1)
    last_hop(-1)
    in_pairs(score, ((0, 2), (2, 1)), ((1, 2), (2, -1)))
    last_hop(2)
    in_pairs(score, ((-1, 2), (2, 2)))

    rows_n, cols_n = {}, {}
    plane = [(dy, dz) for dy in (0, 1, 3, 2) for dz in (0, 1, 3, 2)][1:]
    line = [(dx, swap) for dx in (0, 1, 3, 2) for swap in (0, 1)][1:]
    rowq[me_col] = rowl[...]
    for dy, dz in plane:
        own = rowq.at[me_col]
        rows_n[dy, dz] = net.send(own, own, net.dev(dy=dy, dz=dz))
    peak = jnp.max(cmax[...], axis=0, keepdims=True)
    lcol = peak + jnp.log(jnp.sum(csum[...] * jnp.exp(cmax[...] - peak), axis=0, keepdims=True))
    me_row = 2 * x + c
    for r in range(NROW):
        colq[me_row, r : r + 1, :] = lcol[:, r * PAIRS : (r + 1) * PAIRS]
    for dx, swap in line:
        own = colq.at[me_row]
        cols_n[dx, swap] = net.send(own, own, net.dev(dx=dx, swap=swap))
    for d in (1, 2, 3):
        net.recv(py[d], pid.at[pl.ds(4 * ((y - d + 4) % 4), 4)])
    for dy, dz in plane:
        net.recv(rows_n[dy, dz], rowq.at[rel(-dy, -dz)])
    rowl[...] = lse_over([rowq[i] for i in range(NCOL)])
    for dx, swap in line:
        flip = c + swap - 2 * c * swap
        net.recv(cols_n[dx, swap], colq.at[2 * ((x - dx + 4) % 4) + flip])
    coll[...] = lse_over([colq[i] for i in range(NROW)])

    first = (me_col * NROW * PAIRS).astype(F32)
    place = lax.broadcasted_iota(jnp.int32, (PAIRS, PAIRS), 1).astype(F32) + first

    def soft_grad(*pair_of):
        for q in pair_of:
            lrow = sublanes(rowl[pl.ds(q, 1), :])
            target = sublanes(pid[q][0:1, :]) - place
            hit_sum = jnp.zeros((PAIRS, PAIRS), F32)
            dot_sum = jnp.zeros((PAIRS, PAIRS), F32)
            here = pl.ds(pl.multiple_of(q * PAIRS, PAIRS), PAIRS)
            for r in range(NROW):
                at = slice(r * PAIRS, (r + 1) * PAIRS)
                s = scores[q, :, at]
                soft = 0.5 * (jnp.exp(s - lrow) + jnp.exp(s - coll[r : r + 1, :]))
                hit = (target == float(r * PAIRS)).astype(F32)
                g = soft - hit
                hit_sum += s * hit
                dot_sum += s * g
                gb[here, at] = g.astype(BF16)
            acc[0] += hit_sum
            acc[1] += dot_sum

    def image_product(qa, qb):
        rows = [gb[pl.ds(pl.multiple_of(q * PAIRS, PAIRS), PAIRS), :] for q in (qa, qb)]
        prod = jnp.dot(jnp.concatenate(rows, axis=0), txt[...], preferred_element_type=F32)
        pimg[qa] = prod[:PAIRS].astype(BF16)
        pimg[qb] = prod[PAIRS:].astype(BF16)

    def grad(qa, qb):
        soft_grad(qa, qb)
        image_product(qa, qb)

    rg1n, rg2n, rf1n, rf2n = {}, {}, {}, {}
    slot = {2: 0, 1: 1, -1: 2, 0: 3}
    side = {1: 0, -1: 1}

    def scatter1(h, *js):
        for j in js:
            for d in DIRS:
                q = block(h, 2, j)
                rg1n[h, j, d] = net.send(
                    sub(pimg, q, h, d), rg1.at[h, slot[j], side[d]], gdev(h, d)
                )

    def scatter2(j):
        for h in (0, 1):
            for d in DIRS:
                q = block(h, d, j)
                got = rg1.at[h, slot[j], side[d]]
                net.recv(rg1n[h, j, d], got)
                part = sub(pimg, q, h, d)
                part[...] = (part[...].astype(F32) + got[...].astype(F32)).astype(BF16)
                rg2n[h, j, d] = net.send(
                    half(pimg, q, h), rg2.at[h, slot[j], side[d]], gdev(h, d)
                )

    def line_sum(h, j):
        for d in DIRS:
            net.recv(rg2n[h, j, d], rg2.at[h, slot[j], side[d]])
        total = half(pimg, block(h, 0, j), h)[...].astype(F32)
        for d in DIRS:
            total += rg2[h, slot[j], side[d]].astype(F32)
        return total

    in_pairs(grad, ((2, 2), (2, 1)))
    scatter1(0, 2, 1)
    scatter1(1, 2)
    in_pairs(grad, ((1, 2), (2, -1)))
    scatter1(1, 1)
    scatter1(0, -1)
    in_pairs(grad, ((-1, 2), (2, 0)))
    scatter1(1, -1)
    scatter1(0, 0)
    in_pairs(grad, ((0, 2), (1, 1)))
    scatter1(1, 0)
    scatter2(2)
    near_pairs = (((1, -1), (-1, 1)), ((-1, -1), (1, 0)))
    last_pairs = (((0, 1), (-1, 0)), ((0, -1), (0, 0)))
    in_pairs(soft_grad, *near_pairs, *last_pairs)

    mate_n, tx1n, tx2n = {}, {}, {}

    def text_product(dx):
        xx = (x + dx + 4) % 4
        at = pl.ds(pl.multiple_of(xx * 2 * PAIRS, 2 * PAIRS), 2 * PAIRS)
        prod = lax.dot_general(
            gb[:, at], img[...].reshape(NCOL * PAIRS, EMB), (((0,), (0,)), ((), ())),
            preferred_element_type=F32,
        )
        ptxt[at, :] = prod.astype(BF16)
        mate_n[dx] = net.send(ptxt.at[tblock(dx, 1 - c)], rc.at[xx], net.mate())

    def text_pair(dx):
        xx = (x + dx + 4) % 4
        net.recv(mate_n[dx], rc.at[xx])
        return ptxt[tblock(dx, c), :].astype(F32) + rc[xx].astype(F32)

    text_product(2)
    in_pairs(image_product, *near_pairs)
    scatter2(1)
    scatter2(-1)
    ptxt[tblock(2, c), :] = text_pair(2).astype(BF16)
    for d in DIRS:
        tx1n[d] = net.send(ptxt.at[tsub(2, c, d)], rx1.at[side[d]], net.dev(dx=d))
    text_product(1)
    text_product(-1)
    for h in (0, 1):
        rb[h, 0] = line_sum(h, 2).astype(BF16)
        for d in DIRS:
            at = pl.ds(0 if d == 1 else 32, 32)
            rf1n[h, d] = net.send(rb.at[h, 0, at], rf1.at[h, side[d]], fdev(h, d))
    in_pairs(image_product, *last_pairs)
    for d in DIRS:
        ptxt[tblock(d, c), :] = text_pair(d).astype(BF16)
        net.recv(tx1n[d], rx1.at[side[d]])
        part = ptxt.at[tsub(d, c, d)]
        part[...] = (part[...].astype(F32) + rx1[side[d]].astype(F32)).astype(BF16)
        tx2n[d] = net.send(ptxt.at[tblock(d, c)], rx2.at[side[d]], net.dev(dx=d))
    net.drain(rg2n[h, j, d] for h in (0, 1) for j in (1, -1) for d in DIRS)
    scatter2(0)
    text_product(0)
    for h in (0, 1):
        for d in DIRS:
            total = line_sum(h, d)
            net.recv(rf1n[h, d], rf1.at[h, side[d]])
            extra = rf1[h, side[d]].astype(F32)
            lo, hi = total[0:32], total[32:64]
            if d == 1:
                lo = lo + extra
            else:
                hi = hi + extra
            rb[h, 1 + side[d], 0:32] = lo.astype(BF16)
            rb[h, 1 + side[d], 32:64] = hi.astype(BF16)
            rf2n[h, d] = net.send(rb.at[h, 1 + side[d]], rf2.at[h, side[d]], fdev(h, d))

    where = (x, y, z)

    def dev(axis, d):
        return net.dev(**{("dx", "dy", "dz")[axis]: d})

    tot_n = {}

    def tot_send(axis):
        own = s4.at[axis, where[axis]]
        for d in (1, 2, 3):
            tot_n[axis, d] = net.send(own, own, dev(axis, d))

    def tot_recv(axis):
        for d in (1, 2, 3):
            net.recv(tot_n[axis, d], s4.at[axis, (where[axis] - d + 4) % 4])
        return s4[axis, 0] + s4[axis, 1] + s4[axis, 2] + s4[axis, 3]

    half_lse = (0.5 / NCOL) * jnp.sum(rowl[...].reshape(2, 8, PAIRS), axis=0) + (
        0.5 / NROW
    ) * coll[...]
    s4[0, x, 0:8] = half_lse - jnp.sum(acc[0].reshape(16, 8, PAIRS), axis=0)
    s4[0, x, 8:16] = jnp.sum(acc[1].reshape(16, 8, PAIRS), axis=0)
    tot_send(0)

    def normal_grad(grads, unit, norm, dz, halves):
        u = unit[...]
        inner = jnp.sum(u * grads, axis=1, keepdims=True)
        dz[...] = ((grads - u * inner) / norm[:, 0:1]).astype(BF16)
        number = net.send(dz.at[:, give], halves.at[mine], net.mate())
        halves[mine, :] = dz[:, keep]
        return number

    total = text_pair(0)
    for d in DIRS:
        net.recv(tx2n[d], rx2.at[side[d]])
        total += rx2[side[d]].astype(F32)
    dt_n = normal_grad(scale * total, unit_t, norm_t, dz_t, dt)
    w[DI + DT :, :] = jnp.zeros((WROWS - DI - DT, HALF), BF16)
    net.recv(turn_n, turned.at[:, other])

    orders = ((0, 1, 2), (1, 2, 0), (2, 0, 1))

    def near(axis, d):
        return (where[axis] + d + 4) % 4

    def rows_at(k, a, b=None, e=None, size=256):
        start = 1024 * k + 256 * a
        if b is not None:
            start = start + 64 * b
        if e is not None:
            start = start + 16 * e
        return pl.ds(pl.multiple_of(start, 16), size)

    def part_at(k, d, s):
        return pl.ds(pl.multiple_of(1024 * k + 256 * near(orders[k][0], d) + 128 * s, 128), 128)

    def weights(first_row, rows, right):
        tall = rows // 4

        @pl.loop(0, 4)
        def _(i):
            at = pl.ds(pl.multiple_of(first_row + i * tall, 16), tall)
            w[at, :] = jnp.dot(turned[at, :], right[...], preferred_element_type=F32).astype(BF16)

    def pooled_grad(dz, proj, result, rows):
        @pl.loop(0, rows // 128)
        def _(i):
            at = pl.ds(pl.multiple_of(i * 128, 128), 128)
            result[:, at] = lax.dot_general(
                dz[...], proj[at, :], (((1,), (1,)), ((), ())), preferred_element_type=F32
            ).astype(BF16)

    groups = [[(k, first, size) for k in range(3)] for first, size in LANES]
    n1, n2, n3, n4 = {}, {}, {}, {}
    m1, m2, m3, m4, back = {}, {}, {}, {}, {}
    over = []

    def step(k, d):
        return dev(orders[k][0], d)

    def cut(ch, rows):
        start = pl.multiple_of(c * HALF + ch[1], 128)
        return out.at[rows, pl.ds(start, ch[2])]

    def at_mate(ch, rows):
        start = pl.multiple_of((1 - c) * HALF + ch[1], 128)
        return out.at[rows, pl.ds(start, ch[2])]

    def to_mate_w(ch, rows):
        over.append((net.send(cut(ch, rows), cut(ch, rows), net.mate()), ch, rows))

    def reduce1(ch, behind=()):
        k, lane = ch[0], pl.ds(ch[1], ch[2])
        net.drain(behind)
        for d in DIRS:
            n1[ch, d] = net.send(
                w.at[part_at(k, 2, side[d]), lane], r1.at[k, side[d], :, lane], step(k, d)
            )

    def reduce2(ch, behind=()):
        k, lane = ch[0], pl.ds(ch[1], ch[2])
        for d in DIRS:
            net.recv(n1[ch, d], r1.at[k, side[d], :, lane])
            got = part_at(k, d, side[d])
            w[got, lane] = (w[got, lane].astype(F32) + r1[k, side[d], :, lane].astype(F32)).astype(
                BF16
            )
        net.drain(behind)
        for d in DIRS:
            n2[ch, d] = net.send(
                w.at[rows_at(k, near(orders[k][0], d)), lane], r2.at[k, side[d], :, lane],
                step(k, d),
            )

    def reduce3(ch, behind=()):
        k, lane = ch[0], pl.ds(ch[1], ch[2])
        a_ax, b_ax, _ = orders[k]
        total = w[rows_at(k, where[a_ax]), lane].astype(F32)
        for d in DIRS:
            net.recv(n2[ch, d], r2.at[k, side[d], :, lane])
            total += r2[k, side[d], :, lane].astype(F32)
        q1[k, :, lane] = total.astype(BF16)
        net.drain(behind)
        for d in (2, 1, 3):
            to = pl.ds(pl.multiple_of(64 * near(b_ax, d), 64), 64)
            n3[ch, d] = net.send(q1.at[k, to, lane], r3.at[k, d - 1, :, lane], dev(b_ax, d))

    def reduce4(ch, behind=()):
        k, lane = ch[0], pl.ds(ch[1], ch[2])
        _, b_ax, c_ax = orders[k]
        total = q1[k, pl.ds(pl.multiple_of(64 * where[b_ax], 64), 64), lane].astype(F32)
        for d in (1, 3, 2):
            net.recv(n3[ch, d], r3.at[k, d - 1, :, lane])
            total += r3[k, d - 1, :, lane].astype(F32)
        q2[k, :, lane] = total.astype(BF16)
        net.drain(behind)
        for d in (2, 1, 3):
            to = pl.ds(pl.multiple_of(16 * near(c_ax, d), 16), 16)
            n4[ch, d] = net.send(q2.at[k, to, lane], r4.at[k, d - 1, :, lane], dev(c_ax, d))

    def gather1(ch, behind=()):
        k, lane = ch[0], pl.ds(ch[1], ch[2])
        a_ax, b_ax, c_ax = orders[k]
        total = q2[k, pl.ds(pl.multiple_of(16 * where[c_ax], 16), 16), lane].astype(F32)
        for d in (1, 3, 2):
            net.recv(n4[ch, d], r4.at[k, d - 1, :, lane])
            total += r4[k, d - 1, :, lane].astype(F32)
        fin[k, :, lane] = total.astype(BF16)
        own = cut(ch, rows_at(k, where[a_ax], where[b_ax], where[c_ax], 16))
        net.drain(behind)
        for d in (2, 1, 3):
            m1[ch, d] = net.send(fin.at[k, :, lane], own, dev(c_ax, d))
        back[ch] = pltpu.make_async_copy(fin.at[k, :, lane], own, local_sem.at[2 + len(back)])
        back[ch].start()

    def gather2(ch, behind=()):
        k = ch[0]
        a_ax, b_ax, c_ax = orders[k]
        back[ch].wait()
        for d in (1, 3, 2):
            rows = rows_at(k, where[a_ax], where[b_ax], near(c_ax, -d), 16)
            net.recv(m1[ch, d], cut(ch, rows))
        own = cut(ch, rows_at(k, where[a_ax], where[b_ax], None, 64))
        net.drain(behind)
        for d in (2, 1, 3):
            m2[ch, d] = net.send(own, own, dev(b_ax, d))

    def gather3(ch, behind=()):
        k = ch[0]
        a_ax, b_ax, _ = orders[k]
        for d in (1, 3, 2):
            net.recv(m2[ch, d], cut(ch, rows_at(k, where[a_ax], near(b_ax, -d), None, 64)))
        rows = rows_at(k, where[a_ax])
        net.drain(behind)
        for d in DIRS:
            m3[ch, d] = net.send(cut(ch, rows), cut(ch, rows), step(k, d))
        to_mate_w(ch, rows)

    def gather4(ch, behind=()):
        k = ch[0]
        for d in DIRS:
            net.recv(m3[ch, d], cut(ch, rows_at(k, near(orders[k][0], -d))))
        net.drain(behind)
        for d in DIRS:
            rows = cut(ch, part_at(k, -d, side[d]))
            m4[ch, d] = net.send(rows, rows, step(k, d))
        for d in DIRS:
            to_mate_w(ch, rows_at(k, near(orders[k][0], -d)))

    def gather5(ch):
        for d in DIRS:
            rows = part_at(ch[0], 2, side[d])
            net.recv(m4[ch, d], cut(ch, rows))
            to_mate_w(ch, rows)

    def both(work, sent, ways):
        for n, group in enumerate(groups):
            for k, ch in enumerate(group):
                hold = HOLD and n > 0
                work(ch, [sent[groups[n - 1][k], d] for d in ways] if hold else ())

    net.recv(dt_n, dt.at[other])
    weights(0, DT, dt)
    pooled_grad(dz_t, wt, dpt, DT)

    halves = []
    for h in (0, 1):
        total = line_sum(h, 0)
        for d in DIRS:
            net.recv(rf2n[h, d], rf2.at[h, side[d]])
            total += rf2[h, side[d]].astype(F32)
        halves.append(scale * total)
    di_n = normal_grad(jnp.concatenate(halves, axis=0), unit_i, norm_i, dz_i, di)
    net.recv(di_n, di.at[other])
    weights(DT, DI, di)
    both(reduce1, n1, DIRS)
    pooled_grad(dz_i, wi, dpi, DI)

    both(reduce2, n2, DIRS)
    s4[1, y] = tot_recv(0)
    tot_send(1)
    hops = (1, 2, 3)
    both(reduce3, n3, hops)
    s4[2, z] = tot_recv(1)
    tot_send(2)
    both(reduce4, n4, hops)
    s2[c] = tot_recv(2)
    tot_mate = net.send(s2.at[c], s2.at[c], net.mate())
    both(gather1, m1, hops)
    both(gather2, m2, hops)
    both(gather3, m3, DIRS)
    both(gather4, m4, DIRS)
    for group in groups:
        for ch in group:
            gather5(ch)
    net.recv(tot_mate, s2.at[1 - c])
    totals = s2[0] + s2[1]
    loss_ref[0] = jnp.sum(totals[0:8]) * (1.0 / (PAIRS * NROW * NCOL))
    dscale_ref[0] = jnp.sum(totals[8:16])
    for number, ch, rows in over:
        net.recv(number, at_mate(ch, rows))
    net.finish()


def cast_kernel(w, dpi, dpt, wt_out, wi_out, dpi_out, dpt_out, narrow, wide, got, put, passed):
    hand_on = [
        pltpu.make_async_copy(dpi, dpi_out, passed.at[0]),
        pltpu.make_async_copy(dpt, dpt_out, passed.at[1]),
    ]
    blocks = (DT + DI) // CAST
    reads, writes = [], []
    for i in range(blocks):
        reads.append(pltpu.make_async_copy(w.at[pl.ds(i * CAST, CAST)], narrow.at[i], got.at[i]))
        first = i * CAST
        to = wt_out.at[pl.ds(first, CAST)] if first < DT else wi_out.at[pl.ds(first - DT, CAST)]
        writes.append(pltpu.make_async_copy(wide.at[i], to, put.at[i]))
    for copy in reads + hand_on:
        copy.start()
    for i in range(blocks):
        reads[i].wait()
        wide[i] = narrow[i].astype(F32)
        writes[i].start()
    for copy in writes + hand_on:
        copy.wait()


def local(image_pooled, text_pooled, image_proj, text_proj, log_scale, pair_index):
    cols = NROW * PAIRS
    vmem = pltpu.VMEM
    held = pl.BlockSpec(memory_space=pltpu.VMEM)
    scalar = pl.BlockSpec(memory_space=pltpu.SMEM)
    far = pl.BlockSpec(memory_space=pl.ANY)
    weights, dpi, dpt, loss, dscale = pl.pallas_call(
        kernel,
        name="contrastive_loss",
        out_shape=(
            jax.ShapeDtypeStruct((WROWS, EMB), BF16),
            jax.ShapeDtypeStruct((PAIRS, DI), BF16),
            jax.ShapeDtypeStruct((PAIRS, DT), BF16),
            jax.ShapeDtypeStruct((1,), F32),
            jax.ShapeDtypeStruct((1,), F32),
        ),
        in_specs=[scalar, held, held, far, far, held],
        out_specs=(far, held, held, scalar, scalar),
        scratch_shapes=[
            vmem((NCOL, PAIRS, EMB), BF16),
            vmem((cols, EMB), BF16),
            vmem((NCOL, 8, PAIRS), F32),
            vmem((NCOL, PAIRS, cols), F32),
            vmem((NCOL * PAIRS, cols), BF16),
            vmem((NCOL, PAIRS, EMB), BF16),
            vmem((cols, EMB), BF16),
            vmem((2, 4, 2, 32, EMB), BF16),
            vmem((2, 4, 2, 64, EMB), BF16),
            vmem((2, 3, 64, EMB), BF16),
            vmem((2, 2, 32, EMB), BF16),
            vmem((2, 2, 64, EMB), BF16),
            vmem((4, PAIRS, EMB), BF16),
            vmem((2, 64, EMB), BF16),
            vmem((2, PAIRS, EMB), BF16),
            vmem((8, cols), F32),
            vmem((8, cols), F32),
            vmem((NCOL, PAIRS), F32),
            vmem((NCOL, NCOL, PAIRS), F32),
            vmem((NROW, PAIRS), F32),
            vmem((NROW, NROW, PAIRS), F32),
            vmem((2, PAIRS, PAIRS), F32),
            vmem((DI, EMB), BF16),
            vmem((DT, EMB), BF16),
            vmem((PAIRS, EMB), F32),
            vmem((PAIRS, EMB), F32),
            vmem((PAIRS, 128), F32),
            vmem((PAIRS, 128), F32),
            vmem((DI + DT, 2 * PAIRS), BF16),
            vmem((PAIRS, EMB), BF16),
            vmem((PAIRS, EMB), BF16),
            vmem((2 * PAIRS, HALF), BF16),
            vmem((2 * PAIRS, HALF), BF16),
            vmem((WROWS, HALF), BF16),
            vmem((3, 2, 128, HALF), BF16),
            vmem((3, 2, 256, HALF), BF16),
            vmem((3, 256, HALF), BF16),
            vmem((3, 3, 64, HALF), BF16),
            vmem((3, 64, HALF), BF16),
            vmem((3, 3, 16, HALF), BF16),
            vmem((3, 16, HALF), BF16),
            vmem((3, 4, 16, 128), F32),
            vmem((2, 16, 128), F32),
            pltpu.SemaphoreType.DMA((384,)),
            pltpu.SemaphoreType.DMA((384,)),
            pltpu.SemaphoreType.DMA((16,)),
        ],
        compiler_params=pltpu.CompilerParams(
            collective_id=0, has_side_effects=True, vmem_limit_bytes=60 * 1024 * 1024
        ),
        cost_estimate=pl.CostEstimate(
            flops=19 * 10**9, bytes_accessed=24 * 10**6, transcendentals=8 * 10**6
        ),
    )(
        log_scale, image_pooled, text_pooled, image_proj, text_proj,
        pair_index.reshape(1, PAIRS),
    )
    blocks = (DT + DI) // CAST
    dwt, dwi, dpi, dpt = pl.pallas_call(
        cast_kernel,
        name="casts",
        out_shape=(
            jax.ShapeDtypeStruct((DT, EMB), F32),
            jax.ShapeDtypeStruct((DI, EMB), F32),
            jax.ShapeDtypeStruct((PAIRS, DI), BF16),
            jax.ShapeDtypeStruct((PAIRS, DT), BF16),
        ),
        in_specs=[far, held, held],
        out_specs=(far, far, far, far),
        scratch_shapes=[
            vmem((blocks, CAST, EMB), BF16),
            vmem((blocks, CAST, EMB), F32),
            pltpu.SemaphoreType.DMA((blocks,)),
            pltpu.SemaphoreType.DMA((blocks,)),
            pltpu.SemaphoreType.DMA((2,)),
        ],
        compiler_params=pltpu.CompilerParams(vmem_limit_bytes=48 * 1024 * 1024),
        cost_estimate=pl.CostEstimate(flops=0, bytes_accessed=24 * 10**6, transcendentals=0),
    )(weights, dpi, dpt)
    return (loss, dpi, dpt, dwi, dwt, dscale)


def solution(mesh):
    return jax.shard_map(
        local,
        mesh=mesh,
        in_specs=(
            P(("row", "col"), None),
            P(("col", "row"), None),
            P(),
            P(),
            P(),
            P(("row", "col")),
        ),
        out_specs=(P(), P(("row", "col"), None), P(("col", "row"), None), P(), P(), P()),
        check_vma=False,
    )
```
